32 devices in a mesh: inst: 2 (over x), space: 16 (over z, y, core).
Axes of the slice: x: 2, y: 2, z: 4, core: 2. Of those that a mesh axis runs over, the one named last changes fastest.
Arguments:
- state: float32 [2, 5, 64, 8192], P('inst', None, None, 'space'), may hold values from -6 to 6
- metric: float32 [8192], P('space'), may hold values from 1 to 4
- jacobians: float32 [3, 5, 5], replicated, may hold values from -2.5 to 2.5
- dissipation: float32 [1], replicated, may hold values from 0.5 to 2
- omega: float32 [1], replicated, may hold values from 0.5 to 2
- rotor_angle: float32 [2], P('inst'), may hold values from -3.140625 to 3.140625
- counts: int32 [16], P('space'), may hold values from 384 to 512, as said below
- neighbours: int32 [6, 8192], P(None, 'space'), may hold values from 0 to 639, as said below
- mortar_pairs: int32 [2, 4096], P('inst', 'space'), may hold values from 0 to 4095, as said below
Outputs:
- updated: float32 [2, 5, 64, 8192], P('inst', None, None, 'space')
The draws below stay inside these ranges and needn't reach their ends.
Inputs may be any that keep to these rules, and one draw needn't show every extreme that they name: Some index of space has all 512 slots live; live slots are the first counts ones of a device. `neighbours`: extended numbering of a device: 64 halo slots from the previous device (its slots 64 to 127), its own 512 slots, 64 from the next device (its slots 0 to 63); every entry names a live element. `mortar_pairs`: each row is a permutation; for each instance there is one device offset, the same for all devices, such that the partners of device p's 256 faces lie on devices p plus that offset and the one after it, counted cyclically.
All inputs are finite; a program needn't handle non-finite values.
Results may differ from the reference program's by a relative error of at most 0.0001.
Values sent between devices are 32-bit elements; how exact they have to be, the bound alone decides.
No kernel may reach another device: no remote copies, remote signals or barrier semaphores. Data moves between devices by JAX's collectives and lax.ppermute only.
A program may use at most 64 MiB of HBM per device.

```python
import math
import jax
import jax.numpy as jnp
import numpy as np
from jax import lax

FIELDS = 5
MODES = 64
E_DEV = 512
RIM = 64
MORT = 256
INSTANCES = 2
ELEMS = 8192
PLANE = 4096
N_SPACE = 16


def shared_counts(key):
    partitions = ELEMS // E_DEV
    values = jax.random.randint(jax.random.fold_in(key, 11), (partitions,), 2 * RIM + MORT, E_DEV + 1)
    busiest = jax.random.randint(jax.random.fold_in(key, 12), (), 0, partitions)
    return values.at[busiest].set(E_DEV).astype(jnp.int32)


def draw_counts(key, part):
    return shared_counts(key)


def draw_neighbours(key, part):
    per_column = jnp.repeat(shared_counts(key), E_DEV)
    upper = per_column[None, :] + 2 * RIM
    drawn = jax.random.randint(jax.random.fold_in(key, 13), (6, ELEMS), 0, upper)
    result = jnp.where(drawn < RIM + per_column[None, :], drawn, drawn - per_column[None, :] + E_DEV)
    return result.astype(jnp.int32)


def draw_mortar_pairs(key, part):
    partitions = PLANE // MORT
    faces_all = jnp.arange(PLANE, dtype=jnp.int32)
    device_shift = jax.random.randint(jax.random.fold_in(key, 21), (INSTANCES,), 0, partitions)
    chosen = jax.random.permutation(jax.random.fold_in(key, 23), INSTANCES)
    device_shift = device_shift.at[chosen[0]].set(partitions // 2)
    device_shift = device_shift.at[chosen[1]].set(partitions - 1)
    within = jax.random.randint(jax.random.fold_in(key, 24), (INSTANCES,), 1, MORT)
    offsets = (device_shift * MORT + within)[:, None]
    flips = jax.random.randint(jax.random.fold_in(key, 22), (INSTANCES, 1), 0, 4)
    return jnp.mod(jnp.bitwise_xor(faces_all[None, :], flips) + offsets, PLANE).astype(jnp.int32)


def block_scale(rng, dims, cuts, low, top_value):
    level, own = 1.0, jax.random.fold_in(rng, 6)
    for dim, blocks in cuts:
        draws = jnp.exp(jax.random.uniform(jax.random.fold_in(own, dim), (blocks,), jnp.float32, low / len(cuts), top_value / len(cuts)))
        level = level * jnp.repeat(draws, dims[dim] // blocks).reshape([-1 if axis == dim else 1 for axis in range(len(dims))])
    return level


def bell_draw(key, shape, width, reach, cuts=(), held_as=jnp.bfloat16):
    gain = block_scale(key, shape, cuts, -0.22, 0.18) if cuts else 1.0
    entries = jax.random.normal(key, shape, jnp.float32) * width * gain
    return jnp.minimum(jnp.maximum(entries, -reach), reach).astype(held_as)


def setup_inputs(seed: int = 0) -> dict:
    key_list = jax.random.split(jax.random.key(seed), 10)
    state = bell_draw(key_list[0], (INSTANCES, FIELDS, MODES, ELEMS), 1.0, 6.0, ((0, 2), (3, 16)), jnp.float32)
    metric = jnp.clip(jnp.exp(math.log(4.0) - 1.3862944 * jax.random.uniform(key_list[1], (ELEMS,), jnp.float32) ** block_scale(key_list[1], (ELEMS,), ((0, 16),), -0.2, 0.2)), 1.0, 4.0)
    jacobians = bell_draw(key_list[2], (3, FIELDS, FIELDS), FIELDS ** -0.5, 2.5, (), jnp.float32)
    dissipation = jnp.clip(jax.random.uniform(key_list[3], (1,), jnp.float32, 0.5, 2.0), 0.5, 2.0)
    omega = jnp.clip(jnp.exp(jax.random.uniform(key_list[4], (1,), jnp.float32, math.log(0.5), math.log(2.0))), 0.5, 2.0)
    rotor_angle = jnp.clip(jax.random.uniform(key_list[5], (INSTANCES,), jnp.float32, -3.140625, 3.140625), -3.140625, 3.140625)
    counts = draw_counts(jax.random.fold_in(key_list[9], 71), 0)
    neighbours = draw_neighbours(jax.random.fold_in(key_list[9], 71), 0)
    mortar_pairs = draw_mortar_pairs(jax.random.fold_in(key_list[9], 71), 0)
    return dict(state=state, metric=metric, jacobians=jacobians, dissipation=dissipation, omega=omega, rotor_angle=rotor_angle, counts=counts, neighbours=neighbours, mortar_pairs=mortar_pairs)


courant_number = 0.5

def gll_derivative():
    nodes = np.array([-1.0, -1.0 / math.sqrt(5.0), 1.0 / math.sqrt(5.0), 1.0])
    barycentric = np.array([1.0 / np.prod([nodes[j] - nodes[k] for k in range(4) if k != j]) for j in range(4)])
    derivative = np.zeros((4, 4))
    for i in range(4):
        for j in range(4):
            if i != j:
                derivative[i, j] = barycentric[j] / barycentric[i] / (nodes[i] - nodes[j])
        derivative[i, i] = -np.sum(derivative[i])
    return jnp.asarray(derivative, jnp.float32)

def spectral_matrix(inst_count, omega):
    positions = jnp.arange(inst_count)
    offset = positions[:, None] - positions[None, :]
    parity = 1.0 - 2.0 * jnp.mod(offset, 2).astype(jnp.float32)
    safe_offset = jnp.where(offset == 0, 1, offset).astype(jnp.float32)
    angle_value = jnp.pi * safe_offset / inst_count
    cot_value = 0.5 * parity / jnp.tan(angle_value)
    sine_value = jnp.sin(angle_value)
    viscous_value = parity / (2.0 * inst_count * sine_value * sine_value)
    diagonal_value = jnp.float32((inst_count * inst_count + 2.0) / (12.0 * inst_count))
    return jnp.where(offset == 0, diagonal_value, cot_value + viscous_value).astype(jnp.float32) * omega[0]

def face_trace(nodal_field, face_number):
    node_index = 3 * (face_number % 2)
    trace_block = lax.index_in_dim(nodal_field, node_index, 2 + face_number // 2, keepdims=False)
    return trace_block.reshape(trace_block.shape[0], trace_block.shape[1], 16, trace_block.shape[-1])

def face_add(nodal_field, face_number, face_values):
    direction = face_number // 2
    node_index = 3 * (face_number % 2)
    shaped = face_values.reshape(face_values.shape[0], face_values.shape[1], 4, 4, face_values.shape[-1])
    if direction == 0:
        return nodal_field.at[:, :, node_index].add(shaped)
    if direction == 1:
        return nodal_field.at[:, :, :, node_index].add(shaped)
    return nodal_field.at[:, :, :, :, node_index].add(shaped)

def mix_fields(jacobian, nodal_field):
    return jnp.einsum('gf,if...->ig...', jacobian, nodal_field, precision=lax.Precision.HIGHEST)

def derive(derivative, nodal_field, direction):
    product = jnp.tensordot(derivative, nodal_field, axes=([1], [2 + direction]), precision=lax.Precision.HIGHEST)
    return jnp.moveaxis(product, 0, 2 + direction)

def rotate(trace_block, angles):
    cosines = jnp.cos(angles)[:, None, None]
    sines = jnp.sin(angles)[:, None, None]
    velocity_two = trace_block[:, 2]
    velocity_three = trace_block[:, 3]
    new_two = cosines * velocity_two - sines * velocity_three
    new_three = sines * velocity_two + cosines * velocity_three
    return jnp.concatenate([trace_block[:, :2], new_two[:, None], new_three[:, None], trace_block[:, 4:]], axis=1)

def reference(state, metric, jacobians, dissipation, omega, rotor_angle, counts, neighbours, mortar_pairs):
    inst_count = state.shape[0]
    columns_all = state.shape[-1]
    nodal_field = state.reshape(inst_count, 5, 4, 4, 4, columns_all)
    derivative = gll_derivative()
    volume = derive(derivative, mix_fields(jacobians[0], nodal_field), 0)
    volume = volume + derive(derivative, mix_fields(jacobians[1], nodal_field), 1)
    volume = volume + derive(derivative, mix_fields(jacobians[2], nodal_field), 2)
    tendency = -metric * volume
    columns = jnp.arange(columns_all, dtype=jnp.int32)
    owners = columns // E_DEV
    positions = columns % E_DEV
    for face_number in range(6):
        neighbour_index = neighbours[face_number]
        prev_col = jnp.mod(owners - 1, N_SPACE) * E_DEV + RIM + neighbour_index
        own_col = owners * E_DEV + neighbour_index - RIM
        next_col = jnp.mod(owners + 1, N_SPACE) * E_DEV + neighbour_index - RIM - E_DEV
        source = jnp.where(neighbour_index < RIM, prev_col, jnp.where(neighbour_index < RIM + E_DEV, own_col, next_col)).astype(jnp.int32)
        inner_trace = face_trace(nodal_field, face_number)
        opposite = face_trace(nodal_field, face_number ^ 1)
        outer_trace = jnp.take(opposite, source, axis=3)
        if face_number == 5:
            interface = (positions >= 2 * RIM) & (positions < 2 * RIM + MORT)
            plane_index = jnp.where(interface, owners * MORT + positions - 2 * RIM, 0).astype(jnp.int32)
            partner = jnp.take(mortar_pairs, plane_index, axis=1)
            partner_col = (partner // MORT * E_DEV + 2 * RIM + partner % MORT).astype(jnp.int32)
            rotor_trace = jnp.take_along_axis(opposite, partner_col[:, None, None, :], axis=3)
            rotor_trace = rotate(rotor_trace, rotor_angle)
            outer_trace = jnp.where(interface[None, None, None, :], rotor_trace, outer_trace)
        normal_sign = 1.0 if face_number % 2 else -1.0
        jump_value = inner_trace - outer_trace
        flux_term = 0.5 * (normal_sign * mix_fields(jacobians[face_number // 2], jump_value) - dissipation[0] * jump_value)
        tendency = face_add(tendency, face_number, 6.0 * metric * flux_term)
    coupling = jnp.einsum('ij,j...->i...', spectral_matrix(inst_count, omega), state, precision=lax.Precision.HIGHEST)
    pseudo_step = courant_number / (metric * dissipation[0] + omega[0])
    result = state + pseudo_step * (tendency.reshape(state.shape) - coupling)
    live_mask = positions < jnp.take(counts, owners)
    return jnp.where(live_mask, result, jnp.float32(0.0))
```

```python
import functools
import math

import jax
import jax.numpy as jnp
import numpy as np
from jax import lax
from jax.experimental import pallas as pl
from jax.experimental.pallas import tpu as pltpu
from jax.sharding import PartitionSpec as P

RIM = 64
FIELDS = 5
MODES = 64
FACE = 16
TRACE = FIELDS * FACE
LANES = 128
COURANT = 0.5

VMEM = pl.BlockSpec(memory_space=pltpu.VMEM)
SMEM = pl.BlockSpec(memory_space=pltpu.SMEM)


def gll_table():
    nodes = np.array([-1.0, -1.0 / math.sqrt(5.0), 1.0 / math.sqrt(5.0), 1.0])
    barycentric = np.array(
        [1.0 / np.prod([nodes[j] - nodes[k] for k in range(4) if k != j]) for j in range(4)]
    )
    derivative = np.zeros((4, 4))
    for i in range(4):
        for j in range(4):
            if i != j:
                derivative[i, j] = barycentric[j] / barycentric[i] / (nodes[i] - nodes[j])
        derivative[i, i] = -np.sum(derivative[i])
    return derivative


def face_nodes(face):
    direction, index = face // 2, 3 * (face % 2)
    nodes = []
    for first in range(4):
        for second in range(4):
            if direction == 0:
                nodes.append(16 * index + 4 * first + second)
            elif direction == 1:
                nodes.append(16 * first + 4 * index + second)
            else:
                nodes.append(16 * first + 4 * second + index)
    return nodes


def operator_tables():
    derivative, identity = gll_table(), np.eye(4)
    along = [
        np.kron(np.kron(derivative, identity), identity),
        np.kron(np.kron(identity, derivative), identity),
        np.kron(np.kron(identity, identity), derivative),
    ]
    tables = [-table for table in along] + [np.zeros((MODES, MODES))]
    for face in range(6):
        sign = 1.0 if face % 2 else -1.0
        for node in face_nodes(face):
            tables[face // 2][node, node] += 3.0 * sign
            tables[3][node, node] -= 3.0
    return np.stack([np.concatenate([t, t], axis=1) for t in tables]).astype(np.float32)


def lift_table():
    table = np.zeros((MODES, 6 * TRACE), np.float32)
    for face in range(6):
        for m, node in enumerate(face_nodes(face)):
            for field in range(FIELDS):
                table[node, face * TRACE + field * FACE + m] = 1.0
    return table


def spectral_table(count):
    table = np.zeros((count, count))
    for i in range(count):
        for j in range(count):
            k = i - j
            if k == 0:
                table[i, j] = (count * count + 2.0) / (12.0 * count)
            else:
                parity = -1.0 if k % 2 else 1.0
                angle = math.pi * k / count
                table[i, j] = 0.5 * parity / math.tan(angle) + parity / (
                    2.0 * count * math.sin(angle) ** 2
                )
    return table.astype(np.float32)


def split(value):
    high = value.astype(jnp.bfloat16)
    low = (value - high.astype(jnp.float32)).astype(jnp.bfloat16)
    return high, low


def dot(a, b):
    return jnp.dot(a, b, preferred_element_type=jnp.float32)


def dot3(a_high, a_low, b_high, b_low):
    return dot(a_high, b_high) + (dot(a_high, b_low) + dot(a_low, b_high))


def read_trace(cells, tile, field, face):
    direction, index = face // 2, 3 * (face % 2)
    if direction == 0:
        return [(0, cells[tile, field, 16 * index : 16 * index + 16, :])]
    if direction == 1:
        return [
            (4 * a, cells[tile, field, 16 * a + 4 * index : 16 * a + 4 * index + 4, :])
            for a in range(4)
        ]
    return [(0, cells[tile, field, pl.ds(index, 16, stride=4), :])]


def gather_trace(cells, trace, face, positions):
    for tile in range(cells.shape[0]):
        for field in range(FIELDS):
            for row, block in read_trace(cells, tile, field, face ^ 1):
                first = field * FACE + row
                trace[first : first + block.shape[0], tile * LANES : (tile + 1) * LANES] = block
    columns = trace.shape[1]
    rows = lax.broadcasted_iota(jnp.int32, (columns, positions.shape[1]), 0)
    choice = jnp.where(rows == positions, 1.0, 0.0).astype(jnp.bfloat16)
    high, low = split(trace[...])
    return dot(high, choice) + dot(low, choice)


def prep_kernel(plane, state, pairs, rotor, head, tail, shift, tiles):
    n = lax.axis_size("space")
    me = lax.axis_index("space")
    for tile in range(plane // LANES):
        columns = slice(tile * LANES, (tile + 1) * LANES)
        source = slice(2 * RIM + tile * LANES, 2 * RIM + (tile + 1) * LANES)
        tiles[tile] = state[0, :, :, source]
        for field in range(FIELDS):
            [(_, block)] = read_trace(tiles, tile, field, 4)
            rotor[field * FACE : (field + 1) * FACE, columns] = block
    rows = FIELDS * MODES // 2
    lane = lax.broadcasted_iota(jnp.int32, (MODES // 2, 2 * RIM), 1)
    rim = []
    for field in range(FIELDS):
        for half in range(2):
            rim.append(state[0, field, 32 * half : 32 * half + 32, 0 : 2 * RIM])
    for k in range(FIELDS):
        top, bottom = rim[k], rim[k + FIELDS]
        head[32 * k : 32 * k + 32, :] = jnp.where(lane < RIM, top, pltpu.roll(bottom, RIM, 1))
        tail[32 * k : 32 * k + 32, :] = jnp.where(lane < RIM, pltpu.roll(top, RIM, 1), bottom)
    owners = (pairs[...] // plane).astype(jnp.float32)
    lowest = jnp.min(owners).astype(jnp.int32)
    highest = jnp.max(owners).astype(jnp.int32)
    base = jnp.where(highest - lowest <= 1, lowest, highest)
    shift[0] = lax.rem(base - me + n, n)


def own_kernel(state, neighbours, jacobians, dissipation, tables, lift, tendency, outer, lift_high, lift_low, trace, matrix, tiles):
    lane = lax.broadcasted_iota(jnp.int32, (1, 2 * MODES), 1)
    for g in range(FIELDS):
        for pair in range(3):
            block = None
            for d in range(3):
                left = jacobians[d, g, 2 * pair]
                right = jacobians[d, g, 2 * pair + 1] if 2 * pair + 1 < FIELDS else 0.0
                term = jnp.where(lane < MODES, left, right) * tables[d]
                block = term if block is None else block + term
            if g // 2 == pair:
                own = (lane >= MODES) == (g % 2 == 1)
                block = block + jnp.where(own, dissipation[0], 0.0) * tables[3]
            matrix[g * MODES : (g + 1) * MODES, pair * 128 : (pair + 1) * 128] = block
    matrix_high, matrix_low = split(matrix[:, : FIELDS * MODES])
    cells = state[0].reshape(FIELDS * MODES, state.shape[-1])
    cells_high, cells_low = split(cells)
    tendency[...] = dot3(matrix_high, matrix_low, cells_high, cells_low)

    column = lax.broadcasted_iota(jnp.int32, (1, 6 * TRACE), 1)
    for g in range(FIELDS):
        weights = jnp.zeros((1, 6 * TRACE), jnp.float32)
        for segment in reversed(range(6 * FIELDS)):
            face, field = segment // FIELDS, segment % FIELDS
            sign = 1.0 if face % 2 else -1.0
            value = 3.0 * sign * jacobians[face // 2, g, field]
            if field == g:
                value = value - 3.0 * dissipation[0]
            weights = jnp.where(column < (segment + 1) * FACE, value, weights)
        high, low = split(weights * lift[...])
        lift_high[g * MODES : (g + 1) * MODES, :] = high
        lift_low[g * MODES : (g + 1) * MODES, :] = low

    for tile in range(tiles.shape[0]):
        tiles[tile] = state[0, :, :, tile * LANES : (tile + 1) * LANES]
    for face in range(6):
        positions = neighbours[face : face + 1, :] - RIM
        outer[face * TRACE : (face + 1) * TRACE, :] = gather_trace(
            tiles, trace, face, positions
        )


def join_kernel(
    plane, state, metric, dissipation, omega, angle, counts, spectral, neighbours, pairs, shift,
    tendency, outer, lift_high, lift_low, before, after, first, second,
    partial, weights, rim, trace, joined, partners,
):
    n = lax.axis_size("space")
    me = lax.axis_index("space")
    inst_count = lax.axis_size("inst")
    inst = lax.axis_index("inst")
    elems = state.shape[-1]
    lane = lax.broadcasted_iota(jnp.int32, (MODES // 2, 2 * RIM), 1)
    for k in range(2 * FIELDS):
        field, half = k // 2, k % 2
        piece = pl.ds(32 * (k % FIELDS), 32)
        left, right = before[piece, :], after[piece, :]
        if k < FIELDS:
            right = pltpu.roll(right, RIM, 1)
        else:
            left = pltpu.roll(left, RIM, 1)
        rim[0, field, 32 * half : 32 * half + 32, :] = jnp.where(lane < RIM, left, right)
    for face in range(6):
        number = neighbours[face : face + 1, :]
        positions = jnp.where(
            number < RIM, number, jnp.where(number >= RIM + elems, number - elems, -1)
        )
        rows = pl.ds(face * TRACE, TRACE)
        joined[rows, :] = outer[rows, :] + gather_trace(rim, trace, face, positions)

    partners[:, :plane] = first[...]
    partners[:, plane:] = second[...]
    start = lax.rem(me + shift[0], n) * plane
    offset = pairs[...] - start
    offset = jnp.where(offset < 0, offset + n * plane, offset)
    rows = lax.broadcasted_iota(jnp.int32, (2 * plane, plane), 0)
    choice = jnp.where(rows == offset, 1.0, 0.0).astype(jnp.bfloat16)
    high, low = split(partners[...])
    picked = dot(high, choice) + dot(low, choice)
    turn = jnp.full((1, plane), angle[0], jnp.float32)
    cosine, sine = jnp.cos(turn), jnp.sin(turn)
    two, three = picked[2 * FACE : 3 * FACE], picked[3 * FACE : 4 * FACE]
    base = 5 * TRACE
    columns = pl.ds(2 * RIM, plane)
    joined[base : base + 2 * FACE, columns] = picked[: 2 * FACE]
    joined[base + 2 * FACE : base + 3 * FACE, columns] = cosine * two - sine * three
    joined[base + 3 * FACE : base + 4 * FACE, columns] = sine * two + cosine * three
    joined[base + 4 * FACE : base + 5 * FACE, columns] = picked[4 * FACE :]

    outer_high, outer_low = split(joined[...])
    change = tendency[...] - dot3(lift_high[...], lift_low[...], outer_high, outer_low)
    scale = metric[...]
    step = COURANT / (scale * dissipation[0] + omega[0])
    live = lax.broadcasted_iota(jnp.int32, (1, elems), 1) < counts[0]
    step = jnp.where(live, step, 0.0)
    keep = jnp.where(live, 1.0, 0.0) - step * (omega[0] * spectral[inst, inst])
    cells = state[0].reshape(FIELDS * MODES, elems)
    partial[0] = (keep * cells + (step * scale) * change).reshape(FIELDS, MODES, elems)
    for away in range(1, inst_count):
        other = lax.rem(inst + away, inst_count)
        weights[away - 1 : away, :] = -step * (omega[0] * spectral[inst, other])


def shards(
    state, metric, jacobians, dissipation, omega, rotor_angle, counts, neighbours, mortar_pairs
):
    elems = state.shape[-1]
    plane = mortar_pairs.shape[-1]
    n = lax.axis_size("space")
    inst_count = lax.axis_size("inst")
    f32 = jnp.float32
    rows = FIELDS * MODES

    others = [
        lax.ppermute(state, "inst", [((i + away) % inst_count, i) for i in range(inst_count)])
        for away in range(1, inst_count)
    ]

    rim_shape = jax.ShapeDtypeStruct((rows // 2, 2 * RIM), f32)
    rotor, head, tail, shift = pl.pallas_call(
        functools.partial(prep_kernel, plane),
        out_shape=(
            jax.ShapeDtypeStruct((TRACE, plane), f32),
            rim_shape,
            rim_shape,
            jax.ShapeDtypeStruct((1,), jnp.int32),
        ),
        in_specs=[VMEM, VMEM],
        out_specs=(VMEM, VMEM, VMEM, SMEM),
        scratch_shapes=[pltpu.VMEM((plane // LANES, FIELDS, MODES, LANES), f32)],
        name="prep",
    )(state, mortar_pairs)

    before = lax.ppermute(tail, "space", [(i, (i + 1) % n) for i in range(n)])
    after = lax.ppermute(head, "space", [((i + 1) % n, i) for i in range(n)])

    def fetch(away, block):
        if away % n == 0:
            return block
        return lax.ppermute(block, "space", [((i + away) % n, i) for i in range(n)])

    def branch(away, block):
        return fetch(away, block), fetch(away + 1, block)

    first, second = lax.switch(
        shift[0], [functools.partial(branch, away) for away in range(n)], rotor
    )

    tendency, outer, lift_high, lift_low = pl.pallas_call(
        own_kernel,
        out_shape=(
            jax.ShapeDtypeStruct((rows, elems), f32),
            jax.ShapeDtypeStruct((6 * TRACE, elems), f32),
            jax.ShapeDtypeStruct((rows, 6 * TRACE), jnp.bfloat16),
            jax.ShapeDtypeStruct((rows, 6 * TRACE), jnp.bfloat16),
        ),
        in_specs=[VMEM, VMEM, SMEM, SMEM, VMEM, VMEM],
        out_specs=(VMEM,) * 4,
        scratch_shapes=[pltpu.VMEM((TRACE, elems), f32), pltpu.VMEM((rows, 6 * MODES), f32), pltpu.VMEM((elems // LANES, FIELDS, MODES, LANES), f32)],
        compiler_params=pltpu.CompilerParams(vmem_limit_bytes=32 * 2**20),
        cost_estimate=pl.CostEstimate(
            flops=12 * TRACE * elems * elems * 2, bytes_accessed=4 * 1024 * 1024, transcendentals=0
        ),
        name="own",
    )(state, neighbours, jacobians, dissipation, jnp.asarray(operator_tables()), jnp.asarray(lift_table()))

    partial, weights = pl.pallas_call(
        functools.partial(join_kernel, plane),
        out_shape=(
            jax.ShapeDtypeStruct(state.shape, f32),
            jax.ShapeDtypeStruct((max(inst_count - 1, 1), elems), f32),
        ),
        in_specs=[VMEM, VMEM, SMEM, SMEM, SMEM, SMEM, SMEM, VMEM, VMEM, SMEM] + [VMEM] * 8,
        out_specs=(VMEM, VMEM),
        scratch_shapes=[
            pltpu.VMEM((1, FIELDS, MODES, 2 * RIM), f32),
            pltpu.VMEM((TRACE, 2 * RIM), f32),
            pltpu.VMEM((6 * TRACE, elems), f32),
            pltpu.VMEM((TRACE, 2 * plane), f32),
        ],
        compiler_params=pltpu.CompilerParams(vmem_limit_bytes=32 * 2**20),
        cost_estimate=pl.CostEstimate(
            flops=6 * TRACE * rows * elems * 6, bytes_accessed=4 * 1024 * 1024, transcendentals=0
        ),
        name="join",
    )(
        state, metric.reshape(1, elems), dissipation, omega, rotor_angle, counts,
        jnp.asarray(spectral_table(inst_count)), neighbours, mortar_pairs, shift,
        tendency, outer, lift_high, lift_low, before, after, first, second,
    )

    result = partial
    for away in range(1, inst_count):
        result = result + weights[away - 1] * others[away - 1]
    return result


def solution(mesh):
    return jax.shard_map(
        shards,
        mesh=mesh,
        in_specs=(
            P("inst", None, None, "space"),
            P("space"),
            P(),
            P(),
            P(),
            P("inst"),
            P("space"),
            P(None, "space"),
            P("inst", "space"),
        ),
        out_specs=P("inst", None, None, "space"),
        check_vma=False,
    )
```

```python
import functools
import math

import jax
import jax.numpy as jnp
import numpy as np
from jax import lax
from jax.experimental import pallas as pl
from jax.experimental.pallas import tpu as pltpu
from jax.sharding import PartitionSpec as P

RIM = 64
FIELDS = 5
MODES = 64
FACE = 16
TRACE = FIELDS * FACE
LANES = 128
COURANT = 0.5

VMEM = pl.BlockSpec(memory_space=pltpu.VMEM)
SMEM = pl.BlockSpec(memory_space=pltpu.SMEM)


def gll_table():
    nodes = np.array([-1.0, -1.0 / math.sqrt(5.0), 1.0 / math.sqrt(5.0), 1.0])
    barycentric = np.array(
        [1.0 / np.prod([nodes[j] - nodes[k] for k in range(4) if k != j]) for j in range(4)]
    )
    derivative = np.zeros((4, 4))
    for i in range(4):
        for j in range(4):
            if i != j:
                derivative[i, j] = barycentric[j] / barycentric[i] / (nodes[i] - nodes[j])
        derivative[i, i] = -np.sum(derivative[i])
    return derivative


def face_nodes(face):
    direction, index = face // 2, 3 * (face % 2)
    nodes = []
    for first in range(4):
        for second in range(4):
            if direction == 0:
                nodes.append(16 * index + 4 * first + second)
            elif direction == 1:
                nodes.append(16 * first + 4 * index + second)
            else:
                nodes.append(16 * first + 4 * second + index)
    return nodes


def operator_tables():
    derivative, identity = gll_table(), np.eye(4)
    along = [
        np.kron(np.kron(derivative, identity), identity),
        np.kron(np.kron(identity, derivative), identity),
        np.kron(np.kron(identity, identity), derivative),
    ]
    tables = [-table for table in along] + [np.zeros((MODES, MODES))]
    for face in range(6):
        sign = 1.0 if face % 2 else -1.0
        for node in face_nodes(face):
            tables[face // 2][node, node] += 3.0 * sign
            tables[3][node, node] -= 3.0
    return np.stack([np.concatenate([t, t], axis=1) for t in tables]).astype(np.float32)


def lift_table():
    table = np.zeros((MODES, 6 * TRACE), np.float32)
    for face in range(6):
        for m, node in enumerate(face_nodes(face)):
            for field in range(FIELDS):
                table[node, face * TRACE + field * FACE + m] = 1.0
    return table


def spectral_values(count):
    values = {0: (count * count + 2.0) / (12.0 * count)}
    for k in range(1 - count, count):
        if k:
            parity = -1.0 if k % 2 else 1.0
            angle = math.pi * k / count
            values[k] = 0.5 * parity / math.tan(angle) + parity / (
                2.0 * count * math.sin(angle) ** 2
            )
    return values


def split(value):
    high = value.astype(jnp.bfloat16)
    low = (value - high.astype(jnp.float32)).astype(jnp.bfloat16)
    return high, low


def dot(a, b):
    return jnp.dot(a, b, preferred_element_type=jnp.float32)


def dot3(a_high, a_low, b_high, b_low):
    return dot(a_high, b_high) + (dot(a_high, b_low) + dot(a_low, b_high))


def read_trace(cells, tile, field, face):
    direction, index = face // 2, 3 * (face % 2)
    if direction == 0:
        return [(0, cells[tile, field, 16 * index : 16 * index + 16, :])]
    if direction == 1:
        return [
            (4 * a, cells[tile, field, 16 * a + 4 * index : 16 * a + 4 * index + 4, :])
            for a in range(4)
        ]
    return [(0, cells[tile, field, pl.ds(index, 16, stride=4), :])]


def gather_trace(cells, trace, face, positions):
    for tile in range(cells.shape[0]):
        for field in range(FIELDS):
            for row, block in read_trace(cells, tile, field, face ^ 1):
                first = field * FACE + row
                trace[first : first + block.shape[0], tile * LANES : (tile + 1) * LANES] = block
    return pick(trace[...], positions)


def pick(values, positions):
    rows = lax.broadcasted_iota(jnp.int32, (values.shape[1], positions.shape[1]), 0)
    choice = jnp.where(rows == positions, 1.0, 0.0).astype(jnp.bfloat16)
    return dot(jnp.concatenate(split(values), axis=0), choice)


def prep_kernel(plane, state, pairs, rotor, head, tail, shift, rim, tiles, rim_sem, plane_sem):
    n = lax.axis_size("space")
    me = lax.axis_index("space")
    copies = [
        pltpu.make_async_copy(
            state.at[0, :, :, pl.ds(2 * RIM + tile * LANES, LANES)], tiles.at[tile], plane_sem.at[tile]
        )
        for tile in range(plane // LANES)
    ]
    copies.append(pltpu.make_async_copy(state.at[0, :, :, pl.ds(0, 2 * RIM)], rim, rim_sem))
    for copy in copies:
        copy.start()
    owners = (pairs[...] // plane).astype(jnp.float32)
    lowest = jnp.min(owners).astype(jnp.int32)
    highest = jnp.max(owners).astype(jnp.int32)
    base = jnp.where(highest - lowest <= 1, lowest, highest)
    shift[0] = lax.rem(base - me + n, n)
    for tile in range(plane // LANES):
        copies[tile].wait()
        for field in range(FIELDS):
            [(_, block)] = read_trace(tiles, tile, field, 4)
            rotor[field * FACE : (field + 1) * FACE, tile * LANES : (tile + 1) * LANES] = block
    copies[-1].wait()
    lane = lax.broadcasted_iota(jnp.int32, (MODES // 2, 2 * RIM), 1)
    pieces = [
        rim[field, 32 * half : 32 * half + 32, :] for field in range(FIELDS) for half in range(2)
    ]
    for k in range(FIELDS):
        top, bottom = pieces[k], pieces[k + FIELDS]
        head[32 * k : 32 * k + 32, :] = jnp.where(lane < RIM, top, pltpu.roll(bottom, RIM, 1))
        tail[32 * k : 32 * k + 32, :] = jnp.where(lane < RIM, pltpu.roll(top, RIM, 1), bottom)


def inside(positions, plane):
    column = lax.broadcasted_iota(jnp.int32, positions.shape, 1)
    return jnp.where((column >= 2 * RIM) & (column < 2 * RIM + plane), -1, positions)


def own_kernel(
    plane, state, neighbours, jacobians, dissipation, tables, lift,
    tendency, outer, lift_high, lift_low, trace, matrix, tiles,
):
    loss = dissipation[...]
    lane = lax.broadcasted_iota(jnp.int32, (1, 2 * MODES), 1)
    for g in range(FIELDS):
        for pair in range(3):
            block = None
            for d in range(3):
                row = jacobians[g, d : d + 1, :]
                left = row[:, 2 * pair : 2 * pair + 1]
                right = row[:, 2 * pair + 1 : 2 * pair + 2] if 2 * pair + 1 < FIELDS else 0.0
                term = jnp.where(lane < MODES, left, right) * tables[d]
                block = term if block is None else block + term
            if g // 2 == pair:
                own = (lane >= MODES) == (g % 2 == 1)
                block = block + jnp.where(own, loss, 0.0) * tables[3]
            matrix[g * MODES : (g + 1) * MODES, pair * 128 : (pair + 1) * 128] = block
    matrix_high, matrix_low = split(matrix[:, : FIELDS * MODES])
    cells = state[0].reshape(FIELDS * MODES, state.shape[-1])
    cells_high, cells_low = split(cells)
    tendency[...] = dot3(matrix_high, matrix_low, cells_high, cells_low)

    column = lax.broadcasted_iota(jnp.int32, (1, 6 * TRACE), 1)
    for g in range(FIELDS):
        weights = jnp.zeros((1, 6 * TRACE), jnp.float32)
        for segment in reversed(range(6 * FIELDS)):
            face, field = segment // FIELDS, segment % FIELDS
            sign = 1.0 if face % 2 else -1.0
            value = 3.0 * sign * jacobians[g, face // 2 : face // 2 + 1, field : field + 1]
            if field == g:
                value = value - 3.0 * loss
            weights = jnp.where(column < (segment + 1) * FACE, value, weights)
        high, low = split(weights * lift[...])
        lift_high[g * MODES : (g + 1) * MODES, :] = high
        lift_low[g * MODES : (g + 1) * MODES, :] = low

    for tile in range(tiles.shape[0]):
        tiles[tile] = state[0, :, :, tile * LANES : (tile + 1) * LANES]
    for face in range(6):
        positions = neighbours[face : face + 1, :] - RIM
        if face == 5:
            positions = inside(positions, plane)
        outer[2 * face * TRACE : 2 * (face + 1) * TRACE, :] = gather_trace(
            tiles, trace, face, positions
        ).astype(jnp.bfloat16)


def halo_kernel(
    plane, state, metric, dissipation, omega, angle, counts, neighbours, pairs,
    tendency, outer, lift_high, lift_low, before, after,
    partial, weights, turned, places, rim, trace, high, low,
):
    n = lax.axis_size("space")
    me = lax.axis_index("space")
    inst_count = lax.axis_size("inst")
    inst = lax.axis_index("inst")
    elems = state.shape[-1]
    lane = lax.broadcasted_iota(jnp.int32, (MODES // 2, 2 * RIM), 1)
    for k in range(2 * FIELDS):
        field, half = k // 2, k % 2
        piece = pl.ds(32 * (k % FIELDS), 32)
        left, right = before[piece, :], after[piece, :]
        if k < FIELDS:
            right = pltpu.roll(right, RIM, 1)
        else:
            left = pltpu.roll(left, RIM, 1)
        rim[0, field, 32 * half : 32 * half + 32, :] = jnp.where(lane < RIM, left, right)
    for face in range(6):
        number = neighbours[face : face + 1, :]
        positions = jnp.where(
            number < RIM, number, jnp.where(number >= RIM + elems, number - elems, -1)
        )
        if face == 5:
            positions = inside(positions, plane)
        found = gather_trace(rim, trace, face, positions)
        found = found + outer[2 * face * TRACE : 2 * (face + 1) * TRACE, :].astype(jnp.float32)
        high[face * TRACE : (face + 1) * TRACE, :] = found[:TRACE].astype(jnp.bfloat16)
        low[face * TRACE : (face + 1) * TRACE, :] = found[TRACE:].astype(jnp.bfloat16)

    change = tendency[...] - dot3(lift_high[...], lift_low[...], high[...], low[...])
    scale = metric[...]
    frequency = omega[...]
    step = COURANT / (scale * dissipation[...] + frequency)
    live = lax.broadcasted_iota(jnp.int32, (1, elems), 1) < counts[...]
    step = jnp.where(live, step, 0.0)
    spectral = spectral_values(inst_count)
    keep = jnp.where(live, 1.0, 0.0) - step * (frequency * spectral[0])
    cells = state[0].reshape(FIELDS * MODES, elems)
    partial[0] = (keep * cells + (step * scale) * change).reshape(FIELDS, MODES, elems)
    weights[0:1, :] = step * scale
    for away in range(1, inst_count):
        value = jnp.where(inst + away < inst_count, spectral[-away], spectral[inst_count - away])
        weights[away : away + 1, :] = -step * (frequency * value)

    base = 5 * TRACE
    face_lift = lift_high[:, base:].astype(jnp.float32) + lift_low[:, base:].astype(jnp.float32)
    cosine, sine = jnp.cos(angle[...]), jnp.sin(angle[...])
    column = lax.broadcasted_iota(jnp.int32, (1, TRACE), 1)
    two = (column >= 2 * FACE) & (column < 3 * FACE)
    three = (column >= 3 * FACE) & (column < 4 * FACE)
    same = jnp.where(two | three, cosine, 1.0)
    cross = jnp.where(two, sine, jnp.where(three, -sine, 0.0))
    other = jnp.concatenate(
        [
            face_lift[:, : 2 * FACE],
            face_lift[:, 3 * FACE : 4 * FACE],
            face_lift[:, 2 * FACE : 3 * FACE],
            face_lift[:, 4 * FACE :],
        ],
        axis=1,
    )
    turned_high, turned_low = split(same * face_lift + cross * other)
    turned[...] = jnp.concatenate([turned_high, turned_high, turned_low], axis=1)
    owners = (pairs[...] // plane).astype(jnp.float32)
    lowest = jnp.min(owners, axis=1, keepdims=True).astype(jnp.int32)
    highest = jnp.max(owners, axis=1, keepdims=True).astype(jnp.int32)
    start = jnp.where(highest - lowest <= 1, lowest, highest) * plane
    place = pairs[...] - start
    places[...] = jnp.where(place < 0, place + n * plane, place)


def final_kernel(plane, partial, weights, turned, places, first, second, *refs):
    inst_count = lax.axis_size("inst")
    others, (result, partners, buffer, sems) = refs[: inst_count - 1], refs[inst_count - 1 :]
    partners[:, :plane] = first[...]
    partners[:, plane:] = second[...]
    picked = pick(partners[...], places[...])
    high, low = picked[:TRACE].astype(jnp.bfloat16), picked[TRACE:].astype(jnp.bfloat16)
    columns = slice(2 * RIM, 2 * RIM + plane)
    slide = weights[0:1, columns] * dot(turned[...], jnp.concatenate([high, low, high], axis=0))
    for field in range(FIELDS):
        total = partial[0, field]
        for away in range(1, inst_count):
            total = total + weights[away : away + 1, :] * others[away - 1][0, field]
        buffer[field] = total
        buffer[field, :, columns] = (
            total[:, columns] - slide[field * MODES : (field + 1) * MODES]
        )
        pltpu.make_async_copy(buffer.at[field], result.at[0, field], sems.at[field]).start()
    for field in range(FIELDS):
        pltpu.make_async_copy(buffer.at[field], result.at[0, field], sems.at[field]).wait()


def shards(
    state, metric, jacobians, dissipation, omega, rotor_angle, counts, neighbours, mortar_pairs
):
    elems = state.shape[-1]
    plane = mortar_pairs.shape[-1]
    n = lax.axis_size("space")
    inst_count = lax.axis_size("inst")
    f32, bf16 = jnp.float32, jnp.bfloat16
    rows = FIELDS * MODES
    shape = jax.ShapeDtypeStruct
    mixing = jnp.transpose(jacobians, (1, 0, 2))
    loss = dissipation.reshape(1, 1)

    others = [
        lax.ppermute(state, "inst", [((i + away) % inst_count, i) for i in range(inst_count)])
        for away in range(1, inst_count)
    ]

    rotor, head, tail, shift = pl.pallas_call(
        functools.partial(prep_kernel, plane),
        out_shape=(
            shape((TRACE, plane), f32),
            shape((rows // 2, 2 * RIM), f32),
            shape((rows // 2, 2 * RIM), f32),
            shape((1,), jnp.int32),
        ),
        in_specs=[pl.BlockSpec(memory_space=pl.ANY), VMEM],
        out_specs=(VMEM, VMEM, VMEM, SMEM),
        scratch_shapes=[
            pltpu.VMEM((FIELDS, MODES, 2 * RIM), f32),
            pltpu.VMEM((plane // LANES, FIELDS, MODES, LANES), f32),
            pltpu.SemaphoreType.DMA,
            pltpu.SemaphoreType.DMA((plane // LANES,)),
        ],
        name="prep",
    )(state, mortar_pairs)

    before = lax.ppermute(tail, "space", [(i, (i + 1) % n) for i in range(n)])
    after = lax.ppermute(head, "space", [((i + 1) % n, i) for i in range(n)])

    def fetch(away, block):
        if away == 0:
            return block
        return lax.ppermute(block, "space", [((i + away) % n, i) for i in range(n)])

    def branch(away, block, state, neighbours, mixing, loss, tables, lift):
        first = fetch(away, block)
        own = pl.pallas_call(
            functools.partial(own_kernel, plane),
            out_shape=(
                shape((rows, elems), f32),
                shape((12 * TRACE, elems), bf16),
                shape((rows, 6 * TRACE), bf16),
                shape((rows, 6 * TRACE), bf16),
            ),
            in_specs=[VMEM] * 6,
            out_specs=(VMEM,) * 4,
            scratch_shapes=[
                pltpu.VMEM((TRACE, elems), f32),
                pltpu.VMEM((rows, 6 * MODES), f32),
                pltpu.VMEM((elems // LANES, FIELDS, MODES, LANES), f32),
            ],
            compiler_params=pltpu.CompilerParams(vmem_limit_bytes=32 * 2**20),
            cost_estimate=pl.CostEstimate(
                flops=24 * TRACE * elems * elems, bytes_accessed=2**22, transcendentals=0
            ),
            name="own",
        )(state, neighbours, mixing, loss, tables, lift)
        return first, own

    first, (tendency, outer, lift_high, lift_low) = lax.switch(
        shift[0],
        [functools.partial(branch, away) for away in range(n)],
        rotor, state, neighbours, mixing, loss,
        jnp.asarray(operator_tables()), jnp.asarray(lift_table()),
    )
    second = fetch(1, first)

    partial, weights, turned, places = pl.pallas_call(
        functools.partial(halo_kernel, plane),
        out_shape=(
            shape(state.shape, f32),
            shape((inst_count, elems), f32),
            shape((rows, 3 * TRACE), bf16),
            shape((1, plane), jnp.int32),
        ),
        in_specs=[VMEM] * 14,
        out_specs=(VMEM,) * 4,
        scratch_shapes=[
            pltpu.VMEM((1, FIELDS, MODES, 2 * RIM), f32),
            pltpu.VMEM((TRACE, 2 * RIM), f32),
            pltpu.VMEM((6 * TRACE, elems), bf16),
            pltpu.VMEM((6 * TRACE, elems), bf16),
        ],
        compiler_params=pltpu.CompilerParams(vmem_limit_bytes=32 * 2**20),
        cost_estimate=pl.CostEstimate(
            flops=36 * TRACE * rows * elems, bytes_accessed=2**22, transcendentals=0
        ),
        name="halo",
    )(
        state, metric.reshape(1, elems), loss, omega.reshape(1, 1), rotor_angle.reshape(1, 1),
        counts.reshape(1, 1), neighbours, mortar_pairs,
        tendency, outer, lift_high, lift_low, before, after,
    )

    return pl.pallas_call(
        functools.partial(final_kernel, plane),
        out_shape=shape(state.shape, f32),
        in_specs=[VMEM] * (5 + inst_count),
        out_specs=pl.BlockSpec(memory_space=pl.ANY),
        scratch_shapes=[
            pltpu.VMEM((TRACE, 2 * plane), f32),
            pltpu.VMEM((FIELDS, MODES, elems), f32),
            pltpu.SemaphoreType.DMA((FIELDS,)),
        ],
        compiler_params=pltpu.CompilerParams(vmem_limit_bytes=32 * 2**20),
        name="final",
    )(partial, weights, turned, places, first, second, *others)


def solution(mesh):
    return jax.shard_map(
        shards,
        mesh=mesh,
        in_specs=(
            P("inst", None, None, "space"),
            P("space"),
            P(),
            P(),
            P(),
            P("inst"),
            P("space"),
            P(None, "space"),
            P("inst", "space"),
        ),
        out_specs=P("inst", None, None, "space"),
        check_vma=False,
    )
```

```python
import functools
import math

import jax
import jax.numpy as jnp
import numpy as np
from jax import lax
from jax.experimental import pallas as pl
from jax.experimental.pallas import tpu as pltpu
from jax.sharding import PartitionSpec as P

RIM = 64
FIELDS = 5
MODES = 64
FACE = 16
TRACE = FIELDS * FACE
LANES = 128
COURANT = 0.5

VMEM = pl.BlockSpec(memory_space=pltpu.VMEM)
SMEM = pl.BlockSpec(memory_space=pltpu.SMEM)
ANY = pl.BlockSpec(memory_space=pl.ANY)


def gll_table():
    nodes = np.array([-1.0, -1.0 / math.sqrt(5.0), 1.0 / math.sqrt(5.0), 1.0])
    barycentric = np.array(
        [1.0 / np.prod([nodes[j] - nodes[k] for k in range(4) if k != j]) for j in range(4)]
    )
    derivative = np.zeros((4, 4))
    for i in range(4):
        for j in range(4):
            if i != j:
                derivative[i, j] = barycentric[j] / barycentric[i] / (nodes[i] - nodes[j])
        derivative[i, i] = -np.sum(derivative[i])
    return derivative


def face_nodes(face):
    direction, index = face // 2, 3 * (face % 2)
    nodes = []
    for first in range(4):
        for second in range(4):
            if direction == 0:
                nodes.append(16 * index + 4 * first + second)
            elif direction == 1:
                nodes.append(16 * first + 4 * index + second)
            else:
                nodes.append(16 * first + 4 * second + index)
    return nodes


def operator_tables():
    derivative, identity = gll_table(), np.eye(4)
    along = [
        np.kron(np.kron(derivative, identity), identity),
        np.kron(np.kron(identity, derivative), identity),
        np.kron(np.kron(identity, identity), derivative),
    ]
    tables = [-table for table in along] + [np.zeros((MODES, MODES))]
    for face in range(6):
        sign = 1.0 if face % 2 else -1.0
        for node in face_nodes(face):
            tables[face // 2][node, node] += 3.0 * sign
            tables[3][node, node] -= 3.0
    return np.stack([np.concatenate([t, t], axis=1) for t in tables]).astype(np.float32)


def spectral_values(count):
    values = {0: (count * count + 2.0) / (12.0 * count)}
    for k in range(1 - count, count):
        if k:
            parity = -1.0 if k % 2 else 1.0
            angle = math.pi * k / count
            values[k] = 0.5 * parity / math.tan(angle) + parity / (
                2.0 * count * math.sin(angle) ** 2
            )
    return values


def split(value):
    high = value.astype(jnp.bfloat16)
    low = (value - high.astype(jnp.float32)).astype(jnp.bfloat16)
    return high, low


def fetch_all(pairs, sems):
    copies = [
        pltpu.make_async_copy(source, target, sems.at[k]) for k, (source, target) in enumerate(pairs)
    ]
    for copy in copies:
        copy.start()
    return copies


def tile_of(number):
    return slice(number * LANES, (number + 1) * LANES)


def face_pieces(face):
    direction, index = face // 2, 3 * (face % 2)
    if direction == 0:
        return [(slice(0, 16), slice(16 * index, 16 * index + 16))]
    if direction == 1:
        return [
            (slice(4 * a, 4 * a + 4), slice(16 * a + 4 * index, 16 * a + 4 * index + 4))
            for a in range(4)
        ]
    return [(slice(0, 16), pl.ds(index, 16, stride=4))]


def load_trace(cells, tile, face, trace):
    for field in range(FIELDS):
        for rows, nodes in face_pieces(face):
            target = slice(field * FACE + rows.start, field * FACE + rows.stop)
            trace[tile, target, :] = cells[tile, field, nodes, :]


def choose(sources, positions):
    shape = sources[0].shape
    lane = jnp.broadcast_to(positions & (LANES - 1), shape)
    tile = jnp.broadcast_to(positions >> 7, shape)
    result = None
    for number, source in enumerate(sources):
        found = jnp.take_along_axis(source, lane, axis=1, mode="promise_in_bounds")
        result = found if result is None else jnp.where(tile == number, found, result)
    return result


def face_weight(mixing, loss, face, g, field):
    sign = 1.0 if face % 2 else -1.0
    value = (3.0 * sign) * mixing[g, face // 2, field]
    return value - 3.0 * loss[0] if g == field else value


def base_owner(pairs, plane):
    owners = (pairs // plane).astype(jnp.float32)
    lowest = jnp.min(owners, axis=1, keepdims=True).astype(jnp.int32)
    highest = jnp.max(owners, axis=1, keepdims=True).astype(jnp.int32)
    return jnp.where(highest - lowest <= 1, lowest, highest)


def prep_kernel(plane, state, pairs, rotor, head, tail, shift, pairs_here, rim, tiles, sems):
    n = lax.axis_size("space")
    me = lax.axis_index("space")
    count = plane // LANES
    copies = fetch_all(
        [(pairs, pairs_here)]
        + [
            (state.at[0, :, :, pl.ds(2 * RIM + tile * LANES, LANES)], tiles.at[tile])
            for tile in range(count)
        ]
        + [(state.at[0, :, :, pl.ds(0, 2 * RIM)], rim)],
        sems,
    )
    copies[0].wait()
    shift[0] = lax.rem(jnp.max(base_owner(pairs_here[...], plane)) - me + n, n)
    for tile in range(count):
        copies[1 + tile].wait()
        for field in range(FIELDS):
            rotor[field * FACE : (field + 1) * FACE, tile_of(tile)] = tiles[
                tile, field, pl.ds(0, FACE, stride=4), :
            ]
    copies[-1].wait()
    lane = lax.broadcasted_iota(jnp.int32, (MODES // 2, 2 * RIM), 1)
    pieces = [
        rim[field, 32 * half : 32 * half + 32, :] for field in range(FIELDS) for half in range(2)
    ]
    for k in range(FIELDS):
        top, bottom = pieces[k], pieces[k + FIELDS]
        head[32 * k : 32 * k + 32, :] = jnp.where(lane < RIM, top, pltpu.roll(bottom, RIM, 1))
        tail[32 * k : 32 * k + 32, :] = jnp.where(lane < RIM, pltpu.roll(top, RIM, 1), bottom)


def own_kernel(
    state, neighbours, jacobians, dissipation, tables,
    tendency, outer, mixing, loss, table, matrix, cells, trace, sems,
):
    copies = fetch_all([(jacobians, mixing), (dissipation, loss), (tables, table)], sems)
    count = cells.shape[0]

    for tile in range(count):
        cells[tile] = state[0, :, :, tile_of(tile)]
    for face in range(6):
        for tile in range(count):
            load_trace(cells, tile, face ^ 1, trace)
        for tile in range(count):
            outer[face, tile] = choose(
                [trace[source] for source in range(count)],
                neighbours[face : face + 1, tile_of(tile)] - RIM,
            )

    for copy in copies:
        copy.wait()
    lane = lax.broadcasted_iota(jnp.int32, (1, LANES), 1)
    order = [("high", f) for f in range(FIELDS)] * 2 + [("low", f) for f in range(FIELDS)]
    order.append(("low", None))
    for g in range(FIELDS):
        for pair in range(len(order) // 2):
            (part, left), (_, right) = order[2 * pair], order[2 * pair + 1]
            block = None
            for d in range(3):
                weight = jnp.where(
                    lane < MODES, mixing[g, d, left], 0.0 if right is None else mixing[g, d, right]
                )
                term = weight * table[d]
                block = term if block is None else block + term
            if g in (left, right):
                own = lane < MODES if g == left else lane >= MODES
                block = block + jnp.where(own, loss[0], 0.0) * table[3]
            if right is None:
                block = jnp.where(lane < MODES, block, 0.0)
            high, low = split(block)
            matrix[g * MODES : (g + 1) * MODES, tile_of(pair)] = high if part == "high" else low
    high, low = split(state[0].reshape(FIELDS * MODES, state.shape[-1]))
    stacked = jnp.concatenate([high, low, high, jnp.zeros_like(high[:MODES])], axis=0)
    product = jnp.dot(matrix[...], stacked, preferred_element_type=jnp.float32)
    for tile in range(count):
        tendency[tile] = product[:, tile_of(tile)].reshape(FIELDS, MODES, LANES)


def halo_kernel(
    plane, state, metric, jacobians, dissipation, omega, angle, counts, neighbours, pairs,
    tendency, outer, before, after, partial, weights, turned, places,
    metric_here, mixing, loss, frequency, turn, live_count, pairs_here, rim, trace, sems,
):
    n = lax.axis_size("space")
    inst_count = lax.axis_size("inst")
    inst = lax.axis_index("inst")
    count = partial.shape[0]
    copies = fetch_all(
        [
            (metric, metric_here),
            (jacobians, mixing),
            (dissipation, loss),
            (omega, frequency),
            (angle, turn),
            (counts, live_count),
            (pairs, pairs_here),
        ],
        sems,
    )
    elems = state.shape[-1]
    half_lane = lax.broadcasted_iota(jnp.int32, (MODES // 2, 2 * RIM), 1)
    for k in range(2 * FIELDS):
        field, half = k // 2, k % 2
        piece = pl.ds(32 * (k % FIELDS), 32)
        left, right = before[piece, :], after[piece, :]
        if k < FIELDS:
            right = pltpu.roll(right, RIM, 1)
        else:
            left = pltpu.roll(left, RIM, 1)
        rim[0, field, 32 * half : 32 * half + 32, :] = jnp.where(half_lane < RIM, left, right)
    for copy in copies:
        copy.wait()
    lane = lax.broadcasted_iota(jnp.int32, (1, LANES), 1)

    partial[...] = tendency[...]
    for face in range(6):
        load_trace(rim, 0, face ^ 1, trace)
        given = [
            [face_weight(mixing, loss, face, g, field) for field in range(FIELDS)]
            for g in range(FIELDS)
        ]
        for tile in range(count):
            number = neighbours[face : face + 1, tile_of(tile)]
            previous = number < RIM
            remote = previous | (number >= RIM + elems)
            found = choose([trace[0]], jnp.where(previous, number, number - elems))
            found = jnp.where(remote, found, outer[face, tile])
            if face == 5:
                column = lane + tile * LANES
                sliding = (column >= 2 * RIM) & (column < 2 * RIM + plane)
                found = jnp.where(sliding, 0.0, found)
            for g in range(FIELDS):
                lifted = None
                for field in range(FIELDS):
                    term = given[g][field] * found[field * FACE : (field + 1) * FACE]
                    lifted = term if lifted is None else lifted + term
                for rows, nodes in face_pieces(face):
                    partial[tile, g, nodes, :] = partial[tile, g, nodes, :] - lifted[rows]

    spectral = spectral_values(inst_count)
    for tile in range(count):
        scale = metric_here[:, tile_of(tile)]
        step = COURANT / (scale * loss[0] + frequency[0])
        live = lane + tile * LANES < live_count[0]
        step = jnp.where(live, step, 0.0)
        keep = jnp.where(live, 1.0, 0.0) - step * (frequency[0] * spectral[0])
        partial[tile] = keep * state[0, :, :, tile_of(tile)] + (step * scale) * partial[tile]
        weights[0:1, tile_of(tile)] = step * scale
        for away in range(1, inst_count):
            value = jnp.where(
                inst + away < inst_count, spectral[-away], spectral[inst_count - away]
            )
            weights[away : away + 1, tile_of(tile)] = -step * (frequency[0] * value)

    turns = jnp.full((1, LANES), turn[0], jnp.float32)
    cosine, sine = jnp.cos(turns), jnp.sin(turns)
    for g in range(FIELDS):
        given = [face_weight(mixing, loss, 5, g, field) for field in range(FIELDS)]
        for field in range(FIELDS):
            if field == 2:
                row = given[2] * cosine + given[3] * sine
            elif field == 3:
                row = given[3] * cosine - given[2] * sine
            else:
                row = jnp.full((1, LANES), given[field], jnp.float32)
            turned[g * FIELDS + field : g * FIELDS + field + 1, :] = row
    place = pairs_here[...] - base_owner(pairs_here[...], plane) * plane
    places[...] = jnp.where(place < 0, place + n * plane, place)


def final_kernel(plane, partial, weights, turned, places, first, second, *refs):
    inst_count = lax.axis_size("inst")
    others, (result, buffer, sems) = refs[: inst_count - 1], refs[inst_count - 1 :]
    count = buffer.shape[0]
    start, stop = 2 * RIM // LANES, (2 * RIM + plane) // LANES
    copies = []
    for tile in [*range(start, stop), *range(start), *range(stop, count)]:
        for field in range(FIELDS):
            total = partial[tile, field]
            for away in range(1, inst_count):
                row = weights[away : away + 1, tile_of(tile)]
                total = total + row * others[away - 1][0, field, :, tile_of(tile)]
            buffer[tile, field] = total
        if start <= tile < stop:
            positions = places[:, tile_of(tile - start)]
            found = choose(
                [
                    block[:, tile_of(source)]
                    for block in (first, second)
                    for source in range(plane // LANES)
                ],
                positions,
            )
            scale = weights[0:1, tile_of(tile)]
            for g in range(FIELDS):
                lifted = None
                for field in range(FIELDS):
                    row = g * FIELDS + field
                    term = turned[row : row + 1, :] * found[field * FACE : (field + 1) * FACE]
                    lifted = term if lifted is None else lifted + term
                [(_, nodes)] = face_pieces(5)
                buffer[tile, g, nodes, :] = buffer[tile, g, nodes, :] - scale * lifted
        copies.append(
            pltpu.make_async_copy(
                buffer.at[tile], result.at[0, :, :, pl.ds(tile * LANES, LANES)], sems.at[tile]
            )
        )
        copies[-1].start()
    for copy in copies:
        copy.wait()


def shards(
    state, metric, jacobians, dissipation, omega, rotor_angle, counts, neighbours, mortar_pairs
):
    elems = state.shape[-1]
    tiles = elems // LANES
    plane = mortar_pairs.shape[-1]
    n = lax.axis_size("space")
    inst_count = lax.axis_size("inst")
    f32 = jnp.float32
    shape = jax.ShapeDtypeStruct
    mixing = jnp.transpose(jacobians, (1, 0, 2))
    sems = pltpu.SemaphoreType.DMA
    scalar = pltpu.SMEM((1,), f32)
    mixing_here = pltpu.SMEM((FIELDS, 3, FIELDS), f32)
    params = pltpu.CompilerParams(vmem_limit_bytes=32 * 2**20)

    others = [
        lax.ppermute(state, "inst", [((i + away) % inst_count, i) for i in range(inst_count)])
        for away in range(1, inst_count)
    ]

    rotor, head, tail, shift = pl.pallas_call(
        functools.partial(prep_kernel, plane),
        out_shape=(
            shape((TRACE, plane), f32),
            shape((FIELDS * MODES // 2, 2 * RIM), f32),
            shape((FIELDS * MODES // 2, 2 * RIM), f32),
            shape((1,), jnp.int32),
        ),
        in_specs=[ANY, ANY],
        out_specs=(VMEM, VMEM, VMEM, SMEM),
        scratch_shapes=[
            pltpu.VMEM((1, plane), jnp.int32),
            pltpu.VMEM((FIELDS, MODES, 2 * RIM), f32),
            pltpu.VMEM((plane // LANES, FIELDS, MODES, LANES), f32),
            sems((plane // LANES + 2,)),
        ],
        name="prep",
    )(state, mortar_pairs)

    before = lax.ppermute(tail, "space", [(i, (i + 1) % n) for i in range(n)])
    after = lax.ppermute(head, "space", [((i + 1) % n, i) for i in range(n)])

    def fetch(away, block):
        if away == 0:
            return block
        return lax.ppermute(block, "space", [((i + away) % n, i) for i in range(n)])

    def branch(away, block, state, neighbours, mixing, loss, tables):
        first = fetch(away, block)
        own = pl.pallas_call(
            own_kernel,
            out_shape=(
                shape((tiles, FIELDS, MODES, LANES), f32),
                shape((6, tiles, TRACE, LANES), f32),
            ),
            in_specs=[VMEM, VMEM, ANY, ANY, ANY],
            out_specs=(VMEM, VMEM),
            scratch_shapes=[
                mixing_here,
                scalar,
                pltpu.VMEM((4, MODES, LANES), f32),
                pltpu.VMEM((FIELDS * MODES, 8 * LANES), jnp.bfloat16),
                pltpu.VMEM((tiles, FIELDS, MODES, LANES), f32),
                pltpu.VMEM((tiles, TRACE, LANES), f32),
                sems((3,)),
            ],
            compiler_params=params,
            cost_estimate=pl.CostEstimate(
                flops=2**31, bytes_accessed=2**22, transcendentals=0
            ),
            name="own",
        )(state, neighbours, mixing, loss, tables)
        return first, own

    first, (tendency, outer) = lax.switch(
        shift[0],
        [functools.partial(branch, away) for away in range(n)],
        rotor, state, neighbours, mixing, dissipation, jnp.asarray(operator_tables()),
    )
    second = fetch(1, first)

    partial, weights, turned, places = pl.pallas_call(
        functools.partial(halo_kernel, plane),
        out_shape=(
            shape((tiles, FIELDS, MODES, LANES), f32),
            shape((inst_count, elems), f32),
            shape((FIELDS * FIELDS, LANES), f32),
            shape((1, plane), jnp.int32),
        ),
        in_specs=[VMEM] + [ANY] * 6 + [VMEM, ANY] + [VMEM] * 4,
        out_specs=(VMEM,) * 4,
        scratch_shapes=[
            pltpu.VMEM((1, elems), f32),
            mixing_here,
            scalar,
            scalar,
            scalar,
            pltpu.SMEM((1,), jnp.int32),
            pltpu.VMEM((1, plane), jnp.int32),
            pltpu.VMEM((1, FIELDS, MODES, 2 * RIM), f32),
            pltpu.VMEM((1, TRACE, LANES), f32),
            sems((7,)),
        ],
        compiler_params=params,
        cost_estimate=pl.CostEstimate(flops=2**31, bytes_accessed=2**22, transcendentals=0),
        name="halo",
    )(
        state, metric.reshape(1, elems), mixing, dissipation, omega, rotor_angle, counts,
        neighbours, mortar_pairs, tendency, outer, before, after,
    )

    return pl.pallas_call(
        functools.partial(final_kernel, plane),
        out_shape=shape(state.shape, f32),
        in_specs=[VMEM] * (5 + inst_count),
        out_specs=ANY,
        scratch_shapes=[
            pltpu.VMEM((tiles, FIELDS, MODES, LANES), f32),
            sems((tiles,)),
        ],
        compiler_params=params,
        name="final",
    )(partial, weights, turned, places, first, second, *others)


def solution(mesh):
    return jax.shard_map(
        shards,
        mesh=mesh,
        in_specs=(
            P("inst", None, None, "space"),
            P("space"),
            P(),
            P(),
            P(),
            P("inst"),
            P("space"),
            P(None, "space"),
            P("inst", "space"),
        ),
        out_specs=P("inst", None, None, "space"),
        check_vma=False,
    )
```

```python
import functools
import math

import jax
import jax.numpy as jnp
import numpy as np
from jax import lax
from jax.experimental import pallas as pl
from jax.experimental.pallas import tpu as pltpu
from jax.sharding import PartitionSpec as P

RIM = 64
FIELDS = 5
MODES = 64
FACE = 16
TRACE = FIELDS * FACE
LANES = 128
COURANT = 0.5

VMEM = pl.BlockSpec(memory_space=pltpu.VMEM)
SMEM = pl.BlockSpec(memory_space=pltpu.SMEM)
ANY = pl.BlockSpec(memory_space=pl.ANY)


def gll_table():
    nodes = np.array([-1.0, -1.0 / math.sqrt(5.0), 1.0 / math.sqrt(5.0), 1.0])
    barycentric = np.array(
        [1.0 / np.prod([nodes[j] - nodes[k] for k in range(4) if k != j]) for j in range(4)]
    )
    derivative = np.zeros((4, 4))
    for i in range(4):
        for j in range(4):
            if i != j:
                derivative[i, j] = barycentric[j] / barycentric[i] / (nodes[i] - nodes[j])
        derivative[i, i] = -np.sum(derivative[i])
    return derivative


def face_nodes(face):
    direction, index = face // 2, 3 * (face % 2)
    nodes = []
    for first in range(4):
        for second in range(4):
            if direction == 0:
                nodes.append(16 * index + 4 * first + second)
            elif direction == 1:
                nodes.append(16 * first + 4 * index + second)
            else:
                nodes.append(16 * first + 4 * second + index)
    return nodes


def operator_tables():
    derivative, identity = gll_table(), np.eye(4)
    along = [
        np.kron(np.kron(derivative, identity), identity),
        np.kron(np.kron(identity, derivative), identity),
        np.kron(np.kron(identity, identity), derivative),
    ]
    tables = [-table for table in along] + [np.zeros((MODES, MODES))]
    for face in range(6):
        sign = 1.0 if face % 2 else -1.0
        for node in face_nodes(face):
            tables[face // 2][node, node] += 3.0 * sign
            tables[3][node, node] -= 3.0
    return np.stack([np.concatenate([t, t], axis=1) for t in tables]).astype(np.float32)


def spectral_values(count):
    values = {0: (count * count + 2.0) / (12.0 * count)}
    for k in range(1 - count, count):
        if k:
            parity = -1.0 if k % 2 else 1.0
            angle = math.pi * k / count
            values[k] = 0.5 * parity / math.tan(angle) + parity / (
                2.0 * count * math.sin(angle) ** 2
            )
    return values


def split(value):
    high = value.astype(jnp.bfloat16)
    low = (value - high.astype(jnp.float32)).astype(jnp.bfloat16)
    return high, low


def fetch_all(pairs, sems):
    copies = [
        pltpu.make_async_copy(source, target, sems.at[k]) for k, (source, target) in enumerate(pairs)
    ]
    for copy in copies:
        copy.start()
    return copies


def tile_of(number):
    return slice(number * LANES, (number + 1) * LANES)


def face_pieces(face):
    direction, index = face // 2, 3 * (face % 2)
    if direction == 0:
        return [(slice(0, 16), slice(16 * index, 16 * index + 16))]
    if direction == 1:
        return [
            (slice(4 * a, 4 * a + 4), slice(16 * a + 4 * index, 16 * a + 4 * index + 4))
            for a in range(4)
        ]
    return [(slice(0, 16), pl.ds(index, 16, stride=4))]


def load_trace(cells, tile, face, trace):
    for field in range(FIELDS):
        for rows, nodes in face_pieces(face):
            target = slice(field * FACE + rows.start, field * FACE + rows.stop)
            trace[tile, target, :] = cells[tile, field, nodes, :]


def choose(sources, positions):
    shape = sources[0].shape
    lane = jnp.broadcast_to(positions & (LANES - 1), shape)
    tile = jnp.broadcast_to(positions >> 7, shape)
    result = None
    for number, source in enumerate(sources):
        found = jnp.take_along_axis(source, lane, axis=1, mode="promise_in_bounds")
        result = found if result is None else jnp.where(tile == number, found, result)
    return result


def face_weight(mixing, loss, face, g, field):
    sign = 1.0 if face % 2 else -1.0
    value = (3.0 * sign) * mixing[g, face // 2, field]
    return value - 3.0 * loss[0] if g == field else value


def base_owner(pairs, plane):
    owners = (pairs // plane).astype(jnp.float32)
    lowest = jnp.min(owners, axis=1, keepdims=True).astype(jnp.int32)
    highest = jnp.max(owners, axis=1, keepdims=True).astype(jnp.int32)
    return jnp.where(highest - lowest <= 1, lowest, highest)


def prep_kernel(plane, state, pairs, rotor, far, near, shift, pairs_here, rim, tiles, sems):
    n = lax.axis_size("space")
    me = lax.axis_index("space")
    count = plane // LANES
    copies = fetch_all(
        [(pairs, pairs_here)]
        + [
            (state.at[0, :, :, pl.ds(2 * RIM + tile * LANES, LANES)], tiles.at[tile])
            for tile in range(count)
        ]
        + [(state.at[0, :, :, pl.ds(0, 2 * RIM)], rim)],
        sems,
    )
    copies[0].wait()
    shift[0] = lax.rem(jnp.max(base_owner(pairs_here[...], plane)) - me + n, n)
    for tile in range(count):
        copies[1 + tile].wait()
        for field in range(FIELDS):
            rotor[field * FACE : (field + 1) * FACE, tile_of(tile)] = tiles[
                tile, field, pl.ds(0, FACE, stride=4), :
            ]
    copies[-1].wait()
    odd = lax.rem(me, 2) == 1
    lane = lax.broadcasted_iota(jnp.int32, (MODES // 2, 2 * RIM), 1)
    pieces = [
        rim[field, 32 * half : 32 * half + 32, :] for field in range(FIELDS) for half in range(2)
    ]
    for k in range(FIELDS):
        top, bottom = pieces[k], pieces[k + FIELDS]
        head = jnp.where(lane < RIM, top, pltpu.roll(bottom, RIM, 1))
        tail = jnp.where(lane < RIM, pltpu.roll(top, RIM, 1), bottom)
        far[32 * k : 32 * k + 32, :] = jnp.where(odd, tail, head)
        near[32 * k : 32 * k + 32, :] = jnp.where(odd, head, tail)


def own_kernel(
    plane, state, neighbours, metric, jacobians, dissipation, omega, angle, counts, pairs, tables,
    tendency, outer, given, turned, weights, places,
    metric_here, mixing, loss, frequency, turn, live_count, pairs_here, table,
    matrix, cells, trace, sems,
):
    n = lax.axis_size("space")
    inst_count = lax.axis_size("inst")
    inst = lax.axis_index("inst")
    copies = fetch_all(
        [
            (jacobians, mixing),
            (dissipation, loss),
            (omega, frequency),
            (angle, turn),
            (counts, live_count),
            (metric, metric_here),
            (pairs, pairs_here),
            (tables, table),
        ],
        sems,
    )
    count = cells.shape[0]

    for tile in range(count):
        cells[tile] = state[0, :, :, tile_of(tile)]
    for face in range(6):
        for tile in range(count):
            load_trace(cells, tile, face ^ 1, trace)
        for tile in range(count):
            outer[face, tile] = choose(
                [trace[source] for source in range(count)],
                neighbours[face : face + 1, tile_of(tile)] - RIM,
            )

    for copy in copies:
        copy.wait()
    lane = lax.broadcasted_iota(jnp.int32, (1, LANES), 1)
    order = [("high", f) for f in range(FIELDS)] * 2 + [("low", f) for f in range(FIELDS)]
    order.append(("low", None))
    for g in range(FIELDS):
        for pair in range(len(order) // 2):
            (part, left), (_, right) = order[2 * pair], order[2 * pair + 1]
            block = None
            for d in range(3):
                weight = jnp.where(
                    lane < MODES, mixing[g, d, left], 0.0 if right is None else mixing[g, d, right]
                )
                term = weight * table[d]
                block = term if block is None else block + term
            if g in (left, right):
                own = lane < MODES if g == left else lane >= MODES
                block = block + jnp.where(own, loss[0], 0.0) * table[3]
            if right is None:
                block = jnp.where(lane < MODES, block, 0.0)
            high, low = split(block)
            matrix[g * MODES : (g + 1) * MODES, tile_of(pair)] = high if part == "high" else low
    high, low = split(state[0].reshape(FIELDS * MODES, state.shape[-1]))
    stacked = jnp.concatenate([high, low, high, jnp.zeros_like(high[:MODES])], axis=0)
    product = jnp.dot(matrix[...], stacked, preferred_element_type=jnp.float32)
    for tile in range(count):
        tendency[tile] = product[:, tile_of(tile)].reshape(FIELDS, MODES, LANES)

    turns = jnp.full((1, LANES), turn[0], jnp.float32)
    cosine, sine = jnp.cos(turns), jnp.sin(turns)
    for face in range(6):
        for g in range(FIELDS):
            row = (face * FIELDS + g) * FIELDS
            values = [face_weight(mixing, loss, face, g, field) for field in range(FIELDS)]
            for field in range(FIELDS):
                given[row + field : row + field + 1, :] = jnp.full((1, LANES), values[field])
            if face == 5:
                values[2], values[3] = (
                    values[2] * cosine + values[3] * sine,
                    values[3] * cosine - values[2] * sine,
                )
                for field in range(FIELDS):
                    row = g * FIELDS + field
                    turned[row : row + 1, :] = jnp.broadcast_to(values[field], (1, LANES))

    spectral = spectral_values(inst_count)
    scale = metric_here[...]
    step = COURANT / (scale * loss[0] + frequency[0])
    live = lax.broadcasted_iota(jnp.int32, scale.shape, 1) < live_count[0]
    step = jnp.where(live, step, 0.0)
    weights[0:1, :] = step * scale
    weights[1:2, :] = jnp.where(live, 1.0, 0.0) - step * (frequency[0] * spectral[0])
    for away in range(1, inst_count):
        value = jnp.where(inst + away < inst_count, spectral[-away], spectral[inst_count - away])
        weights[away + 1 : away + 2, :] = -step * (frequency[0] * value)

    place = pairs_here[...] - base_owner(pairs_here[...], plane) * plane
    places[...] = jnp.where(place < 0, place + n * plane, place)


def halo_kernel(
    plane, state, neighbours, weights, given, tendency, outer, from_far, from_near,
    partial, rim, trace,
):
    count = partial.shape[0]
    elems = state.shape[-1]
    odd = lax.rem(lax.axis_index("space"), 2) == 1
    half_lane = lax.broadcasted_iota(jnp.int32, (MODES // 2, 2 * RIM), 1)
    for k in range(2 * FIELDS):
        field, half = k // 2, k % 2
        piece = pl.ds(32 * (k % FIELDS), 32)
        left = jnp.where(odd, from_near[piece, :], from_far[piece, :])
        right = jnp.where(odd, from_far[piece, :], from_near[piece, :])
        if k < FIELDS:
            right = pltpu.roll(right, RIM, 1)
        else:
            left = pltpu.roll(left, RIM, 1)
        rim[0, field, 32 * half : 32 * half + 32, :] = jnp.where(half_lane < RIM, left, right)
    lane = lax.broadcasted_iota(jnp.int32, (1, LANES), 1)

    partial[...] = tendency[...]
    for face in range(6):
        load_trace(rim, 0, face ^ 1, trace)
        for tile in range(count):
            number = neighbours[face : face + 1, tile_of(tile)]
            previous = number < RIM
            remote = previous | (number >= RIM + elems)
            found = choose([trace[0]], jnp.where(previous, number, number - elems))
            found = jnp.where(remote, found, outer[face, tile])
            if face == 5:
                column = lane + tile * LANES
                sliding = (column >= 2 * RIM) & (column < 2 * RIM + plane)
                found = jnp.where(sliding, 0.0, found)
            lift(partial, tile, face, mix(given, face, found), 1.0)
    for tile in range(count):
        scale, keep = weights[0:1, tile_of(tile)], weights[1:2, tile_of(tile)]
        partial[tile] = keep * state[0, :, :, tile_of(tile)] + scale * partial[tile]


def mix(given, face, found):
    mixed = []
    for g in range(FIELDS):
        total = None
        for field in range(FIELDS):
            row = (face * FIELDS + g) * FIELDS + field
            term = given[row : row + 1, :] * found[field * FACE : (field + 1) * FACE]
            total = term if total is None else total + term
        mixed.append(total)
    return mixed


def lift(cells, tile, face, mixed, scale):
    for g in range(FIELDS):
        change = scale * mixed[g]
        for rows, nodes in face_pieces(face):
            cells[tile, g, nodes, :] = cells[tile, g, nodes, :] - change[rows]


def final_kernel(plane, partial, weights, turned, places, first, second, *refs):
    inst_count = lax.axis_size("inst")
    others, (result, buffer, sems) = refs[: inst_count - 1], refs[inst_count - 1 :]
    count = buffer.shape[0]
    start, stop = 2 * RIM // LANES, (2 * RIM + plane) // LANES
    copies = []
    for tile in [*range(start, stop), *range(start), *range(stop, count)]:
        for field in range(FIELDS):
            total = partial[tile, field]
            for away in range(1, inst_count):
                row = weights[away + 1 : away + 2, tile_of(tile)]
                total = total + row * others[away - 1][0, field, :, tile_of(tile)]
            buffer[tile, field] = total
        if start <= tile < stop:
            positions = places[:, tile_of(tile - start)]
            found = choose(
                [
                    block[:, tile_of(source)]
                    for block in (first, second)
                    for source in range(plane // LANES)
                ],
                positions,
            )
            lift(buffer, tile, 5, mix(turned, 0, found), weights[0:1, tile_of(tile)])
        copies.append(
            pltpu.make_async_copy(
                buffer.at[tile], result.at[0, :, :, pl.ds(tile * LANES, LANES)], sems.at[tile]
            )
        )
        copies[-1].start()
    for copy in copies:
        copy.wait()


def shards(
    state, metric, jacobians, dissipation, omega, rotor_angle, counts, neighbours, mortar_pairs
):
    elems = state.shape[-1]
    tiles = elems // LANES
    plane = mortar_pairs.shape[-1]
    n = lax.axis_size("space")
    inst_count = lax.axis_size("inst")
    f32 = jnp.float32
    shape = jax.ShapeDtypeStruct
    mixing = jnp.transpose(jacobians, (1, 0, 2))
    sems = pltpu.SemaphoreType.DMA
    scalar = pltpu.SMEM((1,), f32)
    params = pltpu.CompilerParams(vmem_limit_bytes=32 * 2**20)

    others = [
        lax.ppermute(state, "inst", [((i + away) % inst_count, i) for i in range(inst_count)])
        for away in range(1, inst_count)
    ]

    rotor, far, near, shift = pl.pallas_call(
        functools.partial(prep_kernel, plane),
        out_shape=(
            shape((TRACE, plane), f32),
            shape((FIELDS * MODES // 2, 2 * RIM), f32),
            shape((FIELDS * MODES // 2, 2 * RIM), f32),
            shape((1,), jnp.int32),
        ),
        in_specs=[ANY, ANY],
        out_specs=(VMEM, VMEM, VMEM, SMEM),
        scratch_shapes=[
            pltpu.VMEM((1, plane), jnp.int32),
            pltpu.VMEM((FIELDS, MODES, 2 * RIM), f32),
            pltpu.VMEM((plane // LANES, FIELDS, MODES, LANES), f32),
            sems((plane // LANES + 2,)),
        ],
        name="prep",
    )(state, mortar_pairs)

    def fetch(away, block):
        if away == 0:
            return block
        return lax.ppermute(block, "space", [((i + away) % n, i) for i in range(n)])

    ends = [(i, (i + 1) % n) for i in range(1, n, 2)]
    middles = [(i, i + 1) for i in range(0, n, 2)]

    def swap(pairs, block):
        return lax.ppermute(block, "space", pairs + [(j, i) for i, j in pairs])

    def branch(away, rotor, far, near, *operands):
        first = fetch(away, rotor)
        from_far, from_near = swap(ends, far), swap(middles, near)
        own = pl.pallas_call(
            functools.partial(own_kernel, plane),
            out_shape=(
                shape((tiles, FIELDS, MODES, LANES), f32),
                shape((6, tiles, TRACE, LANES), f32),
                shape((6 * FIELDS * FIELDS, LANES), f32),
                shape((FIELDS * FIELDS, LANES), f32),
                shape((inst_count + 1, elems), f32),
                shape((1, plane), jnp.int32),
            ),
            in_specs=[VMEM, VMEM] + [ANY] * 8,
            out_specs=(VMEM,) * 6,
            scratch_shapes=[
                pltpu.VMEM((1, elems), f32),
                pltpu.SMEM((FIELDS, 3, FIELDS), f32),
                scalar,
                scalar,
                scalar,
                pltpu.SMEM((1,), jnp.int32),
                pltpu.VMEM((1, plane), jnp.int32),
                pltpu.VMEM((4, MODES, LANES), f32),
                pltpu.VMEM((FIELDS * MODES, 8 * LANES), jnp.bfloat16),
                pltpu.VMEM((tiles, FIELDS, MODES, LANES), f32),
                pltpu.VMEM((tiles, TRACE, LANES), f32),
                sems((8,)),
            ],
            compiler_params=params,
            cost_estimate=pl.CostEstimate(
                flops=2**31, bytes_accessed=2**22, transcendentals=0
            ),
            name="own",
        )(*operands)
        return first, from_far, from_near, own

    first, from_far, from_near, own = lax.switch(
        shift[0],
        [functools.partial(branch, away) for away in range(n)],
        rotor, far, near, state, neighbours, metric.reshape(1, elems), mixing, dissipation, omega,
        rotor_angle, counts, mortar_pairs, jnp.asarray(operator_tables()),
    )
    tendency, outer, given, turned, weights, places = own
    second = fetch(1, first)

    partial = pl.pallas_call(
        functools.partial(halo_kernel, plane),
        out_shape=shape((tiles, FIELDS, MODES, LANES), f32),
        in_specs=[VMEM] * 8,
        out_specs=VMEM,
        scratch_shapes=[
            pltpu.VMEM((1, FIELDS, MODES, 2 * RIM), f32),
            pltpu.VMEM((1, TRACE, LANES), f32),
        ],
        compiler_params=params,
        cost_estimate=pl.CostEstimate(flops=2**31, bytes_accessed=2**22, transcendentals=0),
        name="halo",
    )(state, neighbours, weights, given, tendency, outer, from_far, from_near)

    return pl.pallas_call(
        functools.partial(final_kernel, plane),
        out_shape=shape(state.shape, f32),
        in_specs=[VMEM] * (5 + inst_count),
        out_specs=ANY,
        scratch_shapes=[
            pltpu.VMEM((tiles, FIELDS, MODES, LANES), f32),
            sems((tiles,)),
        ],
        compiler_params=params,
        name="final",
    )(partial, weights, turned, places, first, second, *others)


def solution(mesh):
    return jax.shard_map(
        shards,
        mesh=mesh,
        in_specs=(
            P("inst", None, None, "space"),
            P("space"),
            P(),
            P(),
            P(),
            P("inst"),
            P("space"),
            P(None, "space"),
            P("inst", "space"),
        ),
        out_specs=P("inst", None, None, "space"),
        check_vma=False,
    )
```

```python
import functools
import math

import jax
import jax.numpy as jnp
import numpy as np
from jax import lax
from jax.experimental import pallas as pl
from jax.experimental.pallas import tpu as pltpu
from jax.sharding import PartitionSpec as P

RIM = 64
FIELDS = 5
MODES = 64
FACE = 16
TRACE = FIELDS * FACE
LANES = 128
COURANT = 0.5

VMEM = pl.BlockSpec(memory_space=pltpu.VMEM)
SMEM = pl.BlockSpec(memory_space=pltpu.SMEM)
ANY = pl.BlockSpec(memory_space=pl.ANY)


def gll_table():
    nodes = np.array([-1.0, -1.0 / math.sqrt(5.0), 1.0 / math.sqrt(5.0), 1.0])
    barycentric = np.array(
        [1.0 / np.prod([nodes[j] - nodes[k] for k in range(4) if k != j]) for j in range(4)]
    )
    derivative = np.zeros((4, 4))
    for i in range(4):
        for j in range(4):
            if i != j:
                derivative[i, j] = barycentric[j] / barycentric[i] / (nodes[i] - nodes[j])
        derivative[i, i] = -np.sum(derivative[i])
    return derivative


def face_nodes(face):
    direction, index = face // 2, 3 * (face % 2)
    nodes = []
    for first in range(4):
        for second in range(4):
            if direction == 0:
                nodes.append(16 * index + 4 * first + second)
            elif direction == 1:
                nodes.append(16 * first + 4 * index + second)
            else:
                nodes.append(16 * first + 4 * second + index)
    return nodes


def operator_tables():
    derivative, identity = gll_table(), np.eye(4)
    along = [
        np.kron(np.kron(derivative, identity), identity),
        np.kron(np.kron(identity, derivative), identity),
        np.kron(np.kron(identity, identity), derivative),
    ]
    tables = [-table for table in along] + [np.zeros((MODES, MODES))]
    for face in range(6):
        sign = 1.0 if face % 2 else -1.0
        for node in face_nodes(face):
            tables[face // 2][node, node] += 3.0 * sign
            tables[3][node, node] -= 3.0
    return np.stack([np.concatenate([t, t], axis=1) for t in tables]).astype(np.float32)


def spectral_values(count):
    values = {0: (count * count + 2.0) / (12.0 * count)}
    for k in range(1 - count, count):
        if k:
            parity = -1.0 if k % 2 else 1.0
            angle = math.pi * k / count
            values[k] = 0.5 * parity / math.tan(angle) + parity / (
                2.0 * count * math.sin(angle) ** 2
            )
    return values


def split(value):
    high = value.astype(jnp.bfloat16)
    low = (value - high.astype(jnp.float32)).astype(jnp.bfloat16)
    return high, low


def fetch_all(pairs, sems):
    copies = [
        pltpu.make_async_copy(source, target, sems.at[k]) for k, (source, target) in enumerate(pairs)
    ]
    for copy in copies:
        copy.start()
    return copies


def tile_of(number):
    return slice(number * LANES, (number + 1) * LANES)


def face_pieces(face):
    direction, index = face // 2, 3 * (face % 2)
    if direction == 0:
        return [(slice(0, 16), slice(16 * index, 16 * index + 16))]
    if direction == 1:
        return [
            (slice(4 * a, 4 * a + 4), slice(16 * a + 4 * index, 16 * a + 4 * index + 4))
            for a in range(4)
        ]
    return [(slice(0, 16), pl.ds(index, 16, stride=4))]


def load_trace(cells, tile, face, trace):
    for field in range(FIELDS):
        for rows, nodes in face_pieces(face):
            target = slice(field * FACE + rows.start, field * FACE + rows.stop)
            trace[tile, target, :] = cells[tile, field, nodes, :]


def choose(sources, positions):
    shape = sources[0].shape
    lane = jnp.broadcast_to(positions & (LANES - 1), shape)
    tile = jnp.broadcast_to(positions >> 7, shape)
    result = None
    for number, source in enumerate(sources):
        found = jnp.take_along_axis(source, lane, axis=1, mode="promise_in_bounds")
        result = found if result is None else jnp.where(tile == number, found, result)
    return result


def base_owner(pairs, plane):
    owners = (pairs // plane).astype(jnp.float32)
    lowest = jnp.min(owners, axis=1, keepdims=True).astype(jnp.int32)
    highest = jnp.max(owners, axis=1, keepdims=True).astype(jnp.int32)
    return jnp.where(highest - lowest <= 1, lowest, highest)


def prep_kernel(plane, state, pairs, rotor, far, near, shift, pairs_here, rim, tiles, sems):
    n = lax.axis_size("space")
    me = lax.axis_index("space")
    count = plane // LANES
    copies = fetch_all(
        [(pairs, pairs_here)]
        + [
            (state.at[0, :, :, pl.ds(2 * RIM + tile * LANES, LANES)], tiles.at[tile])
            for tile in range(count)
        ]
        + [(state.at[0, :, :, pl.ds(0, 2 * RIM)], rim)],
        sems,
    )
    copies[0].wait()
    shift[0] = lax.rem(jnp.max(base_owner(pairs_here[...], plane)) - me + n, n)
    for tile in range(count):
        copies[1 + tile].wait()
        for field in range(FIELDS):
            rotor[field * FACE : (field + 1) * FACE, tile_of(tile)] = tiles[
                tile, field, pl.ds(0, FACE, stride=4), :
            ]
    copies[-1].wait()
    odd = lax.rem(me, 2) == 1
    lane = lax.broadcasted_iota(jnp.int32, (MODES // 2, 2 * RIM), 1)
    pieces = [
        rim[field, 32 * half : 32 * half + 32, :] for field in range(FIELDS) for half in range(2)
    ]
    for k in range(FIELDS):
        top, bottom = pieces[k], pieces[k + FIELDS]
        head = jnp.where(lane < RIM, top, pltpu.roll(bottom, RIM, 1))
        tail = jnp.where(lane < RIM, pltpu.roll(top, RIM, 1), bottom)
        far[32 * k : 32 * k + 32, :] = jnp.where(odd, tail, head)
        near[32 * k : 32 * k + 32, :] = jnp.where(odd, head, tail)


def own_kernel(
    plane, state, neighbours, metric, jacobians, dissipation, omega, angle, counts, pairs, tables,
    tendency, outer, frame, weights, places,
    metric_here, mixing, loss, frequency, turn, live_count, pairs_here, table,
    matrix, cells, trace, sems,
):
    n = lax.axis_size("space")
    inst_count = lax.axis_size("inst")
    inst = lax.axis_index("inst")
    copies = fetch_all(
        [
            (jacobians, mixing),
            (dissipation, loss),
            (omega, frequency),
            (angle, turn),
            (counts, live_count),
            (metric, metric_here),
            (pairs, pairs_here),
            (tables, table),
        ],
        sems,
    )
    count = cells.shape[0]

    for tile in range(count):
        cells[tile] = state[0, :, :, tile_of(tile)]
    for face in range(6):
        for tile in range(count):
            load_trace(cells, tile, face ^ 1, trace)
        for tile in range(count):
            outer[face, tile] = choose(
                [trace[source] for source in range(count)],
                neighbours[face : face + 1, tile_of(tile)] - RIM,
            )

    for copy in copies:
        copy.wait()
    lane = lax.broadcasted_iota(jnp.int32, (1, LANES), 1)
    order = [("high", f) for f in range(FIELDS)] * 2 + [("low", f) for f in range(FIELDS)]
    order.append(("low", None))
    for g in range(FIELDS):
        for pair in range(len(order) // 2):
            (part, left), (_, right) = order[2 * pair], order[2 * pair + 1]
            block = None
            for d in range(3):
                weight = jnp.where(
                    lane < MODES, mixing[g, d, left], 0.0 if right is None else mixing[g, d, right]
                )
                term = weight * table[d]
                block = term if block is None else block + term
            if g in (left, right):
                own = lane < MODES if g == left else lane >= MODES
                block = block + jnp.where(own, loss[0], 0.0) * table[3]
            if right is None:
                block = jnp.where(lane < MODES, block, 0.0)
            high, low = split(block)
            matrix[g * MODES : (g + 1) * MODES, tile_of(pair)] = high if part == "high" else low
    high, low = split(state[0].reshape(FIELDS * MODES, state.shape[-1]))
    stacked = jnp.concatenate([high, low, high, jnp.zeros_like(high[:MODES])], axis=0)
    product = jnp.dot(matrix[...], stacked, preferred_element_type=jnp.float32)
    for tile in range(count):
        tendency[tile] = product[:, tile_of(tile)].reshape(FIELDS, MODES, LANES)

    turns = jnp.full((1, LANES), turn[0], jnp.float32)
    frame[0:1, :] = jnp.cos(turns)
    frame[1:2, :] = jnp.sin(turns)
    frame[2:3, :] = jnp.full((1, LANES), 3.0 * loss[0], jnp.float32)

    spectral = spectral_values(inst_count)
    scale = metric_here[...]
    step = COURANT / (scale * loss[0] + frequency[0])
    live = lax.broadcasted_iota(jnp.int32, scale.shape, 1) < live_count[0]
    step = jnp.where(live, step, 0.0)
    weights[0:1, :] = step * scale
    weights[1:2, :] = jnp.where(live, 1.0, 0.0) - step * (frequency[0] * spectral[0])
    for away in range(1, inst_count):
        value = jnp.where(inst + away < inst_count, spectral[-away], spectral[inst_count - away])
        weights[away + 1 : away + 2, :] = -step * (frequency[0] * value)

    place = pairs_here[...] - base_owner(pairs_here[...], plane) * plane
    places[...] = jnp.where(place < 0, place + n * plane, place)


def join_kernel(
    plane, state, neighbours, weights, frame, places, jacobians, tendency, outer,
    from_far, from_near, first, second, partial, mixing, rim, trace, sems,
):
    [copy] = fetch_all([(jacobians, mixing)], sems)
    count = partial.shape[0]
    elems = state.shape[-1]
    odd = lax.rem(lax.axis_index("space"), 2) == 1
    half_lane = lax.broadcasted_iota(jnp.int32, (MODES // 2, 2 * RIM), 1)
    for k in range(2 * FIELDS):
        field, half = k // 2, k % 2
        piece = pl.ds(32 * (k % FIELDS), 32)
        left = jnp.where(odd, from_near[piece, :], from_far[piece, :])
        right = jnp.where(odd, from_far[piece, :], from_near[piece, :])
        if k < FIELDS:
            right = pltpu.roll(right, RIM, 1)
        else:
            left = pltpu.roll(left, RIM, 1)
        rim[0, field, 32 * half : 32 * half + 32, :] = jnp.where(half_lane < RIM, left, right)
    partial[...] = tendency[...]
    copy.wait()

    start, stop = 2 * RIM // LANES, (2 * RIM + plane) // LANES
    for face in range(6):
        load_trace(rim, 0, face ^ 1, trace)
        for tile in range(count):
            if face == 5 and start <= tile < stop:
                found = choose(
                    [
                        block[:, tile_of(source)]
                        for block in (first, second)
                        for source in range(plane // LANES)
                    ],
                    places[:, tile_of(tile - start)],
                )
                parts = [found[field * FACE : (field + 1) * FACE] for field in range(FIELDS)]
                cosine, sine = frame[0:1, :], frame[1:2, :]
                parts[2], parts[3] = (
                    cosine * parts[2] - sine * parts[3],
                    sine * parts[2] + cosine * parts[3],
                )
            else:
                number = neighbours[face : face + 1, tile_of(tile)]
                previous = number < RIM
                remote = previous | (number >= RIM + elems)
                found = choose([trace[0]], jnp.where(previous, number, number - elems))
                found = jnp.where(remote, found, outer[face, tile])
                parts = [found[field * FACE : (field + 1) * FACE] for field in range(FIELDS)]
            for g in range(FIELDS):
                change = -frame[2:3, :] * parts[g]
                for field in range(FIELDS):
                    sign = 3.0 if face % 2 else -3.0
                    change = change + (sign * mixing[g, face // 2, field]) * parts[field]
                for rows, nodes in face_pieces(face):
                    partial[tile, g, nodes, :] = partial[tile, g, nodes, :] - change[rows]
    for tile in range(count):
        scale, keep = weights[0:1, tile_of(tile)], weights[1:2, tile_of(tile)]
        partial[tile] = keep * state[0, :, :, tile_of(tile)] + scale * partial[tile]


def final_kernel(partial, weights, *refs):
    inst_count = lax.axis_size("inst")
    others, (result, buffer, sems) = refs[: inst_count - 1], refs[inst_count - 1 :]
    copies = []
    for tile in range(buffer.shape[0]):
        for field in range(FIELDS):
            total = partial[tile, field]
            for away in range(1, inst_count):
                row = weights[away + 1 : away + 2, tile_of(tile)]
                total = total + row * others[away - 1][0, field, :, tile_of(tile)]
            buffer[tile, field] = total
        copies.append(
            pltpu.make_async_copy(
                buffer.at[tile], result.at[0, :, :, pl.ds(tile * LANES, LANES)], sems.at[tile]
            )
        )
        copies[-1].start()
    for copy in copies:
        copy.wait()


def shards(
    state, metric, jacobians, dissipation, omega, rotor_angle, counts, neighbours, mortar_pairs
):
    elems = state.shape[-1]
    tiles = elems // LANES
    plane = mortar_pairs.shape[-1]
    n = lax.axis_size("space")
    inst_count = lax.axis_size("inst")
    f32 = jnp.float32
    shape = jax.ShapeDtypeStruct
    mixing = jnp.transpose(jacobians, (1, 0, 2))
    sems = pltpu.SemaphoreType.DMA
    scalar = pltpu.SMEM((1,), f32)
    params = pltpu.CompilerParams(vmem_limit_bytes=32 * 2**20)

    others = [
        lax.ppermute(state, "inst", [((i + away) % inst_count, i) for i in range(inst_count)])
        for away in range(1, inst_count)
    ]

    rotor, far, near, shift = pl.pallas_call(
        functools.partial(prep_kernel, plane),
        out_shape=(
            shape((TRACE, plane), f32),
            shape((FIELDS * MODES // 2, 2 * RIM), f32),
            shape((FIELDS * MODES // 2, 2 * RIM), f32),
            shape((1,), jnp.int32),
        ),
        in_specs=[ANY, ANY],
        out_specs=(VMEM, VMEM, VMEM, SMEM),
        scratch_shapes=[
            pltpu.VMEM((1, plane), jnp.int32),
            pltpu.VMEM((FIELDS, MODES, 2 * RIM), f32),
            pltpu.VMEM((plane // LANES, FIELDS, MODES, LANES), f32),
            sems((plane // LANES + 2,)),
        ],
        name="prep",
    )(state, mortar_pairs)

    def fetch(away, block):
        if away % n == 0:
            return block
        return lax.ppermute(block, "space", [((i + away) % n, i) for i in range(n)])

    ends = [(i, (i + 1) % n) for i in range(1, n, 2)]
    middles = [(i, i + 1) for i in range(0, n, 2)]

    def swap(pairs, block):
        return lax.ppermute(block, "space", pairs + [(j, i) for i, j in pairs])

    def branch(away, rotor, far, near, *operands):
        first, second = fetch(away, rotor), fetch(away + 1, rotor)
        from_far, from_near = swap(ends, far), swap(middles, near)
        own = pl.pallas_call(
            functools.partial(own_kernel, plane),
            out_shape=(
                shape((tiles, FIELDS, MODES, LANES), f32),
                shape((6, tiles, TRACE, LANES), f32),
                shape((8, LANES), f32),
                shape((inst_count + 1, elems), f32),
                shape((1, plane), jnp.int32),
            ),
            in_specs=[VMEM, VMEM] + [ANY] * 8,
            out_specs=(VMEM,) * 5,
            scratch_shapes=[
                pltpu.VMEM((1, elems), f32),
                pltpu.SMEM((FIELDS, 3, FIELDS), f32),
                scalar,
                scalar,
                scalar,
                pltpu.SMEM((1,), jnp.int32),
                pltpu.VMEM((1, plane), jnp.int32),
                pltpu.VMEM((4, MODES, LANES), f32),
                pltpu.VMEM((FIELDS * MODES, 8 * LANES), jnp.bfloat16),
                pltpu.VMEM((tiles, FIELDS, MODES, LANES), f32),
                pltpu.VMEM((tiles, TRACE, LANES), f32),
                sems((8,)),
            ],
            compiler_params=params,
            cost_estimate=pl.CostEstimate(
                flops=2**31, bytes_accessed=2**22, transcendentals=0
            ),
            name="own",
        )(*operands)
        return first, second, from_far, from_near, own

    first, second, from_far, from_near, own = lax.switch(
        shift[0],
        [functools.partial(branch, away) for away in range(n)],
        rotor, far, near, state, neighbours, metric.reshape(1, elems), mixing, dissipation, omega,
        rotor_angle, counts, mortar_pairs, jnp.asarray(operator_tables()),
    )
    tendency, outer, frame, weights, places = own

    partial = pl.pallas_call(
        functools.partial(join_kernel, plane),
        out_shape=shape((tiles, FIELDS, MODES, LANES), f32),
        in_specs=[VMEM] * 5 + [ANY] + [VMEM] * 6,
        out_specs=VMEM,
        scratch_shapes=[
            pltpu.SMEM((FIELDS, 3, FIELDS), f32),
            pltpu.VMEM((1, FIELDS, MODES, 2 * RIM), f32),
            pltpu.VMEM((1, TRACE, LANES), f32),
            sems((1,)),
        ],
        compiler_params=params,
        cost_estimate=pl.CostEstimate(flops=2**31, bytes_accessed=2**22, transcendentals=0),
        name="join",
    )(
        state, neighbours, weights, frame, places, mixing, tendency, outer,
        from_far, from_near, first, second,
    )

    return pl.pallas_call(
        final_kernel,
        out_shape=shape(state.shape, f32),
        in_specs=[VMEM] * (1 + inst_count),
        out_specs=ANY,
        scratch_shapes=[
            pltpu.VMEM((tiles, FIELDS, MODES, LANES), f32),
            sems((tiles,)),
        ],
        compiler_params=params,
        name="final",
    )(partial, weights, *others)


def solution(mesh):
    return jax.shard_map(
        shards,
        mesh=mesh,
        in_specs=(
            P("inst", None, None, "space"),
            P("space"),
            P(),
            P(),
            P(),
            P("inst"),
            P("space"),
            P(None, "space"),
            P("inst", "space"),
        ),
        out_specs=P("inst", None, None, "space"),
        check_vma=False,
    )
```

```python
import functools
import math

import jax
import jax.numpy as jnp
import numpy as np
from jax import lax
from jax.experimental import pallas as pl
from jax.experimental.pallas import tpu as pltpu
from jax.sharding import PartitionSpec as P

RIM = 64
FIELDS = 5
MODES = 64
FACE = 16
TRACE = FIELDS * FACE
LANES = 128
COURANT = 0.5

VMEM = pl.BlockSpec(memory_space=pltpu.VMEM)
SMEM = pl.BlockSpec(memory_space=pltpu.SMEM)
ANY = pl.BlockSpec(memory_space=pl.ANY)
HBM = pl.BlockSpec(memory_space=pltpu.HBM)


def gll_table():
    nodes = np.array([-1.0, -1.0 / math.sqrt(5.0), 1.0 / math.sqrt(5.0), 1.0])
    barycentric = np.array(
        [1.0 / np.prod([nodes[j] - nodes[k] for k in range(4) if k != j]) for j in range(4)]
    )
    derivative = np.zeros((4, 4))
    for i in range(4):
        for j in range(4):
            if i != j:
                derivative[i, j] = barycentric[j] / barycentric[i] / (nodes[i] - nodes[j])
        derivative[i, i] = -np.sum(derivative[i])
    return derivative


def face_nodes(face):
    direction, index = face // 2, 3 * (face % 2)
    nodes = []
    for first in range(4):
        for second in range(4):
            if direction == 0:
                nodes.append(16 * index + 4 * first + second)
            elif direction == 1:
                nodes.append(16 * first + 4 * index + second)
            else:
                nodes.append(16 * first + 4 * second + index)
    return nodes


def operator_tables():
    derivative, identity = gll_table(), np.eye(4)
    along = [
        np.kron(np.kron(derivative, identity), identity),
        np.kron(np.kron(identity, derivative), identity),
        np.kron(np.kron(identity, identity), derivative),
    ]
    tables = [-table for table in along] + [np.zeros((MODES, MODES))]
    for face in range(6):
        sign = 1.0 if face % 2 else -1.0
        for node in face_nodes(face):
            tables[face // 2][node, node] += 3.0 * sign
            tables[3][node, node] -= 3.0
    return np.stack([np.concatenate([t, t], axis=1) for t in tables]).astype(np.float32)


def spectral_values(count):
    values = {0: (count * count + 2.0) / (12.0 * count)}
    for k in range(1 - count, count):
        if k:
            parity = -1.0 if k % 2 else 1.0
            angle = math.pi * k / count
            values[k] = 0.5 * parity / math.tan(angle) + parity / (
                2.0 * count * math.sin(angle) ** 2
            )
    return values


def split(value):
    high = value.astype(jnp.bfloat16)
    low = (value - high.astype(jnp.float32)).astype(jnp.bfloat16)
    return high, low


def fetch_all(pairs, sems):
    copies = [
        pltpu.make_async_copy(source, target, sems.at[k]) for k, (source, target) in enumerate(pairs)
    ]
    for copy in copies:
        copy.start()
    return copies


def tile_of(number):
    return slice(number * LANES, (number + 1) * LANES)


def face_pieces(face):
    direction, index = face // 2, 3 * (face % 2)
    if direction == 0:
        return [(slice(0, 16), slice(16 * index, 16 * index + 16))]
    if direction == 1:
        return [
            (slice(4 * a, 4 * a + 4), slice(16 * a + 4 * index, 16 * a + 4 * index + 4))
            for a in range(4)
        ]
    return [(slice(0, 16), pl.ds(index, 16, stride=4))]


def load_trace(cells, tile, face, trace):
    for field in range(FIELDS):
        for rows, nodes in face_pieces(face):
            target = slice(field * FACE + rows.start, field * FACE + rows.stop)
            trace[tile, target, :] = cells[tile, field, nodes, :]


def choose(sources, positions):
    shape = sources[0].shape
    lane = jnp.broadcast_to(positions & (LANES - 1), shape)
    tile = jnp.broadcast_to(positions >> 7, shape)
    result = None
    for number, source in enumerate(sources):
        found = jnp.take_along_axis(source, lane, axis=1, mode="promise_in_bounds")
        result = found if result is None else jnp.where(tile == number, found, result)
    return result


def face_weight(mixing, loss, face, g, field):
    sign = 1.0 if face % 2 else -1.0
    value = (3.0 * sign) * mixing[g, face // 2, field]
    return value - 3.0 * loss if g == field else value


def base_owner(pairs, plane):
    owners = (pairs // plane).astype(jnp.float32)
    lowest = jnp.min(owners, axis=1, keepdims=True).astype(jnp.int32)
    highest = jnp.max(owners, axis=1, keepdims=True).astype(jnp.int32)
    return jnp.where(highest - lowest <= 1, lowest, highest)


def prep_kernel(
    plane, state, pairs, metric, jacobians, rotor, far, near, shift, metric_here, mixing,
    pairs_here, rim, tiles, sems,
):
    n = lax.axis_size("space")
    me = lax.axis_index("space")
    count = plane // LANES
    copies = fetch_all(
        [(pairs, pairs_here)]
        + [
            (state.at[0, :, :, pl.ds(2 * RIM + tile * LANES, LANES)], tiles.at[tile])
            for tile in range(count)
        ]
        + [(state.at[0, :, :, pl.ds(0, 2 * RIM)], rim)]
        + [(metric, metric_here), (jacobians, mixing)],
        sems,
    )
    copies[0].wait()
    shift[0] = lax.rem(jnp.max(base_owner(pairs_here[...], plane)) - me + n, n)
    for tile in range(count):
        copies[1 + tile].wait()
        for field in range(FIELDS):
            rotor[field * FACE : (field + 1) * FACE, tile_of(tile)] = tiles[
                tile, field, pl.ds(0, FACE, stride=4), :
            ]
    for copy in copies[count + 1 :]:
        copy.wait()
    odd = lax.rem(me, 2) == 1
    lane = lax.broadcasted_iota(jnp.int32, (MODES // 2, 2 * RIM), 1)
    pieces = [
        rim[field, 32 * half : 32 * half + 32, :] for field in range(FIELDS) for half in range(2)
    ]
    for k in range(FIELDS):
        top, bottom = pieces[k], pieces[k + FIELDS]
        head = jnp.where(lane < RIM, top, pltpu.roll(bottom, RIM, 1))
        tail = jnp.where(lane < RIM, pltpu.roll(top, RIM, 1), bottom)
        far[32 * k : 32 * k + 32, :] = jnp.where(odd, tail, head)
        near[32 * k : 32 * k + 32, :] = jnp.where(odd, head, tail)


def own_kernel(
    state, neighbours, jacobians, dissipation, omega, angle, counts, tables,
    tendency, outer, scalars, mixing, loss, frequency, turn, live_count, table,
    matrix, cells, trace, sems,
):
    copies = fetch_all(
        [
            (jacobians, mixing),
            (dissipation, loss),
            (omega, frequency),
            (angle, turn),
            (counts, live_count),
            (tables, table),
        ],
        sems,
    )
    count = cells.shape[0]
    elems = state.shape[-1]

    for tile in range(count):
        cells[tile] = state[0, :, :, tile_of(tile)]
    row_number = lax.broadcasted_iota(jnp.int32, (elems, elems), 0)
    for face in range(6):
        for tile in range(count):
            load_trace(cells, tile, face ^ 1, trace.at[face])
        sources = [trace[face, source] for source in range(count)]
        positions = neighbours[face : face + 1, :] - RIM
        if face % 2:
            parts = jnp.concatenate(split(jnp.concatenate(sources, axis=1)), axis=0)
            matches = jnp.where(row_number == positions, 1.0, 0.0).astype(jnp.bfloat16)
            found = jnp.dot(parts, matches, preferred_element_type=jnp.float32)
            for tile in range(count):
                outer[face, tile] = found[:TRACE, tile_of(tile)] + found[TRACE:, tile_of(tile)]
        else:
            for tile in range(count):
                outer[face, tile] = choose(sources, positions[:, tile_of(tile)])

    for copy in copies:
        copy.wait()
    for row, value in enumerate(
        [loss[0], frequency[0], turn[0], live_count[0].astype(jnp.float32)]
    ):
        scalars[row : row + 1, :] = jnp.full((1, LANES), value)
    lane = lax.broadcasted_iota(jnp.int32, (1, LANES), 1)
    layout = [((0, 1), 0, 5), ((2, 3), 1, 6), ((4, 0), 2, 7), ((1, 2), 3, None), ((3, 4), 4, None)]
    for g in range(FIELDS):
        rows = slice(g * MODES, (g + 1) * MODES)
        values = [
            [jnp.full((1, LANES), mixing[g, d, field]) for field in range(FIELDS)] for d in range(3)
        ]
        for (left, right), high_place, low_place in layout:
            block = None
            for d in range(3):
                term = jnp.where(lane < MODES, values[d][left], values[d][right]) * table[d]
                block = term if block is None else block + term
            if g in (left, right):
                own = lane < MODES if g == left else lane >= MODES
                block = block + jnp.where(own, loss[0], 0.0) * table[3]
            high, low = split(block)
            matrix[rows, tile_of(high_place)] = high
            if low_place is not None:
                if left == FIELDS - 1:
                    low = jnp.where(lane < MODES, low, jnp.zeros_like(low))
                matrix[rows, tile_of(low_place)] = low
    high, low = split(state[0].reshape(FIELDS * MODES, elems))
    stacked = jnp.concatenate([high, low, high, jnp.zeros_like(high[:MODES])], axis=0)
    product = jnp.dot(matrix[...], stacked, preferred_element_type=jnp.float32)
    for tile in range(count):
        tendency[tile] = product[:, tile_of(tile)].reshape(FIELDS, MODES, LANES)


def face_weight(mixing, loss, face, g, field):
    sign = 1.0 if face % 2 else -1.0
    value = (3.0 * sign) * mixing[g, face // 2, field]
    return value - 3.0 * loss if g == field else value


def halo_kernel(
    plane, state, metric, jacobians, scalars, neighbours, pairs, tendency, outer,
    from_far, from_near, partial, weights, turned, places, mixing, rim, trace, sem,
):
    n = lax.axis_size("space")
    inst_count = lax.axis_size("inst")
    inst = lax.axis_index("inst")
    count = partial.shape[0]
    copy = pltpu.make_async_copy(jacobians, mixing, sem)
    copy.start()
    elems = state.shape[-1]
    odd = lax.rem(lax.axis_index("space"), 2) == 1
    half_lane = lax.broadcasted_iota(jnp.int32, (MODES // 2, 2 * RIM), 1)
    for k in range(2 * FIELDS):
        field, half = k // 2, k % 2
        piece = pl.ds(32 * (k % FIELDS), 32)
        left = jnp.where(odd, from_near[piece, :], from_far[piece, :])
        right = jnp.where(odd, from_far[piece, :], from_near[piece, :])
        if k < FIELDS:
            right = pltpu.roll(right, RIM, 1)
        else:
            left = pltpu.roll(left, RIM, 1)
        rim[0, field, 32 * half : 32 * half + 32, :] = jnp.where(half_lane < RIM, left, right)
    for face in range(6):
        load_trace(rim, 0, face ^ 1, trace.at[pl.ds(face, 1)])
    partial[...] = tendency[...]
    copy.wait()
    loss, frequency, turn, live_count = [scalars[row : row + 1, :] for row in range(4)]
    lane = lax.broadcasted_iota(jnp.int32, (1, LANES), 1)

    for face in range(6):
        given = [
            [face_weight(mixing, loss, face, g, field) for field in range(FIELDS)]
            for g in range(FIELDS)
        ]
        for tile in range(count):
            number = neighbours[face : face + 1, tile_of(tile)]
            previous = number < RIM
            remote = previous | (number >= RIM + elems)
            found = choose([trace[face]], jnp.where(previous, number, number - elems))
            found = jnp.where(remote, found, outer[face, tile])
            if face == 5:
                column = lane + tile * LANES
                sliding = (column >= 2 * RIM) & (column < 2 * RIM + plane)
                found = jnp.where(sliding, 0.0, found)
            lift(partial, tile, face, mix(given, found), 1.0)

    spectral = spectral_values(inst_count)
    for tile in range(count):
        scale = metric[:, tile_of(tile)]
        step = COURANT / (scale * loss + frequency)
        live = (lane + tile * LANES).astype(jnp.float32) < live_count
        step = jnp.where(live, step, 0.0)
        keep = jnp.where(live, 1.0, 0.0) - step * (frequency * spectral[0])
        partial[tile] = keep * state[0, :, :, tile_of(tile)] + (step * scale) * partial[tile]
        weights[0:1, tile_of(tile)] = step * scale
        for away in range(1, inst_count):
            value = jnp.where(
                inst + away < inst_count, spectral[-away], spectral[inst_count - away]
            )
            weights[away : away + 1, tile_of(tile)] = -step * (frequency * value)

    cosine, sine = jnp.cos(turn), jnp.sin(turn)
    for g in range(FIELDS):
        values = [face_weight(mixing, loss, 5, g, field) for field in range(FIELDS)]
        values[2], values[3] = (
            values[2] * cosine + values[3] * sine,
            values[3] * cosine - values[2] * sine,
        )
        for field in range(FIELDS):
            row = g * FIELDS + field
            turned[row : row + 1, :] = jnp.broadcast_to(values[field], (1, LANES))
    place = pairs[...] - base_owner(pairs[...], plane) * plane
    places[...] = jnp.where(place < 0, place + n * plane, place)


def mix(given, found):
    mixed = []
    for row in given:
        total = None
        for field in range(FIELDS):
            term = row[field] * found[field * FACE : (field + 1) * FACE]
            total = term if total is None else total + term
        mixed.append(total)
    return mixed


def lift(cells, tile, face, mixed, scale):
    for g in range(FIELDS):
        change = scale * mixed[g]
        for rows, nodes in face_pieces(face):
            cells[tile, g, nodes, :] = cells[tile, g, nodes, :] - change[rows]


def final_kernel(plane, partial, weights, turned, places, first, second, *refs):
    inst_count = lax.axis_size("inst")
    others, (result, buffer, sems) = refs[: inst_count - 1], refs[inst_count - 1 :]
    count = buffer.shape[0]
    start, stop = 2 * RIM // LANES, (2 * RIM + plane) // LANES
    copies = []
    for tile in [*range(start, stop), *range(start), *range(stop, count)]:
        for field in range(FIELDS):
            total = partial[tile, field]
            for away in range(1, inst_count):
                row = weights[away : away + 1, tile_of(tile)]
                total = total + row * others[away - 1][0, field, :, tile_of(tile)]
            buffer[tile, field] = total
        if start <= tile < stop:
            positions = places[:, tile_of(tile - start)]
            found = choose(
                [
                    block[:, tile_of(source)]
                    for block in (first, second)
                    for source in range(plane // LANES)
                ],
                positions,
            )
            given = [
                [turned[row : row + 1, :] for row in range(g * FIELDS, (g + 1) * FIELDS)]
                for g in range(FIELDS)
            ]
            lift(buffer, tile, 5, mix(given, found), weights[0:1, tile_of(tile)])
        copies.append(
            pltpu.make_async_copy(
                buffer.at[tile], result.at[0, :, :, pl.ds(tile * LANES, LANES)], sems.at[tile]
            )
        )
        copies[-1].start()
    for copy in copies:
        copy.wait()


def shards(
    state, metric, jacobians, dissipation, omega, rotor_angle, counts, neighbours, mortar_pairs
):
    elems = state.shape[-1]
    tiles = elems // LANES
    plane = mortar_pairs.shape[-1]
    n = lax.axis_size("space")
    inst_count = lax.axis_size("inst")
    f32 = jnp.float32
    shape = jax.ShapeDtypeStruct
    sems = pltpu.SemaphoreType.DMA
    scalar = pltpu.SMEM((1,), f32)
    mixing_here = pltpu.SMEM((FIELDS, 3, FIELDS), f32)
    params = pltpu.CompilerParams(vmem_limit_bytes=32 * 2**20)

    others = [
        lax.ppermute(state, "inst", [((i + away) % inst_count, i) for i in range(inst_count)])
        for away in range(1, inst_count)
    ]

    rotor, far, near, shift, metric_row, mixing, pairs_row = pl.pallas_call(
        functools.partial(prep_kernel, plane),
        out_shape=(
            shape((TRACE, plane), f32),
            shape((FIELDS * MODES // 2, 2 * RIM), f32),
            shape((FIELDS * MODES // 2, 2 * RIM), f32),
            shape((1,), jnp.int32),
            shape((1, elems), f32),
            shape((FIELDS, 3, FIELDS), f32),
            shape((1, plane), jnp.int32),
        ),
        in_specs=[HBM] * 4,
        out_specs=(VMEM, VMEM, VMEM, SMEM, VMEM, VMEM, VMEM),
        scratch_shapes=[
            pltpu.VMEM((FIELDS, MODES, 2 * RIM), f32),
            pltpu.VMEM((plane // LANES, FIELDS, MODES, LANES), f32),
            sems((plane // LANES + 4,)),
        ],
        name="prep",
    )(state, mortar_pairs, metric.reshape(1, elems), jnp.transpose(jacobians, (1, 0, 2)))

    def fetch(away, block):
        if away == 0:
            return block
        return lax.ppermute(block, "space", [((i + away) % n, i) for i in range(n)])

    ends = [(i, (i + 1) % n) for i in range(1, n, 2)]
    middles = [(i, i + 1) for i in range(0, n, 2)]

    def swap(pairs, block):
        return lax.ppermute(block, "space", pairs + [(j, i) for i, j in pairs])

    def branch(away, rotor, far, near, *operands):
        first = fetch(away, rotor)
        from_far, from_near = swap(ends, far), swap(middles, near)
        own = pl.pallas_call(
            own_kernel,
            out_shape=(
                shape((tiles, FIELDS, MODES, LANES), f32),
                shape((6, tiles, TRACE, LANES), f32),
                shape((8, LANES), f32),
            ),
            in_specs=[VMEM] * 3 + [HBM] * 5,
            out_specs=(VMEM,) * 3,
            scratch_shapes=[
                mixing_here,
                scalar,
                scalar,
                scalar,
                pltpu.SMEM((1,), jnp.int32),
                pltpu.VMEM((4, MODES, LANES), f32),
                pltpu.VMEM((FIELDS * MODES, 8 * LANES), jnp.bfloat16),
                pltpu.VMEM((tiles, FIELDS, MODES, LANES), f32),
                pltpu.VMEM((6, tiles, TRACE, LANES), f32),
                sems((6,)),
            ],
            compiler_params=params,
            cost_estimate=pl.CostEstimate(
                flops=2**31, bytes_accessed=2**22, transcendentals=0
            ),
            name="own",
        )(*operands)
        return first, from_far, from_near, own

    first, from_far, from_near, (tendency, outer, scalars) = lax.switch(
        shift[0],
        [functools.partial(branch, away) for away in range(n)],
        rotor, far, near, state, neighbours, mixing, dissipation, omega, rotor_angle, counts,
        jnp.asarray(operator_tables()),
    )
    second = fetch(1, first)

    partial, weights, turned, places = pl.pallas_call(
        functools.partial(halo_kernel, plane),
        out_shape=(
            shape((tiles, FIELDS, MODES, LANES), f32),
            shape((inst_count, elems), f32),
            shape((FIELDS * FIELDS, LANES), f32),
            shape((1, plane), jnp.int32),
        ),
        in_specs=[VMEM] * 10,
        out_specs=(VMEM,) * 4,
        scratch_shapes=[
            mixing_here,
            pltpu.VMEM((1, FIELDS, MODES, 2 * RIM), f32),
            pltpu.VMEM((6, TRACE, LANES), f32),
            sems,
        ],
        compiler_params=params,
        cost_estimate=pl.CostEstimate(flops=2**31, bytes_accessed=2**22, transcendentals=0),
        name="halo",
    )(
        state, metric_row, mixing, scalars, neighbours, pairs_row, tendency, outer,
        from_far, from_near,
    )

    return pl.pallas_call(
        functools.partial(final_kernel, plane),
        out_shape=shape(state.shape, f32),
        in_specs=[VMEM] * (5 + inst_count),
        out_specs=ANY,
        scratch_shapes=[
            pltpu.VMEM((tiles, FIELDS, MODES, LANES), f32),
            sems((tiles,)),
        ],
        compiler_params=params,
        name="final",
    )(partial, weights, turned, places, first, second, *others)


def solution(mesh):
    return jax.shard_map(
        shards,
        mesh=mesh,
        in_specs=(
            P("inst", None, None, "space"),
            P("space"),
            P(),
            P(),
            P(),
            P("inst"),
            P("space"),
            P(None, "space"),
            P("inst", "space"),
        ),
        out_specs=P("inst", None, None, "space"),
        check_vma=False,
    )
```

```python
import functools
import math

import jax
import jax.numpy as jnp
import numpy as np
from jax import lax
from jax.experimental import pallas as pl
from jax.experimental.pallas import tpu as pltpu
from jax.sharding import PartitionSpec as P

RIM = 64
FIELDS = 5
MODES = 64
FACE = 16
TRACE = FIELDS * FACE
LANES = 128
COURANT = 0.5

VMEM = pl.BlockSpec(memory_space=pltpu.VMEM)
SMEM = pl.BlockSpec(memory_space=pltpu.SMEM)
ANY = pl.BlockSpec(memory_space=pl.ANY)
HBM = pl.BlockSpec(memory_space=pltpu.HBM)


def gll_table():
    nodes = np.array([-1.0, -1.0 / math.sqrt(5.0), 1.0 / math.sqrt(5.0), 1.0])
    barycentric = np.array(
        [1.0 / np.prod([nodes[j] - nodes[k] for k in range(4) if k != j]) for j in range(4)]
    )
    derivative = np.zeros((4, 4))
    for i in range(4):
        for j in range(4):
            if i != j:
                derivative[i, j] = barycentric[j] / barycentric[i] / (nodes[i] - nodes[j])
        derivative[i, i] = -np.sum(derivative[i])
    return derivative


def face_nodes(face):
    direction, index = face // 2, 3 * (face % 2)
    nodes = []
    for first in range(4):
        for second in range(4):
            if direction == 0:
                nodes.append(16 * index + 4 * first + second)
            elif direction == 1:
                nodes.append(16 * first + 4 * index + second)
            else:
                nodes.append(16 * first + 4 * second + index)
    return nodes


def operator_tables():
    derivative, identity = gll_table(), np.eye(4)
    along = [
        np.kron(np.kron(derivative, identity), identity),
        np.kron(np.kron(identity, derivative), identity),
        np.kron(np.kron(identity, identity), derivative),
    ]
    tables = [-table for table in along] + [np.zeros((MODES, MODES))]
    for face in range(6):
        sign = 1.0 if face % 2 else -1.0
        for node in face_nodes(face):
            tables[face // 2][node, node] += 3.0 * sign
            tables[3][node, node] -= 3.0
    return np.stack([np.concatenate([t, t], axis=1) for t in tables]).astype(np.float32)


def spectral_values(count):
    values = {0: (count * count + 2.0) / (12.0 * count)}
    for k in range(1 - count, count):
        if k:
            parity = -1.0 if k % 2 else 1.0
            angle = math.pi * k / count
            values[k] = 0.5 * parity / math.tan(angle) + parity / (
                2.0 * count * math.sin(angle) ** 2
            )
    return values


def split(value):
    high = value.astype(jnp.bfloat16)
    low = (value - high.astype(jnp.float32)).astype(jnp.bfloat16)
    return high, low


def fetch_all(pairs, sems):
    copies = [
        pltpu.make_async_copy(source, target, sems.at[k]) for k, (source, target) in enumerate(pairs)
    ]
    for copy in copies:
        copy.start()
    return copies


def tile_of(number):
    return slice(number * LANES, (number + 1) * LANES)


def face_pieces(face):
    direction, index = face // 2, 3 * (face % 2)
    if direction == 0:
        return [(slice(0, 16), slice(16 * index, 16 * index + 16))]
    if direction == 1:
        return [
            (slice(4 * a, 4 * a + 4), slice(16 * a + 4 * index, 16 * a + 4 * index + 4))
            for a in range(4)
        ]
    return [(slice(0, 16), pl.ds(index, 16, stride=4))]


def load_trace(cells, tile, face, trace):
    for field in range(FIELDS):
        for rows, nodes in face_pieces(face):
            target = slice(field * FACE + rows.start, field * FACE + rows.stop)
            trace[tile, target, :] = cells[tile, field, nodes, :]


def choose(sources, positions):
    shape = sources[0].shape
    lane = jnp.broadcast_to(positions & (LANES - 1), shape)
    tile = jnp.broadcast_to(positions >> 7, shape)
    result = None
    for number, source in enumerate(sources):
        found = jnp.take_along_axis(source, lane, axis=1, mode="promise_in_bounds")
        result = found if result is None else jnp.where(tile == number, found, result)
    return result


def base_owner(pairs, plane):
    owners = (pairs // plane).astype(jnp.float32)
    lowest = jnp.min(owners, axis=1, keepdims=True).astype(jnp.int32)
    highest = jnp.max(owners, axis=1, keepdims=True).astype(jnp.int32)
    return jnp.where(highest - lowest <= 1, lowest, highest)


def prep_kernel(
    plane, state, pairs, metric, jacobians, rotor, far, near, shift, rows, mixing,
    pairs_here, metric_here, rim, tiles, sems,
):
    n = lax.axis_size("space")
    me = lax.axis_index("space")
    count = plane // LANES
    copies = fetch_all(
        [(pairs, pairs_here)]
        + [
            (state.at[0, :, :, pl.ds(2 * RIM + tile * LANES, LANES)], tiles.at[tile])
            for tile in range(count)
        ]
        + [(state.at[0, :, :, pl.ds(0, 2 * RIM)], rim)]
        + [(metric, metric_here), (jacobians, mixing)],
        sems,
    )
    copies[0].wait()
    shift[0] = lax.rem(jnp.max(base_owner(pairs_here[...], plane)) - me + n, n)
    rows[1:2, :plane] = pairs_here[...].astype(jnp.float32)
    for tile in range(count):
        copies[1 + tile].wait()
        for field in range(FIELDS):
            rotor[field * FACE : (field + 1) * FACE, tile_of(tile)] = tiles[
                tile, field, pl.ds(0, FACE, stride=4), :
            ]
    for copy in copies[count + 1 :]:
        copy.wait()
    rows[0:1, :] = metric_here[...]
    odd = lax.rem(me, 2) == 1
    lane = lax.broadcasted_iota(jnp.int32, (MODES // 2, 2 * RIM), 1)
    pieces = [
        rim[field, 32 * half : 32 * half + 32, :] for field in range(FIELDS) for half in range(2)
    ]
    for k in range(FIELDS):
        top, bottom = pieces[k], pieces[k + FIELDS]
        head = jnp.where(lane < RIM, top, pltpu.roll(bottom, RIM, 1))
        tail = jnp.where(lane < RIM, pltpu.roll(top, RIM, 1), bottom)
        far[32 * k : 32 * k + 32, :] = jnp.where(odd, tail, head)
        near[32 * k : 32 * k + 32, :] = jnp.where(odd, head, tail)


def own_kernel(
    plane, state, neighbours, rows, mixing, dissipation, omega, angle, counts, tables,
    tendency, outer, flux, frame, weights, places,
    loss, frequency, turn, live_count, table, matrix, cells, trace, sems,
):
    n = lax.axis_size("space")
    inst_count = lax.axis_size("inst")
    inst = lax.axis_index("inst")
    copies = fetch_all(
        [
            (dissipation, loss),
            (omega, frequency),
            (angle, turn),
            (counts, live_count),
            (tables, table),
        ],
        sems,
    )
    for g in range(FIELDS):
        for d in range(3):
            for field in range(FIELDS):
                row = flux_row(g, d, field)
                flux[row : row + 1, :] = jnp.broadcast_to(
                    mixing[g, d : d + 1, field : field + 1], (1, LANES)
                )
    count = cells.shape[0]
    elems = state.shape[-1]

    for tile in range(count):
        cells[tile] = state[0, :, :, tile_of(tile)]
    row_number = lax.broadcasted_iota(jnp.int32, (elems, elems), 0)
    for face in range(6):
        for tile in range(count):
            load_trace(cells, tile, face ^ 1, trace.at[face])
        sources = [trace[face, source] for source in range(count)]
        positions = neighbours[face : face + 1, :] - RIM
        if face % 2:
            parts = jnp.concatenate(split(jnp.concatenate(sources, axis=1)), axis=0)
            matches = jnp.where(row_number == positions, 1.0, 0.0).astype(jnp.bfloat16)
            found = jnp.dot(parts, matches, preferred_element_type=jnp.float32)
            for tile in range(count):
                outer[face, tile] = found[:TRACE, tile_of(tile)] + found[TRACE:, tile_of(tile)]
        else:
            for tile in range(count):
                outer[face, tile] = choose(sources, positions[:, tile_of(tile)])

    for copy in copies:
        copy.wait()
    lane = lax.broadcasted_iota(jnp.int32, (1, LANES), 1)
    layout = [((0, 1), 0, 5), ((2, 3), 1, 6), ((4, 0), 2, 7), ((1, 2), 3, None), ((3, 4), 4, None)]
    for g in range(FIELDS):
        band = slice(g * MODES, (g + 1) * MODES)
        values = [
            [flux[pl.ds(flux_row(g, d, field), 1), :] for field in range(FIELDS)] for d in range(3)
        ]
        for (left, right), high_place, low_place in layout:
            block = None
            for d in range(3):
                term = jnp.where(lane < MODES, values[d][left], values[d][right]) * table[d]
                block = term if block is None else block + term
            if g in (left, right):
                own = lane < MODES if g == left else lane >= MODES
                block = block + jnp.where(own, loss[...], 0.0) * table[3]
            high, low = split(block)
            matrix[band, tile_of(high_place)] = high
            if low_place is not None:
                if left == FIELDS - 1:
                    low = jnp.where(lane < MODES, low, jnp.zeros_like(low))
                matrix[band, tile_of(low_place)] = low
    high, low = split(state[0].reshape(FIELDS * MODES, elems))
    stacked = jnp.concatenate([high, low, high, jnp.zeros_like(high[:MODES])], axis=0)
    product = jnp.dot(matrix[...], stacked, preferred_element_type=jnp.float32)
    for tile in range(count):
        tendency[tile] = product[:, tile_of(tile)].reshape(FIELDS, MODES, LANES)


    turns = jnp.broadcast_to(turn[...], (1, LANES))
    frame[0:1, :] = jnp.broadcast_to(3.0 * loss[...], (1, LANES))
    frame[1:2, :] = jnp.cos(turns)
    frame[2:3, :] = jnp.sin(turns)

    spectral = spectral_values(inst_count)
    scale = rows[0:1, :]
    step = COURANT / (scale * loss[...] + frequency[...])
    live = lax.broadcasted_iota(jnp.int32, (1, elems), 1) < live_count[...]
    step = jnp.where(live, step, 0.0)
    weights[0:1, :] = step * scale
    weights[1:2, :] = jnp.where(live, 1.0, 0.0) - step * (frequency[...] * spectral[0])
    for away in range(1, inst_count):
        value = jnp.where(inst + away < inst_count, spectral[-away], spectral[inst_count - away])
        weights[away + 1 : away + 2, :] = -step * (frequency[...] * value)

    pairs = rows[1:2, :plane].astype(jnp.int32)
    place = pairs - base_owner(pairs, plane) * plane
    places[...] = jnp.where(place < 0, place + n * plane, place)


def flux_row(g, direction, field):
    return (direction * FIELDS + g) * FIELDS + field


def halo_kernel(
    plane, state, neighbours, flux, frame, weights, tendency, outer, from_far, from_near,
    partial, rim, trace,
):
    count = partial.shape[0]
    elems = state.shape[-1]
    odd = lax.rem(lax.axis_index("space"), 2) == 1
    half_lane = lax.broadcasted_iota(jnp.int32, (MODES // 2, 2 * RIM), 1)
    for k in range(2 * FIELDS):
        field, half = k // 2, k % 2
        piece = pl.ds(32 * (k % FIELDS), 32)
        left = jnp.where(odd, from_near[piece, :], from_far[piece, :])
        right = jnp.where(odd, from_far[piece, :], from_near[piece, :])
        if k < FIELDS:
            right = pltpu.roll(right, RIM, 1)
        else:
            left = pltpu.roll(left, RIM, 1)
        rim[0, field, 32 * half : 32 * half + 32, :] = jnp.where(half_lane < RIM, left, right)
    for face in range(6):
        load_trace(rim, 0, face ^ 1, trace.at[pl.ds(face, 1)])
    partial[...] = tendency[...]
    lane = lax.broadcasted_iota(jnp.int32, (1, LANES), 1)
    for face in range(6):
        for tile in range(count):
            number = neighbours[face : face + 1, tile_of(tile)]
            previous = number < RIM
            remote = previous | (number >= RIM + elems)
            found = choose([trace[face]], jnp.where(previous, number, number - elems))
            found = jnp.where(remote, found, outer[face, tile])
            if face == 5:
                column = lane + tile * LANES
                sliding = (column >= 2 * RIM) & (column < 2 * RIM + plane)
                found = jnp.where(sliding, 0.0, found)
            parts = [found[field * FACE : (field + 1) * FACE] for field in range(FIELDS)]
            lift(partial, tile, face, mix(flux, frame, face, parts), 1.0)
    for tile in range(count):
        scale, keep = weights[0:1, tile_of(tile)], weights[1:2, tile_of(tile)]
        partial[tile] = keep * state[0, :, :, tile_of(tile)] + scale * partial[tile]


def mix(flux, frame, face, parts):
    mixed = []
    for g in range(FIELDS):
        total = None
        for field in range(FIELDS):
            row = flux_row(g, face // 2, field)
            term = flux[row : row + 1, :] * parts[field]
            total = term if total is None else total + term
        mixed.append((3.0 if face % 2 else -3.0) * total - frame[0:1, :] * parts[g])
    return mixed


def lift(cells, tile, face, mixed, scale):
    for g in range(FIELDS):
        change = scale * mixed[g]
        for rows, nodes in face_pieces(face):
            cells[tile, g, nodes, :] = cells[tile, g, nodes, :] - change[rows]


def final_kernel(plane, partial, weights, flux, frame, places, first, second, *refs):
    inst_count = lax.axis_size("inst")
    others, (result, buffer, sems) = refs[: inst_count - 1], refs[inst_count - 1 :]
    count = buffer.shape[0]
    start, stop = 2 * RIM // LANES, (2 * RIM + plane) // LANES
    copies = []
    for tile in [*range(start, stop), *range(start), *range(stop, count)]:
        for field in range(FIELDS):
            total = partial[tile, field]
            for away in range(1, inst_count):
                row = weights[away + 1 : away + 2, tile_of(tile)]
                total = total + row * others[away - 1][0, field, :, tile_of(tile)]
            buffer[tile, field] = total
        if start <= tile < stop:
            positions = places[:, tile_of(tile - start)]
            found = choose(
                [
                    block[:, tile_of(source)]
                    for block in (first, second)
                    for source in range(plane // LANES)
                ],
                positions,
            )
            parts = [found[field * FACE : (field + 1) * FACE] for field in range(FIELDS)]
            cosine, sine = frame[1:2, :], frame[2:3, :]
            parts[2], parts[3] = (
                cosine * parts[2] - sine * parts[3],
                sine * parts[2] + cosine * parts[3],
            )
            lift(buffer, tile, 5, mix(flux, frame, 5, parts), weights[0:1, tile_of(tile)])
        copies.append(
            pltpu.make_async_copy(
                buffer.at[tile], result.at[0, :, :, pl.ds(tile * LANES, LANES)], sems.at[tile]
            )
        )
        copies[-1].start()
    for copy in copies:
        copy.wait()


def shards(
    state, metric, jacobians, dissipation, omega, rotor_angle, counts, neighbours, mortar_pairs
):
    elems = state.shape[-1]
    tiles = elems // LANES
    plane = mortar_pairs.shape[-1]
    n = lax.axis_size("space")
    inst_count = lax.axis_size("inst")
    f32 = jnp.float32
    shape = jax.ShapeDtypeStruct
    sems = pltpu.SemaphoreType.DMA
    scalar = pltpu.VMEM((1, 1), f32)
    params = pltpu.CompilerParams(vmem_limit_bytes=32 * 2**20)
    cost = pl.CostEstimate(flops=2**31, bytes_accessed=2**22, transcendentals=0)

    others = [
        lax.ppermute(state, "inst", [((i + away) % inst_count, i) for i in range(inst_count)])
        for away in range(1, inst_count)
    ]

    rotor, far, near, shift, rows, mixing = pl.pallas_call(
        functools.partial(prep_kernel, plane),
        out_shape=(
            shape((TRACE, plane), f32),
            shape((FIELDS * MODES // 2, 2 * RIM), f32),
            shape((FIELDS * MODES // 2, 2 * RIM), f32),
            shape((1,), jnp.int32),
            shape((8, elems), f32),
            shape((FIELDS, 3, FIELDS), f32),
        ),
        in_specs=[HBM] * 4,
        out_specs=(VMEM, VMEM, VMEM, SMEM, VMEM, VMEM),
        scratch_shapes=[
            pltpu.VMEM((1, plane), jnp.int32),
            pltpu.VMEM((1, elems), f32),
            pltpu.VMEM((FIELDS, MODES, 2 * RIM), f32),
            pltpu.VMEM((plane // LANES, FIELDS, MODES, LANES), f32),
            sems((plane // LANES + 4,)),
        ],
        name="prep",
    )(state, mortar_pairs, metric.reshape(1, elems), jnp.transpose(jacobians, (1, 0, 2)))

    def fetch(away, block):
        if away == 0:
            return block
        return lax.ppermute(block, "space", [((i + away) % n, i) for i in range(n)])

    ends = [(i, (i + 1) % n) for i in range(1, n, 2)]
    middles = [(i, i + 1) for i in range(0, n, 2)]

    def swap(pairs, block):
        return lax.ppermute(block, "space", pairs + [(j, i) for i, j in pairs])

    def branch(away, rotor, far, near, state, neighbours, *operands):
        first = fetch(away, rotor)
        from_far, from_near = swap(ends, far), swap(middles, near)
        tendency, outer, flux, frame, weights, places = pl.pallas_call(
            functools.partial(own_kernel, plane),
            out_shape=(
                shape((tiles, FIELDS, MODES, LANES), f32),
                shape((6, tiles, TRACE, LANES), f32),
                shape((3 * FIELDS * FIELDS, LANES), f32),
                shape((8, LANES), f32),
                shape((inst_count + 1, elems), f32),
                shape((1, plane), jnp.int32),
            ),
            in_specs=[VMEM] * 4 + [HBM] * 5,
            out_specs=(VMEM,) * 6,
            scratch_shapes=[
                scalar,
                scalar,
                scalar,
                pltpu.VMEM((1, 1), jnp.int32),
                pltpu.VMEM((4, MODES, LANES), f32),
                pltpu.VMEM((FIELDS * MODES, 8 * LANES), jnp.bfloat16),
                pltpu.VMEM((tiles, FIELDS, MODES, LANES), f32),
                pltpu.VMEM((6, tiles, TRACE, LANES), f32),
                sems((5,)),
            ],
            compiler_params=params,
            cost_estimate=cost,
            name="own",
        )(state, neighbours, *operands)
        second = fetch(1, first)
        partial = pl.pallas_call(
            functools.partial(halo_kernel, plane),
            out_shape=shape((tiles, FIELDS, MODES, LANES), f32),
            in_specs=[VMEM] * 9,
            out_specs=VMEM,
            scratch_shapes=[
                pltpu.VMEM((1, FIELDS, MODES, 2 * RIM), f32),
                pltpu.VMEM((6, TRACE, LANES), f32),
            ],
            compiler_params=params,
            cost_estimate=cost,
            name="halo",
        )(state, neighbours, flux, frame, weights, tendency, outer, from_far, from_near)
        return partial, weights, flux, frame, places, first, second

    operands = lax.switch(
        shift[0],
        [functools.partial(branch, away) for away in range(n)],
        rotor, far, near, state, neighbours, rows, mixing, dissipation.reshape(1, 1),
        omega.reshape(1, 1), rotor_angle.reshape(1, 1), counts.reshape(1, 1),
        jnp.asarray(operator_tables()),
    )

    return pl.pallas_call(
        functools.partial(final_kernel, plane),
        out_shape=shape(state.shape, f32),
        in_specs=[VMEM] * (6 + inst_count),
        out_specs=ANY,
        scratch_shapes=[
            pltpu.VMEM((tiles, FIELDS, MODES, LANES), f32),
            sems((tiles,)),
        ],
        compiler_params=params,
        name="final",
    )(*operands, *others)


def solution(mesh):
    return jax.shard_map(
        shards,
        mesh=mesh,
        in_specs=(
            P("inst", None, None, "space"),
            P("space"),
            P(),
            P(),
            P(),
            P("inst"),
            P("space"),
            P(None, "space"),
            P("inst", "space"),
        ),
        out_specs=P("inst", None, None, "space"),
        check_vma=False,
    )
```

```python
import functools
import math

import jax
import jax.numpy as jnp
import numpy as np
from jax import lax
from jax.experimental import pallas as pl
from jax.experimental.pallas import tpu as pltpu
from jax.sharding import PartitionSpec as P

RIM = 64
FIELDS = 5
MODES = 64
FACE = 16
TRACE = FIELDS * FACE
LANES = 128
COURANT = 0.5

VMEM = pl.BlockSpec(memory_space=pltpu.VMEM)
SMEM = pl.BlockSpec(memory_space=pltpu.SMEM)
ANY = pl.BlockSpec(memory_space=pl.ANY)
HBM = pl.BlockSpec(memory_space=pltpu.HBM)


def gll_table():
    nodes = np.array([-1.0, -1.0 / math.sqrt(5.0), 1.0 / math.sqrt(5.0), 1.0])
    barycentric = np.array(
        [1.0 / np.prod([nodes[j] - nodes[k] for k in range(4) if k != j]) for j in range(4)]
    )
    derivative = np.zeros((4, 4))
    for i in range(4):
        for j in range(4):
            if i != j:
                derivative[i, j] = barycentric[j] / barycentric[i] / (nodes[i] - nodes[j])
        derivative[i, i] = -np.sum(derivative[i])
    return derivative


def face_nodes(face):
    direction, index = face // 2, 3 * (face % 2)
    nodes = []
    for first in range(4):
        for second in range(4):
            if direction == 0:
                nodes.append(16 * index + 4 * first + second)
            elif direction == 1:
                nodes.append(16 * first + 4 * index + second)
            else:
                nodes.append(16 * first + 4 * second + index)
    return nodes


def spectral_values(count):
    values = {0: (count * count + 2.0) / (12.0 * count)}
    for k in range(1 - count, count):
        if k:
            parity = -1.0 if k % 2 else 1.0
            angle = math.pi * k / count
            values[k] = 0.5 * parity / math.tan(angle) + parity / (
                2.0 * count * math.sin(angle) ** 2
            )
    return values


def split(value):
    high = value.astype(jnp.bfloat16)
    low = (value - high.astype(jnp.float32)).astype(jnp.bfloat16)
    return high, low


def fetch_all(pairs, sems):
    copies = [
        pltpu.make_async_copy(source, target, sems.at[k]) for k, (source, target) in enumerate(pairs)
    ]
    for copy in copies:
        copy.start()
    return copies


def tile_of(number):
    return slice(number * LANES, (number + 1) * LANES)


def face_pieces(face):
    direction, index = face // 2, 3 * (face % 2)
    if direction == 0:
        return [(slice(0, 16), slice(16 * index, 16 * index + 16))]
    if direction == 1:
        return [
            (slice(4 * a, 4 * a + 4), slice(16 * a + 4 * index, 16 * a + 4 * index + 4))
            for a in range(4)
        ]
    return [(slice(0, 16), pl.ds(index, 16, stride=4))]


def load_trace(cells, tile, face, trace):
    for field in range(FIELDS):
        for rows, nodes in face_pieces(face):
            target = slice(field * FACE + rows.start, field * FACE + rows.stop)
            trace[tile, target, :] = cells[tile, field, nodes, :]


def choose(sources, positions):
    shape = sources[0].shape
    lane = jnp.broadcast_to(positions & (LANES - 1), shape)
    tile = jnp.broadcast_to(positions >> 7, shape)
    result = None
    for number, source in enumerate(sources):
        found = jnp.take_along_axis(source, lane, axis=1, mode="promise_in_bounds")
        result = found if result is None else jnp.where(tile == number, found, result)
    return result


def base_owner(pairs, plane):
    owners = (pairs // plane).astype(jnp.float32)
    lowest = jnp.min(owners, axis=1, keepdims=True).astype(jnp.int32)
    highest = jnp.max(owners, axis=1, keepdims=True).astype(jnp.int32)
    return jnp.where(highest - lowest <= 1, lowest, highest)


def prep_kernel(
    plane, state, pairs, metric, jacobians, rotor, far, near, shift, rows, mixing,
    pairs_here, metric_here, rim, tiles, sems,
):
    n = lax.axis_size("space")
    me = lax.axis_index("space")
    count = plane // LANES
    copies = fetch_all(
        [(pairs, pairs_here)]
        + [
            (state.at[0, :, :, pl.ds(2 * RIM + tile * LANES, LANES)], tiles.at[tile])
            for tile in range(count)
        ]
        + [(state.at[0, :, :, pl.ds(0, 2 * RIM)], rim)]
        + [(metric, metric_here), (jacobians, mixing)],
        sems,
    )
    copies[0].wait()
    shift[0] = lax.rem(jnp.max(base_owner(pairs_here[...], plane)) - me + n, n)
    rows[1:2, :plane] = pairs_here[...].astype(jnp.float32)
    for tile in range(count):
        copies[1 + tile].wait()
        for field in range(FIELDS):
            rotor[field * FACE : (field + 1) * FACE, tile_of(tile)] = tiles[
                tile, field, pl.ds(0, FACE, stride=4), :
            ]
    for copy in copies[count + 1 :]:
        copy.wait()
    rows[0:1, :] = metric_here[...]
    odd = lax.rem(me, 2) == 1
    lane = lax.broadcasted_iota(jnp.int32, (MODES // 2, 2 * RIM), 1)
    pieces = [
        rim[field, 32 * half : 32 * half + 32, :] for field in range(FIELDS) for half in range(2)
    ]
    for k in range(FIELDS):
        top, bottom = pieces[k], pieces[k + FIELDS]
        head = jnp.where(lane < RIM, top, pltpu.roll(bottom, RIM, 1))
        tail = jnp.where(lane < RIM, pltpu.roll(top, RIM, 1), bottom)
        far[32 * k : 32 * k + 32, :] = jnp.where(odd, tail, head)
        near[32 * k : 32 * k + 32, :] = jnp.where(odd, head, tail)


def derivative_parts(lane):
    table = -gll_table()
    table[0, 0] -= 3.0
    table[3, 3] += 3.0
    table = table.astype(np.float32).tolist()
    row = lax.broadcasted_iota(jnp.int32, (16, LANES), 0)
    column = jnp.broadcast_to(lane & 15, (16, LANES))
    band = (lane & 63) >> 4

    def entry(i, j):
        value = jnp.zeros(j.shape, jnp.float32)
        for first in range(4):
            for second in range(4):
                value = jnp.where((i == first) & (j == second), table[first][second], value)
        return value

    middle = jnp.where((row & 3) == (column & 3), entry(row >> 2, column >> 2), 0.0)
    last = jnp.where((row >> 2) == (column >> 2), entry(row & 3, column & 3), 0.0)
    parts = [[], [], []]
    for a in range(4):
        along = jnp.zeros(lane.shape, jnp.float32)
        for second in range(4):
            along = jnp.where(band == second, table[a][second], along)
        parts[0].append(jnp.where(row == column, along, 0.0))
        parts[1].append(jnp.where(band == a, middle, 0.0))
        parts[2].append(jnp.where(band == a, last, 0.0))
    return parts


def own_kernel(
    state, neighbours, rows, mixing, dissipation, omega, angle, counts,
    tendency, outer, forward, loss, frequency, turn, live_count, matrix, cells, trace, sems,
):
    copies = fetch_all(
        [(dissipation, loss), (omega, frequency), (angle, turn), (counts, live_count)], sems
    )
    count = cells.shape[0]
    elems = state.shape[-1]

    for tile in range(count):
        cells[tile] = state[0, :, :, tile_of(tile)]
    for face in range(6):
        for tile in range(count):
            load_trace(cells, tile, face ^ 1, trace.at[face])

    def gather(face, carry):
        positions = neighbours[pl.ds(face, 1), :] - RIM
        for tile in range(count):
            sources = [trace[face, source] for source in range(count)]
            outer[face, tile] = choose(sources, positions[:, tile_of(tile)])
        return carry

    lax.fori_loop(0, 6, gather, 0)

    lane = lax.broadcasted_iota(jnp.int32, (1, LANES), 1)
    parts = derivative_parts(lane)
    layout = [((0, 1), 0, 5), ((2, 3), 1, 6), ((4, 0), 2, 7), ((1, 2), 3, None), ((3, 4), 4, None)]
    for g in range(FIELDS):
        values = [
            [jnp.broadcast_to(mixing[g, d : d + 1, f : f + 1], (1, LANES)) for f in range(FIELDS)]
            for d in range(3)
        ]
        for (left, right), high_place, low_place in layout:
            weight = [jnp.where(lane < MODES, values[d][left], values[d][right]) for d in range(3)]
            for a in range(4):
                block = weight[0] * parts[0][a] + weight[1] * parts[1][a] + weight[2] * parts[2][a]
                high, low = split(block)
                band = slice(g * MODES + 16 * a, g * MODES + 16 * a + 16)
                matrix[band, tile_of(high_place)] = high
                if low_place is not None:
                    if left == FIELDS - 1:
                        low = jnp.where(lane < MODES, low, jnp.zeros_like(low))
                    matrix[band, tile_of(low_place)] = low
    high, low = split(state[0].reshape(FIELDS * MODES, elems))
    stacked = jnp.concatenate([high, low, high, jnp.zeros_like(high[:MODES])], axis=0)
    product = jnp.dot(matrix[...], stacked, preferred_element_type=jnp.float32)
    for tile in range(count):
        tendency[tile] = product[:, tile_of(tile)].reshape(FIELDS, MODES, LANES)

    forward[0:2, :] = rows[0:2, :]
    for copy in copies:
        copy.wait()
    for row, value in enumerate(
        [loss[...], frequency[...], turn[...], live_count[...].astype(jnp.float32)]
    ):
        forward[2 + row : 3 + row, :] = jnp.broadcast_to(value, (1, elems))


def rim_kernel(from_far, from_near, rim):
    odd = lax.rem(lax.axis_index("space"), 2) == 1
    lane = lax.broadcasted_iota(jnp.int32, (MODES // 2, 2 * RIM), 1)
    for k in range(2 * FIELDS):
        field, half = k // 2, k % 2
        piece = pl.ds(32 * (k % FIELDS), 32)
        left = jnp.where(odd, from_near[piece, :], from_far[piece, :])
        right = jnp.where(odd, from_far[piece, :], from_near[piece, :])
        if k < FIELDS:
            right = pltpu.roll(right, RIM, 1)
        else:
            left = pltpu.roll(left, RIM, 1)
        rim[0, field, 32 * half : 32 * half + 32, :] = jnp.where(lane < RIM, left, right)


def flux_row(g, direction, field):
    return (direction * FIELDS + g) * FIELDS + field


FRAME = 3 * FIELDS * FIELDS
WEIGHTS = FRAME + 5


def halo_kernel(
    plane, state, neighbours, forward, mixing, tendency, outer, rim, partial, small, trace
):
    n = lax.axis_size("space")
    inst_count = lax.axis_size("inst")
    inst = lax.axis_index("inst")
    count = partial.shape[0]
    elems = state.shape[-1]
    for g in range(FIELDS):
        for d in range(3):
            for field in range(FIELDS):
                row = flux_row(g, d, field)
                small[row : row + 1, :] = jnp.broadcast_to(
                    mixing[g, d : d + 1, field : field + 1], (1, LANES)
                )
    loss, frequency, turn, live_count = [
        forward[2 + row : 3 + row, :LANES] for row in range(4)
    ]
    small[FRAME : FRAME + 1, :] = 3.0 * loss
    small[FRAME + 1 : FRAME + 2, :] = jnp.cos(turn)
    small[FRAME + 2 : FRAME + 3, :] = jnp.sin(turn)

    for face in range(6):
        load_trace(rim, 0, face ^ 1, trace.at[pl.ds(face, 1)])
    partial[...] = tendency[...]
    lane = lax.broadcasted_iota(jnp.int32, (1, LANES), 1)
    for face in range(6):
        for tile in range(count):
            number = neighbours[face : face + 1, tile_of(tile)]
            previous = number < RIM
            remote = previous | (number >= RIM + elems)
            found = choose([trace[face]], jnp.where(previous, number, number - elems))
            found = jnp.where(remote, found, outer[face, tile])
            if face == 5:
                column = lane + tile * LANES
                sliding = (column >= 2 * RIM) & (column < 2 * RIM + plane)
                found = jnp.where(sliding, 0.0, found)
            parts = [found[field * FACE : (field + 1) * FACE] for field in range(FIELDS)]
            lift(partial, tile, face, mix(small, face, parts), 1.0)

    node = lax.broadcasted_iota(jnp.int32, (MODES, LANES), 0)
    faces = jnp.zeros((MODES, LANES), jnp.float32)
    for index in (node >> 4, (node >> 2) & 3, node & 3):
        faces = faces + jnp.where((index == 0) | (index == 3), 1.0, 0.0)
    spectral = spectral_values(inst_count)
    for tile in range(count):
        scale = forward[0:1, tile_of(tile)]
        step = COURANT / (scale * loss + frequency)
        live = (lane + tile * LANES).astype(jnp.float32) < live_count
        step = jnp.where(live, step, 0.0)
        keep = jnp.where(live, 1.0, 0.0) - step * (frequency * spectral[0])
        keep = keep - (3.0 * loss * step * scale) * faces
        partial[tile] = keep * state[0, :, :, tile_of(tile)] + (step * scale) * partial[tile]
        small[WEIGHTS + tile : WEIGHTS + tile + 1, :] = step * scale
        for away in range(1, inst_count):
            value = jnp.where(
                inst + away < inst_count, spectral[-away], spectral[inst_count - away]
            )
            row = WEIGHTS + away * count + tile
            small[row : row + 1, :] = -step * (frequency * value)

    pairs = forward[1:2, :plane].astype(jnp.int32)
    place = pairs - base_owner(pairs, plane) * plane
    place = jnp.where(place < 0, place + n * plane, place).astype(jnp.float32)
    for tile in range(plane // LANES):
        row = WEIGHTS + inst_count * count + tile
        small[row : row + 1, :] = place[:, tile_of(tile)]


def mix(small, face, parts):
    mixed = []
    for g in range(FIELDS):
        total = None
        for field in range(FIELDS):
            row = flux_row(g, face // 2, field)
            term = small[row : row + 1, :] * parts[field]
            total = term if total is None else total + term
        mixed.append((3.0 if face % 2 else -3.0) * total - small[FRAME : FRAME + 1, :] * parts[g])
    return mixed


def lift(cells, tile, face, mixed, scale):
    for g in range(FIELDS):
        change = scale * mixed[g]
        for rows, nodes in face_pieces(face):
            cells[tile, g, nodes, :] = cells[tile, g, nodes, :] - change[rows]


def final_kernel(plane, partial, small, first, second, *refs):
    inst_count = lax.axis_size("inst")
    others, (result, buffer, sems) = refs[: inst_count - 1], refs[inst_count - 1 :]
    count = buffer.shape[0]
    start, stop = 2 * RIM // LANES, (2 * RIM + plane) // LANES
    copies = []
    for tile in [*range(start), *range(stop, count), *range(start, stop)]:
        for field in range(FIELDS):
            total = partial[tile, field]
            for away in range(1, inst_count):
                row = WEIGHTS + away * count + tile
                other = others[away - 1][0, field, :, tile_of(tile)]
                total = total + small[row : row + 1, :] * other
            buffer[tile, field] = total
        if start <= tile < stop:
            row = WEIGHTS + inst_count * count + tile - start
            found = choose(
                [
                    block[:, tile_of(source)]
                    for block in (first, second)
                    for source in range(plane // LANES)
                ],
                small[row : row + 1, :].astype(jnp.int32),
            )
            parts = [found[field * FACE : (field + 1) * FACE] for field in range(FIELDS)]
            cosine, sine = small[FRAME + 1 : FRAME + 2, :], small[FRAME + 2 : FRAME + 3, :]
            parts[2], parts[3] = (
                cosine * parts[2] - sine * parts[3],
                sine * parts[2] + cosine * parts[3],
            )
            scale = small[WEIGHTS + tile : WEIGHTS + tile + 1, :]
            lift(buffer, tile, 5, mix(small, 5, parts), scale)
        copies.append(
            pltpu.make_async_copy(
                buffer.at[tile], result.at[0, :, :, pl.ds(tile * LANES, LANES)], sems.at[tile]
            )
        )
        copies[-1].start()
    for copy in copies:
        copy.wait()


def shards(
    state, metric, jacobians, dissipation, omega, rotor_angle, counts, neighbours, mortar_pairs
):
    elems = state.shape[-1]
    tiles = elems // LANES
    plane = mortar_pairs.shape[-1]
    n = lax.axis_size("space")
    inst_count = lax.axis_size("inst")
    f32 = jnp.float32
    shape = jax.ShapeDtypeStruct
    sems = pltpu.SemaphoreType.DMA
    scalar = pltpu.VMEM((1, 1), f32)
    params = pltpu.CompilerParams(vmem_limit_bytes=32 * 2**20)
    cost = pl.CostEstimate(flops=2**31, bytes_accessed=2**22, transcendentals=0)

    others = [
        lax.ppermute(state, "inst", [((i + away) % inst_count, i) for i in range(inst_count)])
        for away in range(1, inst_count)
    ]

    rotor, far, near, shift, rows, mixing = pl.pallas_call(
        functools.partial(prep_kernel, plane),
        out_shape=(
            shape((TRACE, plane), f32),
            shape((FIELDS * MODES // 2, 2 * RIM), f32),
            shape((FIELDS * MODES // 2, 2 * RIM), f32),
            shape((1,), jnp.int32),
            shape((8, elems), f32),
            shape((FIELDS, 3, FIELDS), f32),
        ),
        in_specs=[HBM] * 4,
        out_specs=(VMEM, VMEM, VMEM, SMEM, VMEM, VMEM),
        scratch_shapes=[
            pltpu.VMEM((1, plane), jnp.int32),
            pltpu.VMEM((1, elems), f32),
            pltpu.VMEM((FIELDS, MODES, 2 * RIM), f32),
            pltpu.VMEM((plane // LANES, FIELDS, MODES, LANES), f32),
            sems((plane // LANES + 4,)),
        ],
        name="prep",
    )(state, mortar_pairs, metric.reshape(1, elems), jnp.transpose(jacobians, (1, 0, 2)))

    def fetch(away, block):
        if away == 0:
            return block
        return lax.ppermute(block, "space", [((i + away) % n, i) for i in range(n)])

    ends = [(i, (i + 1) % n) for i in range(1, n, 2)]
    middles = [(i, i + 1) for i in range(0, n, 2)]

    def swap(pairs, block):
        return lax.ppermute(block, "space", pairs + [(j, i) for i, j in pairs])

    def branch(away, rotor, far, near, *operands):
        first = fetch(away, rotor)
        from_far, from_near = swap(ends, far), swap(middles, near)
        own = pl.pallas_call(
            own_kernel,
            out_shape=(
                shape((tiles, FIELDS, MODES, LANES), f32),
                shape((6, tiles, TRACE, LANES), f32),
                shape((8, elems), f32),
            ),
            in_specs=[VMEM] * 4 + [HBM] * 4,
            out_specs=(VMEM,) * 3,
            scratch_shapes=[
                scalar,
                scalar,
                scalar,
                pltpu.VMEM((1, 1), jnp.int32),
                pltpu.VMEM((FIELDS * MODES, 8 * LANES), jnp.bfloat16),
                pltpu.VMEM((tiles, FIELDS, MODES, LANES), f32),
                pltpu.VMEM((6, tiles, TRACE, LANES), f32),
                sems((4,)),
            ],
            compiler_params=params,
            cost_estimate=cost,
            name="own",
        )(*operands)
        rim = pl.pallas_call(
            rim_kernel,
            out_shape=shape((1, FIELDS, MODES, 2 * RIM), f32),
            in_specs=[VMEM] * 2,
            out_specs=VMEM,
            name="rim",
        )(from_far, from_near)
        return first, rim, own

    first, rim, (tendency, outer, forward) = lax.switch(
        shift[0],
        [functools.partial(branch, away) for away in range(n)],
        rotor, far, near, state, neighbours, rows, mixing, dissipation.reshape(1, 1),
        omega.reshape(1, 1), rotor_angle.reshape(1, 1), counts.reshape(1, 1),
    )
    second = fetch(1, first)

    partial, small = pl.pallas_call(
        functools.partial(halo_kernel, plane),
        out_shape=(
            shape((tiles, FIELDS, MODES, LANES), f32),
            shape((-(-(WEIGHTS + inst_count * tiles + plane // LANES) // 8) * 8, LANES), f32),
        ),
        in_specs=[VMEM] * 7,
        out_specs=(VMEM, VMEM),
        scratch_shapes=[pltpu.VMEM((6, TRACE, LANES), f32)],
        compiler_params=params,
        cost_estimate=cost,
        name="halo",
    )(state, neighbours, forward, mixing, tendency, outer, rim)

    return pl.pallas_call(
        functools.partial(final_kernel, plane),
        out_shape=shape(state.shape, f32),
        in_specs=[VMEM] * (3 + inst_count),
        out_specs=ANY,
        scratch_shapes=[
            pltpu.VMEM((tiles, FIELDS, MODES, LANES), f32),
            sems((tiles,)),
        ],
        compiler_params=params,
        name="final",
    )(partial, small, first, second, *others)


def solution(mesh):
    return jax.shard_map(
        shards,
        mesh=mesh,
        in_specs=(
            P("inst", None, None, "space"),
            P("space"),
            P(),
            P(),
            P(),
            P("inst"),
            P("space"),
            P(None, "space"),
            P("inst", "space"),
        ),
        out_specs=P("inst", None, None, "space"),
        check_vma=False,
    )
```

```python
import functools
import math

import jax
import jax.numpy as jnp
import numpy as np
from jax import lax
from jax.experimental import pallas as pl
from jax.experimental.pallas import tpu as pltpu
from jax.sharding import PartitionSpec as P

RIM = 64
FIELDS = 5
MODES = 64
FACE = 16
TRACE = FIELDS * FACE
LANES = 128
COURANT = 0.5

VMEM = pl.BlockSpec(memory_space=pltpu.VMEM)
SMEM = pl.BlockSpec(memory_space=pltpu.SMEM)
ANY = pl.BlockSpec(memory_space=pl.ANY)
HBM = pl.BlockSpec(memory_space=pltpu.HBM)


def gll_table():
    nodes = np.array([-1.0, -1.0 / math.sqrt(5.0), 1.0 / math.sqrt(5.0), 1.0])
    barycentric = np.array(
        [1.0 / np.prod([nodes[j] - nodes[k] for k in range(4) if k != j]) for j in range(4)]
    )
    derivative = np.zeros((4, 4))
    for i in range(4):
        for j in range(4):
            if i != j:
                derivative[i, j] = barycentric[j] / barycentric[i] / (nodes[i] - nodes[j])
        derivative[i, i] = -np.sum(derivative[i])
    return derivative


def face_nodes(face):
    direction, index = face // 2, 3 * (face % 2)
    nodes = []
    for first in range(4):
        for second in range(4):
            if direction == 0:
                nodes.append(16 * index + 4 * first + second)
            elif direction == 1:
                nodes.append(16 * first + 4 * index + second)
            else:
                nodes.append(16 * first + 4 * second + index)
    return nodes


def spectral_values(count):
    values = {0: (count * count + 2.0) / (12.0 * count)}
    for k in range(1 - count, count):
        if k:
            parity = -1.0 if k % 2 else 1.0
            angle = math.pi * k / count
            values[k] = 0.5 * parity / math.tan(angle) + parity / (
                2.0 * count * math.sin(angle) ** 2
            )
    return values


def split(value):
    high = value.astype(jnp.bfloat16)
    low = (value - high.astype(jnp.float32)).astype(jnp.bfloat16)
    return high, low


def fetch_all(pairs, sems):
    copies = [
        pltpu.make_async_copy(source, target, sems.at[k]) for k, (source, target) in enumerate(pairs)
    ]
    for copy in copies:
        copy.start()
    return copies


def tile_of(number):
    return slice(number * LANES, (number + 1) * LANES)


def face_pieces(face):
    direction, index = face // 2, 3 * (face % 2)
    if direction == 0:
        return [(slice(0, 16), slice(16 * index, 16 * index + 16))]
    if direction == 1:
        return [
            (slice(4 * a, 4 * a + 4), slice(16 * a + 4 * index, 16 * a + 4 * index + 4))
            for a in range(4)
        ]
    return [(slice(0, 16), pl.ds(index, 16, stride=4))]


def load_trace(cells, tile, face, trace):
    for field in range(FIELDS):
        for rows, nodes in face_pieces(face):
            target = slice(field * FACE + rows.start, field * FACE + rows.stop)
            trace[tile, target, :] = cells[tile, field, nodes, :]


def choose(sources, positions):
    shape = sources[0].shape
    lane = jnp.broadcast_to(positions & (LANES - 1), shape)
    tile = jnp.broadcast_to(positions >> 7, shape)
    result = None
    for number, source in enumerate(sources):
        found = jnp.take_along_axis(source, lane, axis=1, mode="promise_in_bounds")
        result = found if result is None else jnp.where(tile == number, found, result)
    return result


def base_owner(pairs, plane):
    owners = (pairs // plane).astype(jnp.float32)
    lowest = jnp.min(owners, axis=1, keepdims=True).astype(jnp.int32)
    highest = jnp.max(owners, axis=1, keepdims=True).astype(jnp.int32)
    return jnp.where(highest - lowest <= 1, lowest, highest)


def prep_kernel(
    plane, state, pairs, metric, jacobians, rotor, far, near, shift, rows, mixing,
    pairs_here, metric_here, rim, tiles, sems,
):
    n = lax.axis_size("space")
    me = lax.axis_index("space")
    count = plane // LANES
    copies = fetch_all(
        [(pairs, pairs_here)]
        + [
            (state.at[0, :, :, pl.ds(2 * RIM + tile * LANES, LANES)], tiles.at[tile])
            for tile in range(count)
        ]
        + [(state.at[0, :, :, pl.ds(0, 2 * RIM)], rim)]
        + [(metric, metric_here), (jacobians, mixing)],
        sems,
    )
    copies[0].wait()
    shift[0] = lax.rem(jnp.max(base_owner(pairs_here[...], plane)) - me + n, n)
    rows[1:2, :plane] = pairs_here[...].astype(jnp.float32)
    for tile in range(count):
        copies[1 + tile].wait()
        for field in range(FIELDS):
            rotor[field * FACE : (field + 1) * FACE, tile_of(tile)] = tiles[
                tile, field, pl.ds(0, FACE, stride=4), :
            ]
    for copy in copies[count + 1 :]:
        copy.wait()
    rows[0:1, :] = metric_here[...]
    odd = lax.rem(me, 2) == 1
    lane = lax.broadcasted_iota(jnp.int32, (MODES // 2, 2 * RIM), 1)
    pieces = [
        rim[field, 32 * half : 32 * half + 32, :] for field in range(FIELDS) for half in range(2)
    ]
    for k in range(FIELDS):
        top, bottom = pieces[k], pieces[k + FIELDS]
        head = jnp.where(lane < RIM, top, pltpu.roll(bottom, RIM, 1))
        tail = jnp.where(lane < RIM, pltpu.roll(top, RIM, 1), bottom)
        far[32 * k : 32 * k + 32, :] = jnp.where(odd, tail, head)
        near[32 * k : 32 * k + 32, :] = jnp.where(odd, head, tail)


def derivative_parts(lane):
    table = -gll_table()
    table[0, 0] -= 3.0
    table[3, 3] += 3.0
    table = table.astype(np.float32).tolist()
    row = lax.broadcasted_iota(jnp.int32, (16, LANES), 0)
    column = jnp.broadcast_to(lane & 15, (16, LANES))
    band = (lane & 63) >> 4

    def entry(i, j):
        value = jnp.zeros(j.shape, jnp.float32)
        for first in range(4):
            for second in range(4):
                value = jnp.where((i == first) & (j == second), table[first][second], value)
        return value

    middle = jnp.where((row & 3) == (column & 3), entry(row >> 2, column >> 2), 0.0)
    last = jnp.where((row >> 2) == (column >> 2), entry(row & 3, column & 3), 0.0)
    parts = [[], [], []]
    for a in range(4):
        along = jnp.zeros(lane.shape, jnp.float32)
        for second in range(4):
            along = jnp.where(band == second, table[a][second], along)
        parts[0].append(jnp.where(row == column, along, 0.0))
        parts[1].append(jnp.where(band == a, middle, 0.0))
        parts[2].append(jnp.where(band == a, last, 0.0))
    return parts


def own_kernel(
    state, neighbours, rows, mixing, dissipation, omega, angle, counts,
    tendency, outer, forward, loss, frequency, turn, live_count, matrix, cells, trace, sems,
):
    copies = fetch_all(
        [(dissipation, loss), (omega, frequency), (angle, turn), (counts, live_count)], sems
    )
    count = cells.shape[0]
    elems = state.shape[-1]

    for tile in range(count):
        cells[tile] = state[0, :, :, tile_of(tile)]
    for face in range(6):
        for tile in range(count):
            load_trace(cells, tile, face ^ 1, trace.at[face])

    for face in range(6):
        for tile in range(count):
            sources = [trace[face, source] for source in range(count)]
            outer[face, tile] = choose(sources, neighbours[face : face + 1, tile_of(tile)] - RIM)

    lane = lax.broadcasted_iota(jnp.int32, (1, LANES), 1)
    parts = derivative_parts(lane)
    layout = [((0, 1), 0, 5), ((2, 3), 1, 6), ((4, 0), 2, 7), ((1, 2), 3, None), ((3, 4), 4, None)]
    for g in range(FIELDS):
        values = [
            [jnp.broadcast_to(mixing[g, d : d + 1, f : f + 1], (1, LANES)) for f in range(FIELDS)]
            for d in range(3)
        ]
        for (left, right), high_place, low_place in layout:
            weight = [jnp.where(lane < MODES, values[d][left], values[d][right]) for d in range(3)]
            for a in range(4):
                block = weight[0] * parts[0][a] + weight[1] * parts[1][a] + weight[2] * parts[2][a]
                high, low = split(block)
                band = slice(g * MODES + 16 * a, g * MODES + 16 * a + 16)
                matrix[band, tile_of(high_place)] = high
                if low_place is not None:
                    if left == FIELDS - 1:
                        low = jnp.where(lane < MODES, low, jnp.zeros_like(low))
                    matrix[band, tile_of(low_place)] = low
    high, low = split(state[0].reshape(FIELDS * MODES, elems))
    stacked = jnp.concatenate([high, low, high, jnp.zeros_like(high[:MODES])], axis=0)
    product = jnp.dot(matrix[...], stacked, preferred_element_type=jnp.float32)
    for tile in range(count):
        tendency[tile] = product[:, tile_of(tile)].reshape(FIELDS, MODES, LANES)

    forward[0:2, :] = rows[0:2, :]
    for copy in copies:
        copy.wait()
    for row, value in enumerate(
        [loss[...], frequency[...], turn[...], live_count[...].astype(jnp.float32)]
    ):
        forward[2 + row : 3 + row, :] = jnp.broadcast_to(value, (1, elems))


def flux_row(g, direction, field):
    return (direction * FIELDS + g) * FIELDS + field


FRAME = 3 * FIELDS * FIELDS
WEIGHTS = FRAME + 5


def halo_kernel(
    plane, state, neighbours, forward, mixing, tendency, outer, from_far, from_near,
    partial, small, rim, trace,
):
    n = lax.axis_size("space")
    inst_count = lax.axis_size("inst")
    inst = lax.axis_index("inst")
    count = partial.shape[0]
    elems = state.shape[-1]
    for g in range(FIELDS):
        for d in range(3):
            for field in range(FIELDS):
                row = flux_row(g, d, field)
                small[row : row + 1, :] = jnp.broadcast_to(
                    mixing[g, d : d + 1, field : field + 1], (1, LANES)
                )
    loss, frequency, turn, live_count = [
        forward[2 + row : 3 + row, :LANES] for row in range(4)
    ]
    small[FRAME : FRAME + 1, :] = 3.0 * loss
    small[FRAME + 1 : FRAME + 2, :] = jnp.cos(turn)
    small[FRAME + 2 : FRAME + 3, :] = jnp.sin(turn)

    odd = lax.rem(lax.axis_index("space"), 2) == 1
    half_lane = lax.broadcasted_iota(jnp.int32, (MODES // 2, 2 * RIM), 1)
    for k in range(2 * FIELDS):
        field, half = k // 2, k % 2
        piece = pl.ds(32 * (k % FIELDS), 32)
        left = jnp.where(odd, from_near[piece, :], from_far[piece, :])
        right = jnp.where(odd, from_far[piece, :], from_near[piece, :])
        if k < FIELDS:
            right = pltpu.roll(right, RIM, 1)
        else:
            left = pltpu.roll(left, RIM, 1)
        rim[0, field, 32 * half : 32 * half + 32, :] = jnp.where(half_lane < RIM, left, right)
    for face in range(6):
        load_trace(rim, 0, face ^ 1, trace.at[pl.ds(face, 1)])
    partial[...] = tendency[...]
    lane = lax.broadcasted_iota(jnp.int32, (1, LANES), 1)
    for face in range(6):
        for tile in range(count):
            number = neighbours[face : face + 1, tile_of(tile)]
            previous = number < RIM
            remote = previous | (number >= RIM + elems)
            found = choose([trace[face]], jnp.where(previous, number, number - elems))
            found = jnp.where(remote, found, outer[face, tile])
            if face == 5:
                column = lane + tile * LANES
                sliding = (column >= 2 * RIM) & (column < 2 * RIM + plane)
                found = jnp.where(sliding, 0.0, found)
            parts = [found[field * FACE : (field + 1) * FACE] for field in range(FIELDS)]
            lift(partial, tile, face, mix(small, face, parts), 1.0)

    node = lax.broadcasted_iota(jnp.int32, (MODES, LANES), 0)
    faces = jnp.zeros((MODES, LANES), jnp.float32)
    for index in (node >> 4, (node >> 2) & 3, node & 3):
        faces = faces + jnp.where((index == 0) | (index == 3), 1.0, 0.0)
    spectral = spectral_values(inst_count)
    for tile in range(count):
        scale = forward[0:1, tile_of(tile)]
        step = COURANT / (scale * loss + frequency)
        live = (lane + tile * LANES).astype(jnp.float32) < live_count
        step = jnp.where(live, step, 0.0)
        keep = jnp.where(live, 1.0, 0.0) - step * (frequency * spectral[0])
        keep = keep - (3.0 * loss * step * scale) * faces
        partial[tile] = keep * state[0, :, :, tile_of(tile)] + (step * scale) * partial[tile]
        small[WEIGHTS + tile : WEIGHTS + tile + 1, :] = step * scale
        for away in range(1, inst_count):
            value = jnp.where(
                inst + away < inst_count, spectral[-away], spectral[inst_count - away]
            )
            row = WEIGHTS + away * count + tile
            small[row : row + 1, :] = -step * (frequency * value)

    pairs = forward[1:2, :plane].astype(jnp.int32)
    place = pairs - base_owner(pairs, plane) * plane
    place = jnp.where(place < 0, place + n * plane, place).astype(jnp.float32)
    for tile in range(plane // LANES):
        row = WEIGHTS + inst_count * count + tile
        small[row : row + 1, :] = place[:, tile_of(tile)]


def mix(small, face, parts):
    mixed = []
    for g in range(FIELDS):
        total = None
        for field in range(FIELDS):
            row = flux_row(g, face // 2, field)
            term = small[row : row + 1, :] * parts[field]
            total = term if total is None else total + term
        mixed.append((3.0 if face % 2 else -3.0) * total - small[FRAME : FRAME + 1, :] * parts[g])
    return mixed


def lift(cells, tile, face, mixed, scale):
    for g in range(FIELDS):
        change = scale * mixed[g]
        for rows, nodes in face_pieces(face):
            cells[tile, g, nodes, :] = cells[tile, g, nodes, :] - change[rows]


def final_kernel(plane, partial, small, first, second, *refs):
    inst_count = lax.axis_size("inst")
    others, (result, buffer, sems) = refs[: inst_count - 1], refs[inst_count - 1 :]
    count = buffer.shape[0]
    start, stop = 2 * RIM // LANES, (2 * RIM + plane) // LANES
    copies = []
    for tile in [*range(start), *range(stop, count), *range(start, stop)]:
        for field in range(FIELDS):
            total = partial[tile, field]
            for away in range(1, inst_count):
                row = WEIGHTS + away * count + tile
                other = others[away - 1][0, field, :, tile_of(tile)]
                total = total + small[row : row + 1, :] * other
            buffer[tile, field] = total
        if start <= tile < stop:
            row = WEIGHTS + inst_count * count + tile - start
            found = choose(
                [
                    block[:, tile_of(source)]
                    for block in (first, second)
                    for source in range(plane // LANES)
                ],
                small[row : row + 1, :].astype(jnp.int32),
            )
            parts = [found[field * FACE : (field + 1) * FACE] for field in range(FIELDS)]
            cosine, sine = small[FRAME + 1 : FRAME + 2, :], small[FRAME + 2 : FRAME + 3, :]
            parts[2], parts[3] = (
                cosine * parts[2] - sine * parts[3],
                sine * parts[2] + cosine * parts[3],
            )
            scale = small[WEIGHTS + tile : WEIGHTS + tile + 1, :]
            lift(buffer, tile, 5, mix(small, 5, parts), scale)
        copies.append(
            pltpu.make_async_copy(
                buffer.at[tile], result.at[0, :, :, pl.ds(tile * LANES, LANES)], sems.at[tile]
            )
        )
        copies[-1].start()
    for copy in copies:
        copy.wait()


def shards(
    state, metric, jacobians, dissipation, omega, rotor_angle, counts, neighbours, mortar_pairs
):
    elems = state.shape[-1]
    tiles = elems // LANES
    plane = mortar_pairs.shape[-1]
    n = lax.axis_size("space")
    inst_count = lax.axis_size("inst")
    f32 = jnp.float32
    shape = jax.ShapeDtypeStruct
    sems = pltpu.SemaphoreType.DMA
    scalar = pltpu.VMEM((1, 1), f32)
    params = pltpu.CompilerParams(vmem_limit_bytes=32 * 2**20)
    cost = pl.CostEstimate(flops=2**31, bytes_accessed=2**22, transcendentals=0)

    others = [
        lax.ppermute(state, "inst", [((i + away) % inst_count, i) for i in range(inst_count)])
        for away in range(1, inst_count)
    ]

    rotor, far, near, shift, rows, mixing = pl.pallas_call(
        functools.partial(prep_kernel, plane),
        out_shape=(
            shape((TRACE, plane), f32),
            shape((FIELDS * MODES // 2, 2 * RIM), f32),
            shape((FIELDS * MODES // 2, 2 * RIM), f32),
            shape((1,), jnp.int32),
            shape((8, elems), f32),
            shape((FIELDS, 3, FIELDS), f32),
        ),
        in_specs=[HBM] * 4,
        out_specs=(VMEM, VMEM, VMEM, SMEM, VMEM, VMEM),
        scratch_shapes=[
            pltpu.VMEM((1, plane), jnp.int32),
            pltpu.VMEM((1, elems), f32),
            pltpu.VMEM((FIELDS, MODES, 2 * RIM), f32),
            pltpu.VMEM((plane // LANES, FIELDS, MODES, LANES), f32),
            sems((plane // LANES + 4,)),
        ],
        name="prep",
    )(state, mortar_pairs, metric.reshape(1, elems), jnp.transpose(jacobians, (1, 0, 2)))

    def fetch(away, block):
        if away == 0:
            return block
        return lax.ppermute(block, "space", [((i + away) % n, i) for i in range(n)])

    ends = [(i, (i + 1) % n) for i in range(1, n, 2)]
    middles = [(i, i + 1) for i in range(0, n, 2)]

    def swap(pairs, block):
        return lax.ppermute(block, "space", pairs + [(j, i) for i, j in pairs])

    from_far, from_near = swap(ends, far), swap(middles, near)

    def branch(away, rotor, *operands):
        first = fetch(away, rotor)
        own = pl.pallas_call(
            own_kernel,
            out_shape=(
                shape((tiles, FIELDS, MODES, LANES), f32),
                shape((6, tiles, TRACE, LANES), f32),
                shape((8, elems), f32),
            ),
            in_specs=[VMEM] * 4 + [HBM] * 4,
            out_specs=(VMEM,) * 3,
            scratch_shapes=[
                scalar,
                scalar,
                scalar,
                pltpu.VMEM((1, 1), jnp.int32),
                pltpu.VMEM((FIELDS * MODES, 8 * LANES), jnp.bfloat16),
                pltpu.VMEM((tiles, FIELDS, MODES, LANES), f32),
                pltpu.VMEM((6, tiles, TRACE, LANES), f32),
                sems((4,)),
            ],
            compiler_params=params,
            cost_estimate=cost,
            name="own",
        )(*operands)
        return first, own

    first, (tendency, outer, forward) = lax.switch(
        shift[0],
        [functools.partial(branch, away) for away in range(n)],
        rotor, state, neighbours, rows, mixing, dissipation.reshape(1, 1),
        omega.reshape(1, 1), rotor_angle.reshape(1, 1), counts.reshape(1, 1),
    )
    second = fetch(1, first)

    partial, small = pl.pallas_call(
        functools.partial(halo_kernel, plane),
        out_shape=(
            shape((tiles, FIELDS, MODES, LANES), f32),
            shape((-(-(WEIGHTS + inst_count * tiles + plane // LANES) // 8) * 8, LANES), f32),
        ),
        in_specs=[VMEM] * 8,
        out_specs=(VMEM, VMEM),
        scratch_shapes=[
            pltpu.VMEM((1, FIELDS, MODES, 2 * RIM), f32),
            pltpu.VMEM((6, TRACE, LANES), f32),
        ],
        compiler_params=params,
        cost_estimate=cost,
        name="halo",
    )(state, neighbours, forward, mixing, tendency, outer, from_far, from_near)

    return pl.pallas_call(
        functools.partial(final_kernel, plane),
        out_shape=shape(state.shape, f32),
        in_specs=[VMEM] * (3 + inst_count),
        out_specs=ANY,
        scratch_shapes=[
            pltpu.VMEM((tiles, FIELDS, MODES, LANES), f32),
            sems((tiles,)),
        ],
        compiler_params=params,
        name="final",
    )(partial, small, first, second, *others)


def solution(mesh):
    return jax.shard_map(
        shards,
        mesh=mesh,
        in_specs=(
            P("inst", None, None, "space"),
            P("space"),
            P(),
            P(),
            P(),
            P("inst"),
            P("space"),
            P(None, "space"),
            P("inst", "space"),
        ),
        out_specs=P("inst", None, None, "space"),
        check_vma=False,
    )
```

```python
import functools
import math

import jax
import jax.numpy as jnp
import numpy as np
from jax import lax
from jax.experimental import pallas as pl
from jax.experimental.pallas import tpu as pltpu
from jax.sharding import PartitionSpec as P

RIM = 64
FIELDS = 5
MODES = 64
FACE = 16
TRACE = FIELDS * FACE
LANES = 128
COURANT = 0.5

VMEM = pl.BlockSpec(memory_space=pltpu.VMEM)
SMEM = pl.BlockSpec(memory_space=pltpu.SMEM)
ANY = pl.BlockSpec(memory_space=pl.ANY)
HBM = pl.BlockSpec(memory_space=pltpu.HBM)


def gll_table():
    nodes = np.array([-1.0, -1.0 / math.sqrt(5.0), 1.0 / math.sqrt(5.0), 1.0])
    barycentric = np.array(
        [1.0 / np.prod([nodes[j] - nodes[k] for k in range(4) if k != j]) for j in range(4)]
    )
    derivative = np.zeros((4, 4))
    for i in range(4):
        for j in range(4):
            if i != j:
                derivative[i, j] = barycentric[j] / barycentric[i] / (nodes[i] - nodes[j])
        derivative[i, i] = -np.sum(derivative[i])
    return derivative


def face_nodes(face):
    direction, index = face // 2, 3 * (face % 2)
    nodes = []
    for first in range(4):
        for second in range(4):
            if direction == 0:
                nodes.append(16 * index + 4 * first + second)
            elif direction == 1:
                nodes.append(16 * first + 4 * index + second)
            else:
                nodes.append(16 * first + 4 * second + index)
    return nodes


def spectral_values(count):
    values = {0: (count * count + 2.0) / (12.0 * count)}
    for k in range(1 - count, count):
        if k:
            parity = -1.0 if k % 2 else 1.0
            angle = math.pi * k / count
            values[k] = 0.5 * parity / math.tan(angle) + parity / (
                2.0 * count * math.sin(angle) ** 2
            )
    return values


def split(value):
    high = value.astype(jnp.bfloat16)
    low = (value - high.astype(jnp.float32)).astype(jnp.bfloat16)
    return high, low


def fetch_all(pairs, sems):
    copies = [
        pltpu.make_async_copy(source, target, sems.at[k]) for k, (source, target) in enumerate(pairs)
    ]
    for copy in copies:
        copy.start()
    return copies


def tile_of(number):
    return slice(number * LANES, (number + 1) * LANES)


def face_pieces(face):
    direction, index = face // 2, 3 * (face % 2)
    if direction == 0:
        return [(slice(0, 16), slice(16 * index, 16 * index + 16))]
    if direction == 1:
        return [
            (slice(4 * a, 4 * a + 4), slice(16 * a + 4 * index, 16 * a + 4 * index + 4))
            for a in range(4)
        ]
    return [(slice(0, 16), pl.ds(index, 16, stride=4))]


def load_trace(cells, tile, face, trace):
    for field in range(FIELDS):
        for rows, nodes in face_pieces(face):
            target = slice(field * FACE + rows.start, field * FACE + rows.stop)
            trace[tile, target, :] = cells[tile, field, nodes, :]


def choose(sources, positions):
    shape = sources[0].shape
    lane = jnp.broadcast_to(positions & (LANES - 1), shape)
    tile = jnp.broadcast_to(positions >> 7, shape)
    result = None
    for number, source in enumerate(sources):
        found = jnp.take_along_axis(source, lane, axis=1, mode="promise_in_bounds")
        result = found if result is None else jnp.where(tile == number, found, result)
    return result


def base_owner(pairs, plane):
    owners = (pairs // plane).astype(jnp.float32)
    lowest = jnp.min(owners, axis=1, keepdims=True).astype(jnp.int32)
    highest = jnp.max(owners, axis=1, keepdims=True).astype(jnp.int32)
    return jnp.where(highest - lowest <= 1, lowest, highest)


def prep_kernel(
    plane, state, pairs, metric, jacobians, rotor, far, near, shift, rows, mixing,
    pairs_here, metric_here, rim, tiles, sems,
):
    n = lax.axis_size("space")
    me = lax.axis_index("space")
    count = plane // LANES
    copies = fetch_all(
        [(pairs, pairs_here)]
        + [
            (state.at[0, :, :, pl.ds(2 * RIM + tile * LANES, LANES)], tiles.at[tile])
            for tile in range(count)
        ]
        + [(state.at[0, :, :, pl.ds(0, 2 * RIM)], rim)]
        + [(metric, metric_here), (jacobians, mixing)],
        sems,
    )
    copies[0].wait()
    shift[0] = lax.rem(jnp.max(base_owner(pairs_here[...], plane)) - me + n, n)
    rows[1:2, :plane] = pairs_here[...].astype(jnp.float32)
    for tile in range(count):
        copies[1 + tile].wait()
        for field in range(FIELDS):
            rotor[field * FACE : (field + 1) * FACE, tile_of(tile)] = tiles[
                tile, field, pl.ds(0, FACE, stride=4), :
            ]
    for copy in copies[count + 1 :]:
        copy.wait()
    rows[0:1, :] = metric_here[...]
    odd = lax.rem(me, 2) == 1
    lane = lax.broadcasted_iota(jnp.int32, (MODES // 2, 2 * RIM), 1)
    pieces = [
        rim[field, 32 * half : 32 * half + 32, :] for field in range(FIELDS) for half in range(2)
    ]
    for k in range(FIELDS):
        top, bottom = pieces[k], pieces[k + FIELDS]
        head = jnp.where(lane < RIM, top, pltpu.roll(bottom, RIM, 1))
        tail = jnp.where(lane < RIM, pltpu.roll(top, RIM, 1), bottom)
        far[32 * k : 32 * k + 32, :] = jnp.where(odd, tail, head)
        near[32 * k : 32 * k + 32, :] = jnp.where(odd, head, tail)


def derivative_parts(lane):
    table = -gll_table()
    table[0, 0] -= 3.0
    table[3, 3] += 3.0
    table = table.astype(np.float32).tolist()
    row = lax.broadcasted_iota(jnp.int32, (16, LANES), 0)
    column = jnp.broadcast_to(lane & 15, (16, LANES))
    band = (lane & 63) >> 4

    def entry(i, j):
        value = jnp.zeros(j.shape, jnp.float32)
        for first in range(4):
            for second in range(4):
                value = jnp.where((i == first) & (j == second), table[first][second], value)
        return value

    middle = jnp.where((row & 3) == (column & 3), entry(row >> 2, column >> 2), 0.0)
    last = jnp.where((row >> 2) == (column >> 2), entry(row & 3, column & 3), 0.0)
    parts = [[], [], []]
    for a in range(4):
        along = jnp.zeros(lane.shape, jnp.float32)
        for second in range(4):
            along = jnp.where(band == second, table[a][second], along)
        parts[0].append(jnp.where(row == column, along, 0.0))
        parts[1].append(jnp.where(band == a, middle, 0.0))
        parts[2].append(jnp.where(band == a, last, 0.0))
    return parts


def own_kernel(state, neighbours, mixing, tendency, outer, matrix, cells, trace):
    count = cells.shape[0]
    elems = state.shape[-1]

    for tile in range(count):
        cells[tile] = state[0, :, :, tile_of(tile)]
    for face in range(6):
        for tile in range(count):
            load_trace(cells, tile, face ^ 1, trace.at[face])

    for face in range(6):
        for tile in range(count):
            sources = [trace[face, source] for source in range(count)]
            outer[face, tile] = choose(sources, neighbours[face : face + 1, tile_of(tile)] - RIM)

    lane = lax.broadcasted_iota(jnp.int32, (1, LANES), 1)
    parts = derivative_parts(lane)
    layout = [((0, 1), 0, 5), ((2, 3), 1, 6), ((4, 0), 2, 7), ((1, 2), 3, None), ((3, 4), 4, None)]
    for g in range(FIELDS):
        values = [
            [jnp.broadcast_to(mixing[g, d : d + 1, f : f + 1], (1, LANES)) for f in range(FIELDS)]
            for d in range(3)
        ]
        for (left, right), high_place, low_place in layout:
            weight = [jnp.where(lane < MODES, values[d][left], values[d][right]) for d in range(3)]
            for a in range(4):
                block = weight[0] * parts[0][a] + weight[1] * parts[1][a] + weight[2] * parts[2][a]
                high, low = split(block)
                band = slice(g * MODES + 16 * a, g * MODES + 16 * a + 16)
                matrix[band, tile_of(high_place)] = high
                if low_place is not None:
                    if left == FIELDS - 1:
                        low = jnp.where(lane < MODES, low, jnp.zeros_like(low))
                    matrix[band, tile_of(low_place)] = low
    high, low = split(state[0].reshape(FIELDS * MODES, elems))
    stacked = jnp.concatenate([high, low, high, jnp.zeros_like(high[:MODES])], axis=0)
    product = jnp.dot(matrix[...], stacked, preferred_element_type=jnp.float32)
    for tile in range(count):
        tendency[tile] = product[:, tile_of(tile)].reshape(FIELDS, MODES, LANES)


def pull_kernel(
    rows, dissipation, omega, angle, counts, forward, loss, frequency, turn, live_count, sems
):
    copies = fetch_all(
        [(dissipation, loss), (omega, frequency), (angle, turn), (counts, live_count)], sems
    )
    forward[0:2, :] = rows[0:2, :]
    for copy in copies:
        copy.wait()
    for row, value in enumerate(
        [loss[...], frequency[...], turn[...], live_count[...].astype(jnp.float32)]
    ):
        forward[2 + row : 3 + row, :] = jnp.broadcast_to(value, (1, forward.shape[1]))


def flux_row(g, direction, field):
    return (direction * FIELDS + g) * FIELDS + field


FRAME = 3 * FIELDS * FIELDS
WEIGHTS = FRAME + 5


def halo_kernel(
    plane, state, neighbours, forward, mixing, tendency, outer, from_far, from_near,
    partial, small, rim, trace,
):
    n = lax.axis_size("space")
    inst_count = lax.axis_size("inst")
    inst = lax.axis_index("inst")
    count = partial.shape[0]
    elems = state.shape[-1]
    for g in range(FIELDS):
        for d in range(3):
            for field in range(FIELDS):
                row = flux_row(g, d, field)
                small[row : row + 1, :] = jnp.broadcast_to(
                    mixing[g, d : d + 1, field : field + 1], (1, LANES)
                )
    loss, frequency, turn, live_count = [
        forward[2 + row : 3 + row, :LANES] for row in range(4)
    ]
    small[FRAME : FRAME + 1, :] = 3.0 * loss
    small[FRAME + 1 : FRAME + 2, :] = jnp.cos(turn)
    small[FRAME + 2 : FRAME + 3, :] = jnp.sin(turn)

    odd = lax.rem(lax.axis_index("space"), 2) == 1
    half_lane = lax.broadcasted_iota(jnp.int32, (MODES // 2, 2 * RIM), 1)
    for k in range(2 * FIELDS):
        field, half = k // 2, k % 2
        piece = pl.ds(32 * (k % FIELDS), 32)
        left = jnp.where(odd, from_near[piece, :], from_far[piece, :])
        right = jnp.where(odd, from_far[piece, :], from_near[piece, :])
        if k < FIELDS:
            right = pltpu.roll(right, RIM, 1)
        else:
            left = pltpu.roll(left, RIM, 1)
        rim[0, field, 32 * half : 32 * half + 32, :] = jnp.where(half_lane < RIM, left, right)
    for face in range(6):
        load_trace(rim, 0, face ^ 1, trace.at[pl.ds(face, 1)])
    partial[...] = tendency[...]
    lane = lax.broadcasted_iota(jnp.int32, (1, LANES), 1)
    for face in range(6):
        for tile in range(count):
            number = neighbours[face : face + 1, tile_of(tile)]
            previous = number < RIM
            remote = previous | (number >= RIM + elems)
            found = choose([trace[face]], jnp.where(previous, number, number - elems))
            found = jnp.where(remote, found, outer[face, tile])
            if face == 5:
                column = lane + tile * LANES
                sliding = (column >= 2 * RIM) & (column < 2 * RIM + plane)
                found = jnp.where(sliding, 0.0, found)
            parts = [found[field * FACE : (field + 1) * FACE] for field in range(FIELDS)]
            lift(partial, tile, face, mix(small, face, parts), 1.0)

    node = lax.broadcasted_iota(jnp.int32, (MODES, LANES), 0)
    faces = jnp.zeros((MODES, LANES), jnp.float32)
    for index in (node >> 4, (node >> 2) & 3, node & 3):
        faces = faces + jnp.where((index == 0) | (index == 3), 1.0, 0.0)
    spectral = spectral_values(inst_count)
    for tile in range(count):
        scale = forward[0:1, tile_of(tile)]
        step = COURANT / (scale * loss + frequency)
        live = (lane + tile * LANES).astype(jnp.float32) < live_count
        step = jnp.where(live, step, 0.0)
        keep = jnp.where(live, 1.0, 0.0) - step * (frequency * spectral[0])
        keep = keep - (3.0 * loss * step * scale) * faces
        partial[tile] = keep * state[0, :, :, tile_of(tile)] + (step * scale) * partial[tile]
        small[WEIGHTS + tile : WEIGHTS + tile + 1, :] = step * scale
        for away in range(1, inst_count):
            value = jnp.where(
                inst + away < inst_count, spectral[-away], spectral[inst_count - away]
            )
            row = WEIGHTS + away * count + tile
            small[row : row + 1, :] = -step * (frequency * value)

    pairs = forward[1:2, :plane].astype(jnp.int32)
    place = pairs - base_owner(pairs, plane) * plane
    place = jnp.where(place < 0, place + n * plane, place).astype(jnp.float32)
    for tile in range(plane // LANES):
        row = WEIGHTS + inst_count * count + tile
        small[row : row + 1, :] = place[:, tile_of(tile)]


def mix(small, face, parts):
    mixed = []
    for g in range(FIELDS):
        total = None
        for field in range(FIELDS):
            row = flux_row(g, face // 2, field)
            term = small[row : row + 1, :] * parts[field]
            total = term if total is None else total + term
        mixed.append((3.0 if face % 2 else -3.0) * total - small[FRAME : FRAME + 1, :] * parts[g])
    return mixed


def lift(cells, tile, face, mixed, scale):
    for g in range(FIELDS):
        change = scale * mixed[g]
        for rows, nodes in face_pieces(face):
            cells[tile, g, nodes, :] = cells[tile, g, nodes, :] - change[rows]


def final_kernel(plane, partial, small, first, second, last, *refs):
    inst_count = lax.axis_size("inst")
    others, (result, buffer, chosen, sems) = refs[: inst_count - 1], refs[inst_count - 1 :]
    count = buffer.shape[0]
    is_last = lax.axis_index("space") == lax.axis_size("space") - 1

    @pl.when(is_last)
    def _():
        copy = pltpu.make_async_copy(last, chosen, sems.at[count])
        copy.start()
        copy.wait()

    @pl.when(jnp.logical_not(is_last))
    def _():
        chosen[...] = second[...]

    start, stop = 2 * RIM // LANES, (2 * RIM + plane) // LANES
    copies = []
    for tile in [*range(start), *range(stop, count), *range(start, stop)]:
        for field in range(FIELDS):
            total = partial[tile, field]
            for away in range(1, inst_count):
                row = WEIGHTS + away * count + tile
                other = others[away - 1][0, field, :, tile_of(tile)]
                total = total + small[row : row + 1, :] * other
            buffer[tile, field] = total
        if start <= tile < stop:
            row = WEIGHTS + inst_count * count + tile - start
            found = choose(
                [
                    block[:, tile_of(source)]
                    for block in (first, chosen)
                    for source in range(plane // LANES)
                ],
                small[row : row + 1, :].astype(jnp.int32),
            )
            parts = [found[field * FACE : (field + 1) * FACE] for field in range(FIELDS)]
            cosine, sine = small[FRAME + 1 : FRAME + 2, :], small[FRAME + 2 : FRAME + 3, :]
            parts[2], parts[3] = (
                cosine * parts[2] - sine * parts[3],
                sine * parts[2] + cosine * parts[3],
            )
            scale = small[WEIGHTS + tile : WEIGHTS + tile + 1, :]
            lift(buffer, tile, 5, mix(small, 5, parts), scale)
        copies.append(
            pltpu.make_async_copy(
                buffer.at[tile], result.at[0, :, :, pl.ds(tile * LANES, LANES)], sems.at[tile]
            )
        )
        copies[-1].start()
    for copy in copies:
        copy.wait()


def shards(
    state, metric, jacobians, dissipation, omega, rotor_angle, counts, neighbours, mortar_pairs
):
    elems = state.shape[-1]
    tiles = elems // LANES
    plane = mortar_pairs.shape[-1]
    n = lax.axis_size("space")
    inst_count = lax.axis_size("inst")
    f32 = jnp.float32
    shape = jax.ShapeDtypeStruct
    sems = pltpu.SemaphoreType.DMA
    scalar = pltpu.VMEM((1, 1), f32)
    params = pltpu.CompilerParams(vmem_limit_bytes=32 * 2**20)
    cost = pl.CostEstimate(flops=2**31, bytes_accessed=2**22, transcendentals=0)

    others = [
        lax.ppermute(state, "inst", [((i + away) % inst_count, i) for i in range(inst_count)])
        for away in range(1, inst_count)
    ]

    rotor, far, near, shift, rows, mixing = pl.pallas_call(
        functools.partial(prep_kernel, plane),
        out_shape=(
            shape((TRACE, plane), f32),
            shape((FIELDS * MODES // 2, 2 * RIM), f32),
            shape((FIELDS * MODES // 2, 2 * RIM), f32),
            shape((1,), jnp.int32),
            shape((8, elems), f32),
            shape((FIELDS, 3, FIELDS), f32),
        ),
        in_specs=[HBM] * 4,
        out_specs=(VMEM, VMEM, VMEM, SMEM, VMEM, VMEM),
        scratch_shapes=[
            pltpu.VMEM((1, plane), jnp.int32),
            pltpu.VMEM((1, elems), f32),
            pltpu.VMEM((FIELDS, MODES, 2 * RIM), f32),
            pltpu.VMEM((plane // LANES, FIELDS, MODES, LANES), f32),
            sems((plane // LANES + 4,)),
        ],
        name="prep",
    )(state, mortar_pairs, metric.reshape(1, elems), jnp.transpose(jacobians, (1, 0, 2)))

    def fetch(away, block):
        if away == 0:
            return block
        return lax.ppermute(block, "space", [((i + away) % n, i) for i in range(n)])

    ends = [(i, (i + 1) % n) for i in range(1, n, 2)]
    middles = [(i, i + 1) for i in range(0, n, 2)]

    def swap(pairs, block):
        return lax.ppermute(block, "space", pairs + [(j, i) for i, j in pairs])

    def branch(away, rotor, far, near, state, neighbours, mixing, *operands):
        first = fetch(away, rotor)
        last = rotor if away == n - 1 else lax.ppermute(rotor, "space", [(away, n - 1)])
        from_far, from_near = swap(ends, far), swap(middles, near)
        own = pl.pallas_call(
            own_kernel,
            out_shape=(
                shape((tiles, FIELDS, MODES, LANES), f32),
                shape((6, tiles, TRACE, LANES), f32),
            ),
            in_specs=[VMEM] * 3,
            out_specs=(VMEM,) * 2,
            scratch_shapes=[
                pltpu.VMEM((FIELDS * MODES, 8 * LANES), jnp.bfloat16),
                pltpu.VMEM((tiles, FIELDS, MODES, LANES), f32),
                pltpu.VMEM((6, tiles, TRACE, LANES), f32),
            ],
            compiler_params=params,
            cost_estimate=cost,
            name="own",
        )(state, neighbours, mixing)
        forward = pl.pallas_call(
            pull_kernel,
            out_shape=shape((8, elems), f32),
            in_specs=[VMEM] + [HBM] * 4,
            out_specs=VMEM,
            scratch_shapes=[
                scalar,
                scalar,
                scalar,
                pltpu.VMEM((1, 1), jnp.int32),
                sems((4,)),
            ],
            name="pull",
        )(*operands)
        return first, last, from_far, from_near, own, forward

    first, last, from_far, from_near, (tendency, outer), forward = lax.switch(
        shift[0],
        [functools.partial(branch, away) for away in range(n)],
        rotor, far, near, state, neighbours, mixing, rows, dissipation.reshape(1, 1),
        omega.reshape(1, 1), rotor_angle.reshape(1, 1), counts.reshape(1, 1),
    )
    second = lax.ppermute(first, "space", [(i + 1, i) for i in range(n - 1)])

    partial, small = pl.pallas_call(
        functools.partial(halo_kernel, plane),
        out_shape=(
            shape((tiles, FIELDS, MODES, LANES), f32),
            shape((-(-(WEIGHTS + inst_count * tiles + plane // LANES) // 8) * 8, LANES), f32),
        ),
        in_specs=[VMEM] * 8,
        out_specs=(VMEM, VMEM),
        scratch_shapes=[
            pltpu.VMEM((1, FIELDS, MODES, 2 * RIM), f32),
            pltpu.VMEM((6, TRACE, LANES), f32),
        ],
        compiler_params=params,
        cost_estimate=cost,
        name="halo",
    )(state, neighbours, forward, mixing, tendency, outer, from_far, from_near)

    return pl.pallas_call(
        functools.partial(final_kernel, plane),
        out_shape=shape(state.shape, f32),
        in_specs=[VMEM] * 4 + [ANY] + [VMEM] * (inst_count - 1),
        out_specs=ANY,
        scratch_shapes=[
            pltpu.VMEM((tiles, FIELDS, MODES, LANES), f32),
            pltpu.VMEM((TRACE, plane), f32),
            sems((tiles + 1,)),
        ],
        compiler_params=params,
        name="final",
    )(partial, small, first, second, last, *others)


def solution(mesh):
    return jax.shard_map(
        shards,
        mesh=mesh,
        in_specs=(
            P("inst", None, None, "space"),
            P("space"),
            P(),
            P(),
            P(),
            P("inst"),
            P("space"),
            P(None, "space"),
            P("inst", "space"),
        ),
        out_specs=P("inst", None, None, "space"),
        check_vma=False,
    )
```

```python
import functools
import math

import jax
import jax.numpy as jnp
import numpy as np
from jax import lax
from jax.experimental import pallas as pl
from jax.experimental.pallas import tpu as pltpu
from jax.sharding import PartitionSpec as P

RIM = 64
FIELDS = 5
MODES = 64
FACE = 16
TRACE = FIELDS * FACE
LANES = 128
COURANT = 0.5

VMEM = pl.BlockSpec(memory_space=pltpu.VMEM)
SMEM = pl.BlockSpec(memory_space=pltpu.SMEM)
ANY = pl.BlockSpec(memory_space=pl.ANY)
HBM = pl.BlockSpec(memory_space=pltpu.HBM)


def gll_table():
    nodes = np.array([-1.0, -1.0 / math.sqrt(5.0), 1.0 / math.sqrt(5.0), 1.0])
    barycentric = np.array(
        [1.0 / np.prod([nodes[j] - nodes[k] for k in range(4) if k != j]) for j in range(4)]
    )
    derivative = np.zeros((4, 4))
    for i in range(4):
        for j in range(4):
            if i != j:
                derivative[i, j] = barycentric[j] / barycentric[i] / (nodes[i] - nodes[j])
        derivative[i, i] = -np.sum(derivative[i])
    return derivative


def face_nodes(face):
    direction, index = face // 2, 3 * (face % 2)
    nodes = []
    for first in range(4):
        for second in range(4):
            if direction == 0:
                nodes.append(16 * index + 4 * first + second)
            elif direction == 1:
                nodes.append(16 * first + 4 * index + second)
            else:
                nodes.append(16 * first + 4 * second + index)
    return nodes


def spectral_values(count):
    values = {0: (count * count + 2.0) / (12.0 * count)}
    for k in range(1 - count, count):
        if k:
            parity = -1.0 if k % 2 else 1.0
            angle = math.pi * k / count
            values[k] = 0.5 * parity / math.tan(angle) + parity / (
                2.0 * count * math.sin(angle) ** 2
            )
    return values


def split(value):
    high = value.astype(jnp.bfloat16)
    low = (value - high.astype(jnp.float32)).astype(jnp.bfloat16)
    return high, low


def fetch_all(pairs, sems):
    copies = [
        pltpu.make_async_copy(source, target, sems.at[k]) for k, (source, target) in enumerate(pairs)
    ]
    for copy in copies:
        copy.start()
    return copies


def tile_of(number):
    return slice(number * LANES, (number + 1) * LANES)


def face_pieces(face):
    direction, index = face // 2, 3 * (face % 2)
    if direction == 0:
        return [(slice(0, 16), slice(16 * index, 16 * index + 16))]
    if direction == 1:
        return [
            (slice(4 * a, 4 * a + 4), slice(16 * a + 4 * index, 16 * a + 4 * index + 4))
            for a in range(4)
        ]
    return [(slice(0, 16), pl.ds(index, 16, stride=4))]


def load_trace(cells, tile, face, trace):
    for field in range(FIELDS):
        for rows, nodes in face_pieces(face):
            target = slice(field * FACE + rows.start, field * FACE + rows.stop)
            trace[tile, target, :] = cells[tile, field, nodes, :]


def choose(sources, positions):
    shape = sources[0].shape
    lane = jnp.broadcast_to(positions & (LANES - 1), shape)
    tile = jnp.broadcast_to(positions >> 7, shape)
    result = None
    for number, source in enumerate(sources):
        found = jnp.take_along_axis(source, lane, axis=1, mode="promise_in_bounds")
        result = found if result is None else jnp.where(tile == number, found, result)
    return result


def base_owner(pairs, plane):
    owners = (pairs // plane).astype(jnp.float32)
    lowest = jnp.min(owners, axis=1, keepdims=True).astype(jnp.int32)
    highest = jnp.max(owners, axis=1, keepdims=True).astype(jnp.int32)
    return jnp.where(highest - lowest <= 1, lowest, highest)


def prep_kernel(
    plane, state, pairs, metric, jacobians, rotor, far, near, shift, rows, mixing,
    pairs_here, metric_here, rim, tiles, sems,
):
    n = lax.axis_size("space")
    me = lax.axis_index("space")
    count = plane // LANES
    copies = fetch_all(
        [(pairs, pairs_here)]
        + [
            (state.at[0, :, :, pl.ds(2 * RIM + tile * LANES, LANES)], tiles.at[tile])
            for tile in range(count)
        ]
        + [(state.at[0, :, :, pl.ds(0, 2 * RIM)], rim)]
        + [(metric, metric_here), (jacobians, mixing)],
        sems,
    )
    copies[0].wait()
    shift[0] = lax.rem(jnp.max(base_owner(pairs_here[...], plane)) - me + n, n)
    rows[1:2, :plane] = pairs_here[...].astype(jnp.float32)
    for tile in range(count):
        copies[1 + tile].wait()
        for field in range(FIELDS):
            rotor[field * FACE : (field + 1) * FACE, tile_of(tile)] = tiles[
                tile, field, pl.ds(0, FACE, stride=4), :
            ]
    for copy in copies[count + 1 :]:
        copy.wait()
    rows[0:1, :] = metric_here[...]
    odd = lax.rem(me, 2) == 1
    lane = lax.broadcasted_iota(jnp.int32, (MODES // 2, 2 * RIM), 1)
    pieces = [
        rim[field, 32 * half : 32 * half + 32, :] for field in range(FIELDS) for half in range(2)
    ]
    for k in range(FIELDS):
        top, bottom = pieces[k], pieces[k + FIELDS]
        head = jnp.where(lane < RIM, top, pltpu.roll(bottom, RIM, 1))
        tail = jnp.where(lane < RIM, pltpu.roll(top, RIM, 1), bottom)
        far[32 * k : 32 * k + 32, :] = jnp.where(odd, tail, head)
        near[32 * k : 32 * k + 32, :] = jnp.where(odd, head, tail)


def derivative_parts(lane):
    table = -gll_table()
    table[0, 0] -= 3.0
    table[3, 3] += 3.0
    table = table.astype(np.float32).tolist()
    row = lax.broadcasted_iota(jnp.int32, (16, LANES), 0)
    column = jnp.broadcast_to(lane & 15, (16, LANES))
    band = (lane & 63) >> 4

    def entry(i, j):
        value = jnp.zeros(j.shape, jnp.float32)
        for first in range(4):
            for second in range(4):
                value = jnp.where((i == first) & (j == second), table[first][second], value)
        return value

    middle = jnp.where((row & 3) == (column & 3), entry(row >> 2, column >> 2), 0.0)
    last = jnp.where((row >> 2) == (column >> 2), entry(row & 3, column & 3), 0.0)
    parts = [[], [], []]
    for a in range(4):
        along = jnp.zeros(lane.shape, jnp.float32)
        for second in range(4):
            along = jnp.where(band == second, table[a][second], along)
        parts[0].append(jnp.where(row == column, along, 0.0))
        parts[1].append(jnp.where(band == a, middle, 0.0))
        parts[2].append(jnp.where(band == a, last, 0.0))
    return parts


def own_kernel(
    state, neighbours, rows, mixing, dissipation, omega, angle, counts,
    tendency, outer, forward, loss, frequency, turn, live_count, matrix, cells, trace, sems,
):
    copies = fetch_all(
        [(dissipation, loss), (omega, frequency), (angle, turn), (counts, live_count)], sems
    )
    count = cells.shape[0]
    elems = state.shape[-1]

    for tile in range(count):
        cells[tile] = state[0, :, :, tile_of(tile)]
    for face in range(6):
        for tile in range(count):
            load_trace(cells, tile, face ^ 1, trace.at[face])

    for face in range(6):
        for tile in range(count):
            sources = [trace[face, source] for source in range(count)]
            outer[face, tile] = choose(sources, neighbours[face : face + 1, tile_of(tile)] - RIM)

    lane = lax.broadcasted_iota(jnp.int32, (1, LANES), 1)
    parts = derivative_parts(lane)
    layout = [((0, 1), 0, 5), ((2, 3), 1, 6), ((4, 0), 2, 7), ((1, 2), 3, None), ((3, 4), 4, None)]
    for g in range(FIELDS):
        values = [
            [jnp.broadcast_to(mixing[g, d : d + 1, f : f + 1], (1, LANES)) for f in range(FIELDS)]
            for d in range(3)
        ]
        for (left, right), high_place, low_place in layout:
            weight = [jnp.where(lane < MODES, values[d][left], values[d][right]) for d in range(3)]
            for a in range(4):
                block = weight[0] * parts[0][a] + weight[1] * parts[1][a] + weight[2] * parts[2][a]
                high, low = split(block)
                band = slice(g * MODES + 16 * a, g * MODES + 16 * a + 16)
                matrix[band, tile_of(high_place)] = high
                if low_place is not None:
                    if left == FIELDS - 1:
                        low = jnp.where(lane < MODES, low, jnp.zeros_like(low))
                    matrix[band, tile_of(low_place)] = low
    high, low = split(state[0].reshape(FIELDS * MODES, elems))
    stacked = jnp.concatenate([high, low, high, jnp.zeros_like(high[:MODES])], axis=0)
    product = jnp.dot(matrix[...], stacked, preferred_element_type=jnp.float32)
    for tile in range(count):
        tendency[tile] = product[:, tile_of(tile)].reshape(FIELDS, MODES, LANES)

    forward[0:2, :] = rows[0:2, :]
    for copy in copies:
        copy.wait()
    for row, value in enumerate(
        [loss[...], frequency[...], turn[...], live_count[...].astype(jnp.float32)]
    ):
        forward[2 + row : 3 + row, :] = jnp.broadcast_to(value, (1, elems))


def flux_row(g, direction, field):
    return (direction * FIELDS + g) * FIELDS + field


FRAME = 3 * FIELDS * FIELDS
WEIGHTS = FRAME + 5


def halo_kernel(
    plane, state, neighbours, forward, mixing, tendency, outer, from_far, from_near,
    partial, small, rim, trace,
):
    n = lax.axis_size("space")
    inst_count = lax.axis_size("inst")
    inst = lax.axis_index("inst")
    count = partial.shape[0]
    elems = state.shape[-1]
    for g in range(FIELDS):
        for d in range(3):
            for field in range(FIELDS):
                row = flux_row(g, d, field)
                small[row : row + 1, :] = jnp.broadcast_to(
                    mixing[g, d : d + 1, field : field + 1], (1, LANES)
                )
    loss, frequency, turn, live_count = [
        forward[2 + row : 3 + row, :LANES] for row in range(4)
    ]
    small[FRAME : FRAME + 1, :] = 3.0 * loss
    small[FRAME + 1 : FRAME + 2, :] = jnp.cos(turn)
    small[FRAME + 2 : FRAME + 3, :] = jnp.sin(turn)

    odd = lax.rem(lax.axis_index("space"), 2) == 1
    half_lane = lax.broadcasted_iota(jnp.int32, (MODES // 2, 2 * RIM), 1)
    for k in range(2 * FIELDS):
        field, half = k // 2, k % 2
        piece = pl.ds(32 * (k % FIELDS), 32)
        left = jnp.where(odd, from_near[piece, :], from_far[piece, :])
        right = jnp.where(odd, from_far[piece, :], from_near[piece, :])
        if k < FIELDS:
            right = pltpu.roll(right, RIM, 1)
        else:
            left = pltpu.roll(left, RIM, 1)
        rim[0, field, 32 * half : 32 * half + 32, :] = jnp.where(half_lane < RIM, left, right)
    for face in range(6):
        load_trace(rim, 0, face ^ 1, trace.at[pl.ds(face, 1)])
    partial[...] = tendency[...]
    lane = lax.broadcasted_iota(jnp.int32, (1, LANES), 1)
    for face in range(6):
        for tile in range(count):
            number = neighbours[face : face + 1, tile_of(tile)]
            previous = number < RIM
            remote = previous | (number >= RIM + elems)
            found = choose([trace[face]], jnp.where(previous, number, number - elems))
            found = jnp.where(remote, found, outer[face, tile])
            if face == 5:
                column = lane + tile * LANES
                sliding = (column >= 2 * RIM) & (column < 2 * RIM + plane)
                found = jnp.where(sliding, 0.0, found)
            parts = [found[field * FACE : (field + 1) * FACE] for field in range(FIELDS)]
            lift(partial, tile, face, mix(small, face, parts), 1.0)

    node = lax.broadcasted_iota(jnp.int32, (MODES, LANES), 0)
    faces = jnp.zeros((MODES, LANES), jnp.float32)
    for index in (node >> 4, (node >> 2) & 3, node & 3):
        faces = faces + jnp.where((index == 0) | (index == 3), 1.0, 0.0)
    spectral = spectral_values(inst_count)
    for tile in range(count):
        scale = forward[0:1, tile_of(tile)]
        step = COURANT / (scale * loss + frequency)
        live = (lane + tile * LANES).astype(jnp.float32) < live_count
        step = jnp.where(live, step, 0.0)
        keep = jnp.where(live, 1.0, 0.0) - step * (frequency * spectral[0])
        keep = keep - (3.0 * loss * step * scale) * faces
        partial[tile] = keep * state[0, :, :, tile_of(tile)] + (step * scale) * partial[tile]
        small[WEIGHTS + tile : WEIGHTS + tile + 1, :] = step * scale
        for away in range(1, inst_count):
            value = jnp.where(
                inst + away < inst_count, spectral[-away], spectral[inst_count - away]
            )
            row = WEIGHTS + away * count + tile
            small[row : row + 1, :] = -step * (frequency * value)

    pairs = forward[1:2, :plane].astype(jnp.int32)
    place = pairs - base_owner(pairs, plane) * plane
    place = jnp.where(place < 0, place + n * plane, place).astype(jnp.float32)
    for tile in range(plane // LANES):
        row = WEIGHTS + inst_count * count + tile
        small[row : row + 1, :] = place[:, tile_of(tile)]


def mix(small, face, parts):
    mixed = []
    for g in range(FIELDS):
        total = None
        for field in range(FIELDS):
            row = flux_row(g, face // 2, field)
            term = small[row : row + 1, :] * parts[field]
            total = term if total is None else total + term
        mixed.append((3.0 if face % 2 else -3.0) * total - small[FRAME : FRAME + 1, :] * parts[g])
    return mixed


def lift(cells, tile, face, mixed, scale):
    for g in range(FIELDS):
        change = scale * mixed[g]
        for rows, nodes in face_pieces(face):
            cells[tile, g, nodes, :] = cells[tile, g, nodes, :] - change[rows]


def slide_kernel(plane, partial, small, first, second, joined):
    inst_count = lax.axis_size("inst")
    count = partial.shape[0]
    start, stop = 2 * RIM // LANES, (2 * RIM + plane) // LANES
    for tile in range(count):
        joined[tile, :FIELDS] = partial[tile]
        for away in range(1, inst_count):
            row = WEIGHTS + away * count + tile
            joined[tile, FIELDS, away - 1 : away, :] = small[row : row + 1, :]
    cosine, sine = small[FRAME + 1 : FRAME + 2, :], small[FRAME + 2 : FRAME + 3, :]
    for tile in range(start, stop):
        row = WEIGHTS + inst_count * count + tile - start
        found = choose(
            [
                block[:, tile_of(source)]
                for block in (first, second)
                for source in range(plane // LANES)
            ],
            small[row : row + 1, :].astype(jnp.int32),
        )
        parts = [found[field * FACE : (field + 1) * FACE] for field in range(FIELDS)]
        parts[2], parts[3] = (
            cosine * parts[2] - sine * parts[3],
            sine * parts[2] + cosine * parts[3],
        )
        scale = small[WEIGHTS + tile : WEIGHTS + tile + 1, :]
        lift(joined, tile, 5, mix(small, 5, parts), scale)


def final_kernel(joined, *refs):
    inst_count = lax.axis_size("inst")
    others, (result, buffer, sems) = refs[: inst_count - 1], refs[inst_count - 1 :]
    copies = []
    for tile in range(buffer.shape[0]):
        for field in range(FIELDS):
            total = joined[tile, field]
            for away in range(1, inst_count):
                weight = joined[tile, FIELDS, away - 1 : away, :]
                total = total + weight * others[away - 1][0, field, :, tile_of(tile)]
            buffer[tile, field] = total
        copies.append(
            pltpu.make_async_copy(
                buffer.at[tile], result.at[0, :, :, pl.ds(tile * LANES, LANES)], sems.at[tile]
            )
        )
        copies[-1].start()
    for copy in copies:
        copy.wait()


def shards(
    state, metric, jacobians, dissipation, omega, rotor_angle, counts, neighbours, mortar_pairs
):
    elems = state.shape[-1]
    tiles = elems // LANES
    plane = mortar_pairs.shape[-1]
    n = lax.axis_size("space")
    inst_count = lax.axis_size("inst")
    f32 = jnp.float32
    shape = jax.ShapeDtypeStruct
    sems = pltpu.SemaphoreType.DMA
    scalar = pltpu.VMEM((1, 1), f32)
    params = pltpu.CompilerParams(vmem_limit_bytes=32 * 2**20)
    cost = pl.CostEstimate(flops=2**31, bytes_accessed=2**22, transcendentals=0)

    others = [
        lax.ppermute(state, "inst", [((i + away) % inst_count, i) for i in range(inst_count)])
        for away in range(1, inst_count)
    ]

    rotor, far, near, shift, rows, mixing = pl.pallas_call(
        functools.partial(prep_kernel, plane),
        out_shape=(
            shape((TRACE, plane), f32),
            shape((FIELDS * MODES // 2, 2 * RIM), f32),
            shape((FIELDS * MODES // 2, 2 * RIM), f32),
            shape((1,), jnp.int32),
            shape((8, elems), f32),
            shape((FIELDS, 3, FIELDS), f32),
        ),
        in_specs=[HBM] * 4,
        out_specs=(VMEM, VMEM, VMEM, SMEM, VMEM, VMEM),
        scratch_shapes=[
            pltpu.VMEM((1, plane), jnp.int32),
            pltpu.VMEM((1, elems), f32),
            pltpu.VMEM((FIELDS, MODES, 2 * RIM), f32),
            pltpu.VMEM((plane // LANES, FIELDS, MODES, LANES), f32),
            sems((plane // LANES + 4,)),
        ],
        name="prep",
    )(state, mortar_pairs, metric.reshape(1, elems), jnp.transpose(jacobians, (1, 0, 2)))

    def fetch(away, block):
        if away == 0:
            return block
        return lax.ppermute(block, "space", [((i + away) % n, i) for i in range(n)])

    ends = [(i, (i + 1) % n) for i in range(1, n, 2)]
    middles = [(i, i + 1) for i in range(0, n, 2)]

    def swap(pairs, block):
        return lax.ppermute(block, "space", pairs + [(j, i) for i, j in pairs])

    from_far, from_near = swap(ends, far), swap(middles, near)

    def branch(away, rotor, *operands):
        first = fetch(away, rotor)
        own = pl.pallas_call(
            own_kernel,
            out_shape=(
                shape((tiles, FIELDS, MODES, LANES), f32),
                shape((6, tiles, TRACE, LANES), f32),
                shape((8, elems), f32),
            ),
            in_specs=[VMEM] * 4 + [HBM] * 4,
            out_specs=(VMEM,) * 3,
            scratch_shapes=[
                scalar,
                scalar,
                scalar,
                pltpu.VMEM((1, 1), jnp.int32),
                pltpu.VMEM((FIELDS * MODES, 8 * LANES), jnp.bfloat16),
                pltpu.VMEM((tiles, FIELDS, MODES, LANES), f32),
                pltpu.VMEM((6, tiles, TRACE, LANES), f32),
                sems((4,)),
            ],
            compiler_params=params,
            cost_estimate=cost,
            name="own",
        )(*operands)
        return first, own

    first, (tendency, outer, forward) = lax.switch(
        shift[0],
        [functools.partial(branch, away) for away in range(n)],
        rotor, state, neighbours, rows, mixing, dissipation.reshape(1, 1),
        omega.reshape(1, 1), rotor_angle.reshape(1, 1), counts.reshape(1, 1),
    )

    def finish(second_here, rotor, first, from_far, from_near, *operands):
        second = rotor if second_here else fetch(1, first)
        partial, small = pl.pallas_call(
            functools.partial(halo_kernel, plane),
            out_shape=(
                shape((tiles, FIELDS, MODES, LANES), f32),
                shape((-(-(WEIGHTS + inst_count * tiles + plane // LANES) // 8) * 8, LANES), f32),
            ),
            in_specs=[VMEM] * 8,
            out_specs=(VMEM, VMEM),
            scratch_shapes=[
                pltpu.VMEM((1, FIELDS, MODES, 2 * RIM), f32),
                pltpu.VMEM((6, TRACE, LANES), f32),
            ],
            compiler_params=params,
            cost_estimate=cost,
            name="halo",
        )(*operands, from_far, from_near)
        return pl.pallas_call(
            functools.partial(slide_kernel, plane),
            out_shape=shape((tiles, FIELDS + 1, MODES, LANES), f32),
            in_specs=[VMEM] * 4,
            out_specs=VMEM,
            compiler_params=params,
            name="slide",
        )(partial, small, first, second)

    joined = lax.cond(
        shift[0] == n - 1,
        functools.partial(finish, True),
        functools.partial(finish, False),
        rotor, first, from_far, from_near, state, neighbours, forward, mixing, tendency, outer,
    )

    return pl.pallas_call(
        final_kernel,
        out_shape=shape(state.shape, f32),
        in_specs=[VMEM] * inst_count,
        out_specs=ANY,
        scratch_shapes=[
            pltpu.VMEM((tiles, FIELDS, MODES, LANES), f32),
            sems((tiles,)),
        ],
        compiler_params=params,
        name="final",
    )(joined, *others)


def solution(mesh):
    return jax.shard_map(
        shards,
        mesh=mesh,
        in_specs=(
            P("inst", None, None, "space"),
            P("space"),
            P(),
            P(),
            P(),
            P("inst"),
            P("space"),
            P(None, "space"),
            P("inst", "space"),
        ),
        out_specs=P("inst", None, None, "space"),
        check_vma=False,
    )
```

```python
import functools
import math

import jax
import jax.numpy as jnp
import numpy as np
from jax import lax
from jax.experimental import pallas as pl
from jax.experimental.pallas import tpu as pltpu
from jax.sharding import PartitionSpec as P

RIM = 64
FIELDS = 5
MODES = 64
FACE = 16
TRACE = FIELDS * FACE
LANES = 128
COURANT = 0.5

VMEM = pl.BlockSpec(memory_space=pltpu.VMEM)
SMEM = pl.BlockSpec(memory_space=pltpu.SMEM)
ANY = pl.BlockSpec(memory_space=pl.ANY)
HBM = pl.BlockSpec(memory_space=pltpu.HBM)


def gll_table():
    nodes = np.array([-1.0, -1.0 / math.sqrt(5.0), 1.0 / math.sqrt(5.0), 1.0])
    barycentric = np.array(
        [1.0 / np.prod([nodes[j] - nodes[k] for k in range(4) if k != j]) for j in range(4)]
    )
    derivative = np.zeros((4, 4))
    for i in range(4):
        for j in range(4):
            if i != j:
                derivative[i, j] = barycentric[j] / barycentric[i] / (nodes[i] - nodes[j])
        derivative[i, i] = -np.sum(derivative[i])
    return derivative


def face_nodes(face):
    direction, index = face // 2, 3 * (face % 2)
    nodes = []
    for first in range(4):
        for second in range(4):
            if direction == 0:
                nodes.append(16 * index + 4 * first + second)
            elif direction == 1:
                nodes.append(16 * first + 4 * index + second)
            else:
                nodes.append(16 * first + 4 * second + index)
    return nodes


def spectral_values(count):
    values = {0: (count * count + 2.0) / (12.0 * count)}
    for k in range(1 - count, count):
        if k:
            parity = -1.0 if k % 2 else 1.0
            angle = math.pi * k / count
            values[k] = 0.5 * parity / math.tan(angle) + parity / (
                2.0 * count * math.sin(angle) ** 2
            )
    return values


def split(value):
    high = value.astype(jnp.bfloat16)
    low = (value - high.astype(jnp.float32)).astype(jnp.bfloat16)
    return high, low


def fetch_all(pairs, sems):
    copies = [
        pltpu.make_async_copy(source, target, sems.at[k]) for k, (source, target) in enumerate(pairs)
    ]
    for copy in copies:
        copy.start()
    return copies


def tile_of(number):
    return slice(number * LANES, (number + 1) * LANES)


def face_pieces(face):
    direction, index = face // 2, 3 * (face % 2)
    if direction == 0:
        return [(slice(0, 16), slice(16 * index, 16 * index + 16))]
    if direction == 1:
        return [
            (slice(4 * a, 4 * a + 4), slice(16 * a + 4 * index, 16 * a + 4 * index + 4))
            for a in range(4)
        ]
    return [(slice(0, 16), pl.ds(index, 16, stride=4))]


def load_trace(cells, tile, face, trace):
    for field in range(FIELDS):
        for rows, nodes in face_pieces(face):
            target = slice(field * FACE + rows.start, field * FACE + rows.stop)
            trace[tile, target, :] = cells[tile, field, nodes, :]


def choose(sources, positions):
    shape = sources[0].shape
    lane = jnp.broadcast_to(positions & (LANES - 1), shape)
    tile = jnp.broadcast_to(positions >> 7, shape)
    result = None
    for number, source in enumerate(sources):
        found = jnp.take_along_axis(source, lane, axis=1, mode="promise_in_bounds")
        result = found if result is None else jnp.where(tile == number, found, result)
    return result


def base_owner(pairs, plane):
    owners = (pairs // plane).astype(jnp.float32)
    lowest = jnp.min(owners, axis=1, keepdims=True).astype(jnp.int32)
    highest = jnp.max(owners, axis=1, keepdims=True).astype(jnp.int32)
    return jnp.where(highest - lowest <= 1, lowest, highest)


def prep_kernel(
    plane, state, pairs, metric, jacobians, rotor, far, near, shift, rows, mixing,
    pairs_here, metric_here, rim, tiles, sems,
):
    n = lax.axis_size("space")
    me = lax.axis_index("space")
    count = plane // LANES
    copies = fetch_all(
        [(pairs, pairs_here)]
        + [
            (state.at[0, :, :, pl.ds(2 * RIM + tile * LANES, LANES)], tiles.at[tile])
            for tile in range(count)
        ]
        + [(state.at[0, :, :, pl.ds(0, 2 * RIM)], rim)]
        + [(metric, metric_here), (jacobians, mixing)],
        sems,
    )
    copies[0].wait()
    shift[0] = lax.rem(jnp.max(base_owner(pairs_here[...], plane)) - me + n, n)
    rows[1:2, :plane] = pairs_here[...].astype(jnp.float32)
    for tile in range(count):
        copies[1 + tile].wait()
        for field in range(FIELDS):
            rotor[field * FACE : (field + 1) * FACE, tile_of(tile)] = tiles[
                tile, field, pl.ds(0, FACE, stride=4), :
            ]
    for copy in copies[count + 1 :]:
        copy.wait()
    rows[0:1, :] = metric_here[...]
    odd = lax.rem(me, 2) == 1
    lane = lax.broadcasted_iota(jnp.int32, (MODES // 2, 2 * RIM), 1)
    pieces = [
        rim[field, 32 * half : 32 * half + 32, :] for field in range(FIELDS) for half in range(2)
    ]
    for k in range(FIELDS):
        top, bottom = pieces[k], pieces[k + FIELDS]
        head = jnp.where(lane < RIM, top, pltpu.roll(bottom, RIM, 1))
        tail = jnp.where(lane < RIM, pltpu.roll(top, RIM, 1), bottom)
        far[32 * k : 32 * k + 32, :] = jnp.where(odd, tail, head)
        near[32 * k : 32 * k + 32, :] = jnp.where(odd, head, tail)


def derivative_parts(lane):
    table = -gll_table()
    table[0, 0] -= 3.0
    table[3, 3] += 3.0
    table = table.astype(np.float32).tolist()
    row = lax.broadcasted_iota(jnp.int32, (16, LANES), 0)
    column = jnp.broadcast_to(lane & 15, (16, LANES))
    band = (lane & 63) >> 4

    def entry(i, j):
        value = jnp.zeros(j.shape, jnp.float32)
        for first in range(4):
            for second in range(4):
                value = jnp.where((i == first) & (j == second), table[first][second], value)
        return value

    middle = jnp.where((row & 3) == (column & 3), entry(row >> 2, column >> 2), 0.0)
    last = jnp.where((row >> 2) == (column >> 2), entry(row & 3, column & 3), 0.0)
    parts = [[], [], []]
    for a in range(4):
        along = jnp.zeros(lane.shape, jnp.float32)
        for second in range(4):
            along = jnp.where(band == second, table[a][second], along)
        parts[0].append(jnp.where(row == column, along, 0.0))
        parts[1].append(jnp.where(band == a, middle, 0.0))
        parts[2].append(jnp.where(band == a, last, 0.0))
    return parts


def own_kernel(
    state, neighbours, rows, mixing, dissipation, omega, angle, counts,
    tendency, outer, forward, loss, frequency, turn, live_count, matrix, cells, trace, sems,
):
    copies = fetch_all(
        [(dissipation, loss), (omega, frequency), (angle, turn), (counts, live_count)], sems
    )
    count = cells.shape[0]
    elems = state.shape[-1]

    for tile in range(count):
        cells[tile] = state[0, :, :, tile_of(tile)]
    for face in range(6):
        for tile in range(count):
            load_trace(cells, tile, face ^ 1, trace.at[face])

    for face in range(6):
        for tile in range(count):
            sources = [trace[face, source] for source in range(count)]
            outer[face, tile] = choose(sources, neighbours[face : face + 1, tile_of(tile)] - RIM)

    lane = lax.broadcasted_iota(jnp.int32, (1, LANES), 1)
    parts = derivative_parts(lane)
    layout = [((0, 1), 0, 5), ((2, 3), 1, 6), ((4, 0), 2, 7), ((1, 2), 3, None), ((3, 4), 4, None)]
    for g in range(FIELDS):
        values = [
            [jnp.broadcast_to(mixing[g, d : d + 1, f : f + 1], (1, LANES)) for f in range(FIELDS)]
            for d in range(3)
        ]
        for (left, right), high_place, low_place in layout:
            weight = [jnp.where(lane < MODES, values[d][left], values[d][right]) for d in range(3)]
            for a in range(4):
                block = weight[0] * parts[0][a] + weight[1] * parts[1][a] + weight[2] * parts[2][a]
                high, low = split(block)
                band = slice(g * MODES + 16 * a, g * MODES + 16 * a + 16)
                matrix[band, tile_of(high_place)] = high
                if low_place is not None:
                    if left == FIELDS - 1:
                        low = jnp.where(lane < MODES, low, jnp.zeros_like(low))
                    matrix[band, tile_of(low_place)] = low
    high, low = split(state[0].reshape(FIELDS * MODES, elems))
    stacked = jnp.concatenate([high, low, high, jnp.zeros_like(high[:MODES])], axis=0)
    product = jnp.dot(matrix[...], stacked, preferred_element_type=jnp.float32)
    for tile in range(count):
        tendency[tile] = product[:, tile_of(tile)].reshape(FIELDS, MODES, LANES)

    forward[0:2, :] = rows[0:2, :]
    for copy in copies:
        copy.wait()
    for row, value in enumerate(
        [loss[...], frequency[...], turn[...], live_count[...].astype(jnp.float32)]
    ):
        forward[2 + row : 3 + row, :] = jnp.broadcast_to(value, (1, elems))


def flux_row(g, direction, field):
    return (direction * FIELDS + g) * FIELDS + field


FRAME = 3 * FIELDS * FIELDS
WEIGHTS = FRAME + 5


def halo_kernel(
    plane, state, neighbours, forward, mixing, tendency, outer, from_far, from_near,
    partial, small, rim, trace,
):
    n = lax.axis_size("space")
    inst_count = lax.axis_size("inst")
    inst = lax.axis_index("inst")
    count = partial.shape[0]
    elems = state.shape[-1]
    for g in range(FIELDS):
        for d in range(3):
            for field in range(FIELDS):
                row = flux_row(g, d, field)
                small[row : row + 1, :] = jnp.broadcast_to(
                    mixing[g, d : d + 1, field : field + 1], (1, LANES)
                )
    loss, frequency, turn, live_count = [
        forward[2 + row : 3 + row, :LANES] for row in range(4)
    ]
    small[FRAME : FRAME + 1, :] = 3.0 * loss
    small[FRAME + 1 : FRAME + 2, :] = jnp.cos(turn)
    small[FRAME + 2 : FRAME + 3, :] = jnp.sin(turn)

    odd = lax.rem(lax.axis_index("space"), 2) == 1
    half_lane = lax.broadcasted_iota(jnp.int32, (MODES // 2, 2 * RIM), 1)
    for k in range(2 * FIELDS):
        field, half = k // 2, k % 2
        piece = pl.ds(32 * (k % FIELDS), 32)
        left = jnp.where(odd, from_near[piece, :], from_far[piece, :])
        right = jnp.where(odd, from_far[piece, :], from_near[piece, :])
        if k < FIELDS:
            right = pltpu.roll(right, RIM, 1)
        else:
            left = pltpu.roll(left, RIM, 1)
        rim[0, field, 32 * half : 32 * half + 32, :] = jnp.where(half_lane < RIM, left, right)
    for face in range(6):
        load_trace(rim, 0, face ^ 1, trace.at[pl.ds(face, 1)])
    partial[...] = tendency[...]
    lane = lax.broadcasted_iota(jnp.int32, (1, LANES), 1)
    for face in range(6):
        for tile in range(count):
            number = neighbours[face : face + 1, tile_of(tile)]
            previous = number < RIM
            remote = previous | (number >= RIM + elems)
            found = choose([trace[face]], jnp.where(previous, number, number - elems))
            found = jnp.where(remote, found, outer[face, tile])
            if face == 5:
                column = lane + tile * LANES
                sliding = (column >= 2 * RIM) & (column < 2 * RIM + plane)
                found = jnp.where(sliding, 0.0, found)
            parts = [found[field * FACE : (field + 1) * FACE] for field in range(FIELDS)]
            lift(partial, tile, face, mix(small, face, parts), 1.0)

    node = lax.broadcasted_iota(jnp.int32, (MODES, LANES), 0)
    faces = jnp.zeros((MODES, LANES), jnp.float32)
    for index in (node >> 4, (node >> 2) & 3, node & 3):
        faces = faces + jnp.where((index == 0) | (index == 3), 1.0, 0.0)
    spectral = spectral_values(inst_count)
    for tile in range(count):
        scale = forward[0:1, tile_of(tile)]
        step = COURANT / (scale * loss + frequency)
        live = (lane + tile * LANES).astype(jnp.float32) < live_count
        step = jnp.where(live, step, 0.0)
        keep = jnp.where(live, 1.0, 0.0) - step * (frequency * spectral[0])
        keep = keep - (3.0 * loss * step * scale) * faces
        partial[tile] = keep * state[0, :, :, tile_of(tile)] + (step * scale) * partial[tile]
        small[WEIGHTS + tile : WEIGHTS + tile + 1, :] = step * scale
        for away in range(1, inst_count):
            value = jnp.where(
                inst + away < inst_count, spectral[-away], spectral[inst_count - away]
            )
            row = WEIGHTS + away * count + tile
            small[row : row + 1, :] = -step * (frequency * value)

    pairs = forward[1:2, :plane].astype(jnp.int32)
    place = pairs - base_owner(pairs, plane) * plane
    place = jnp.where(place < 0, place + n * plane, place).astype(jnp.float32)
    for tile in range(plane // LANES):
        row = WEIGHTS + inst_count * count + tile
        small[row : row + 1, :] = place[:, tile_of(tile)]


def mix(small, face, parts):
    mixed = []
    for g in range(FIELDS):
        total = None
        for field in range(FIELDS):
            row = flux_row(g, face // 2, field)
            term = small[row : row + 1, :] * parts[field]
            total = term if total is None else total + term
        mixed.append((3.0 if face % 2 else -3.0) * total - small[FRAME : FRAME + 1, :] * parts[g])
    return mixed


def lift(cells, tile, face, mixed, scale):
    for g in range(FIELDS):
        change = scale * mixed[g]
        for rows, nodes in face_pieces(face):
            cells[tile, g, nodes, :] = cells[tile, g, nodes, :] - change[rows]


def final_kernel(plane, partial, small, first, second, last, *refs):
    inst_count = lax.axis_size("inst")
    others, (result, buffer, blocks, sems, block_sems) = refs[: inst_count - 1], refs[inst_count - 1 :]
    count = buffer.shape[0]
    start, stop = 2 * RIM // LANES, (2 * RIM + plane) // LANES
    is_last = lax.axis_index("space") == lax.axis_size("space") - 1

    def block_copy(number, source):
        return pltpu.make_async_copy(source, blocks.at[number], block_sems.at[number])

    block_copy(0, first).start()

    @pl.when(is_last)
    def _():
        block_copy(1, last).start()

    @pl.when(jnp.logical_not(is_last))
    def _():
        block_copy(1, second).start()

    def send(tile):
        return pltpu.make_async_copy(
            buffer.at[tile], result.at[0, :, :, pl.ds(tile * LANES, LANES)], sems.at[tile]
        )

    for tile in [*range(start), *range(stop, count), *range(start, stop)]:
        for field in range(FIELDS):
            total = partial[tile, field]
            for away in range(1, inst_count):
                row = WEIGHTS + away * count + tile
                other = others[away - 1][0, field, :, tile_of(tile)]
                total = total + small[row : row + 1, :] * other
            buffer[tile, field] = total
        if not start <= tile < stop:
            send(tile).start()
    block_copy(0, first).wait()
    block_copy(1, second).wait()
    cosine, sine = small[FRAME + 1 : FRAME + 2, :], small[FRAME + 2 : FRAME + 3, :]
    for tile in range(start, stop):
        row = WEIGHTS + inst_count * count + tile - start
        found = choose(
            [
                blocks[number, :, tile_of(source)]
                for number in range(2)
                for source in range(plane // LANES)
            ],
            small[row : row + 1, :].astype(jnp.int32),
        )
        parts = [found[field * FACE : (field + 1) * FACE] for field in range(FIELDS)]
        parts[2], parts[3] = (
            cosine * parts[2] - sine * parts[3],
            sine * parts[2] + cosine * parts[3],
        )
        scale = small[WEIGHTS + tile : WEIGHTS + tile + 1, :]
        lift(buffer, tile, 5, mix(small, 5, parts), scale)
        send(tile).start()
    for tile in range(count):
        send(tile).wait()


def shards(
    state, metric, jacobians, dissipation, omega, rotor_angle, counts, neighbours, mortar_pairs
):
    elems = state.shape[-1]
    tiles = elems // LANES
    plane = mortar_pairs.shape[-1]
    n = lax.axis_size("space")
    inst_count = lax.axis_size("inst")
    f32 = jnp.float32
    shape = jax.ShapeDtypeStruct
    sems = pltpu.SemaphoreType.DMA
    scalar = pltpu.VMEM((1, 1), f32)
    params = pltpu.CompilerParams(vmem_limit_bytes=32 * 2**20)
    cost = pl.CostEstimate(flops=2**31, bytes_accessed=2**22, transcendentals=0)

    others = [
        lax.ppermute(state, "inst", [((i + away) % inst_count, i) for i in range(inst_count)])
        for away in range(1, inst_count)
    ]

    rotor, far, near, shift, rows, mixing = pl.pallas_call(
        functools.partial(prep_kernel, plane),
        out_shape=(
            shape((TRACE, plane), f32),
            shape((FIELDS * MODES // 2, 2 * RIM), f32),
            shape((FIELDS * MODES // 2, 2 * RIM), f32),
            shape((1,), jnp.int32),
            shape((8, elems), f32),
            shape((FIELDS, 3, FIELDS), f32),
        ),
        in_specs=[HBM] * 4,
        out_specs=(VMEM, VMEM, VMEM, SMEM, VMEM, VMEM),
        scratch_shapes=[
            pltpu.VMEM((1, plane), jnp.int32),
            pltpu.VMEM((1, elems), f32),
            pltpu.VMEM((FIELDS, MODES, 2 * RIM), f32),
            pltpu.VMEM((plane // LANES, FIELDS, MODES, LANES), f32),
            sems((plane // LANES + 4,)),
        ],
        name="prep",
    )(state, mortar_pairs, metric.reshape(1, elems), jnp.transpose(jacobians, (1, 0, 2)))

    def fetch(away, block):
        if away == 0:
            return block
        return lax.ppermute(block, "space", [((i + away) % n, i) for i in range(n)])

    ends = [(i, (i + 1) % n) for i in range(1, n, 2)]
    middles = [(i, i + 1) for i in range(0, n, 2)]

    def swap(pairs, block):
        return lax.ppermute(block, "space", pairs + [(j, i) for i, j in pairs])

    def branch(away, rotor, far, near, *operands):
        first = fetch(away, rotor)
        last = rotor
        if away != n - 1:
            kept = [(i, i) for i in range(n - 1) if i != away]
            last = lax.ppermute(rotor, "space", kept + [(away, n - 1), (n - 1, away)])
        from_far, from_near = swap(ends, far), swap(middles, near)
        own = pl.pallas_call(
            own_kernel,
            out_shape=(
                shape((tiles, FIELDS, MODES, LANES), f32),
                shape((6, tiles, TRACE, LANES), f32),
                shape((8, elems), f32),
            ),
            in_specs=[VMEM] * 4 + [HBM] * 4,
            out_specs=(VMEM,) * 3,
            scratch_shapes=[
                scalar,
                scalar,
                scalar,
                pltpu.VMEM((1, 1), jnp.int32),
                pltpu.VMEM((FIELDS * MODES, 8 * LANES), jnp.bfloat16),
                pltpu.VMEM((tiles, FIELDS, MODES, LANES), f32),
                pltpu.VMEM((6, tiles, TRACE, LANES), f32),
                sems((4,)),
            ],
            compiler_params=params,
            cost_estimate=cost,
            name="own",
        )(*operands)
        return first, last, from_far, from_near, own

    first, last, from_far, from_near, (tendency, outer, forward) = lax.switch(
        shift[0],
        [functools.partial(branch, away) for away in range(n)],
        rotor, far, near, state, neighbours, rows, mixing, dissipation.reshape(1, 1),
        omega.reshape(1, 1), rotor_angle.reshape(1, 1), counts.reshape(1, 1),
    )
    second = lax.ppermute(first, "space", [(i + 1, i) for i in range(n - 1)])

    partial, small = pl.pallas_call(
        functools.partial(halo_kernel, plane),
        out_shape=(
            shape((tiles, FIELDS, MODES, LANES), f32),
            shape((-(-(WEIGHTS + inst_count * tiles + plane // LANES) // 8) * 8, LANES), f32),
        ),
        in_specs=[VMEM] * 8,
        out_specs=(VMEM, VMEM),
        scratch_shapes=[
            pltpu.VMEM((1, FIELDS, MODES, 2 * RIM), f32),
            pltpu.VMEM((6, TRACE, LANES), f32),
        ],
        compiler_params=params,
        cost_estimate=cost,
        name="halo",
    )(state, neighbours, forward, mixing, tendency, outer, from_far, from_near)

    return pl.pallas_call(
        functools.partial(final_kernel, plane),
        out_shape=shape(state.shape, f32),
        in_specs=[VMEM] * 2 + [ANY] * 3 + [VMEM] * (inst_count - 1),
        out_specs=ANY,
        scratch_shapes=[
            pltpu.VMEM((tiles, FIELDS, MODES, LANES), f32),
            pltpu.VMEM((2, TRACE, plane), f32),
            sems((tiles,)),
            sems((2,)),
        ],
        compiler_params=params,
        name="final",
    )(partial, small, first, second, last, *others)


def solution(mesh):
    return jax.shard_map(
        shards,
        mesh=mesh,
        in_specs=(
            P("inst", None, None, "space"),
            P("space"),
            P(),
            P(),
            P(),
            P("inst"),
            P("space"),
            P(None, "space"),
            P("inst", "space"),
        ),
        out_specs=P("inst", None, None, "space"),
        check_vma=False,
    )
```

```python
import functools
import math

import jax
import jax.numpy as jnp
import numpy as np
from jax import lax
from jax.experimental import pallas as pl
from jax.experimental.pallas import tpu as pltpu
from jax.sharding import PartitionSpec as P

RIM = 64
FIELDS = 5
MODES = 64
FACE = 16
TRACE = FIELDS * FACE
LANES = 128
COURANT = 0.5

VMEM = pl.BlockSpec(memory_space=pltpu.VMEM)
SMEM = pl.BlockSpec(memory_space=pltpu.SMEM)
ANY = pl.BlockSpec(memory_space=pl.ANY)
HBM = pl.BlockSpec(memory_space=pltpu.HBM)


def gll_table():
    nodes = np.array([-1.0, -1.0 / math.sqrt(5.0), 1.0 / math.sqrt(5.0), 1.0])
    barycentric = np.array(
        [1.0 / np.prod([nodes[j] - nodes[k] for k in range(4) if k != j]) for j in range(4)]
    )
    derivative = np.zeros((4, 4))
    for i in range(4):
        for j in range(4):
            if i != j:
                derivative[i, j] = barycentric[j] / barycentric[i] / (nodes[i] - nodes[j])
        derivative[i, i] = -np.sum(derivative[i])
    return derivative


def face_nodes(face):
    direction, index = face // 2, 3 * (face % 2)
    nodes = []
    for first in range(4):
        for second in range(4):
            if direction == 0:
                nodes.append(16 * index + 4 * first + second)
            elif direction == 1:
                nodes.append(16 * first + 4 * index + second)
            else:
                nodes.append(16 * first + 4 * second + index)
    return nodes


def spectral_values(count):
    values = {0: (count * count + 2.0) / (12.0 * count)}
    for k in range(1 - count, count):
        if k:
            parity = -1.0 if k % 2 else 1.0
            angle = math.pi * k / count
            values[k] = 0.5 * parity / math.tan(angle) + parity / (
                2.0 * count * math.sin(angle) ** 2
            )
    return values


def split(value):
    high = value.astype(jnp.bfloat16)
    low = (value - high.astype(jnp.float32)).astype(jnp.bfloat16)
    return high, low


def fetch_all(pairs, sems):
    copies = [
        pltpu.make_async_copy(source, target, sems.at[k]) for k, (source, target) in enumerate(pairs)
    ]
    for copy in copies:
        copy.start()
    return copies


def tile_of(number):
    return slice(number * LANES, (number + 1) * LANES)


def face_pieces(face):
    direction, index = face // 2, 3 * (face % 2)
    if direction == 0:
        return [(slice(0, 16), slice(16 * index, 16 * index + 16))]
    if direction == 1:
        return [
            (slice(4 * a, 4 * a + 4), slice(16 * a + 4 * index, 16 * a + 4 * index + 4))
            for a in range(4)
        ]
    return [(slice(0, 16), pl.ds(index, 16, stride=4))]


def load_trace(cells, tile, face, trace):
    for field in range(FIELDS):
        for rows, nodes in face_pieces(face):
            target = slice(field * FACE + rows.start, field * FACE + rows.stop)
            trace[tile, target, :] = cells[tile, field, nodes, :]


def choose(sources, positions):
    shape = sources[0].shape
    lane = jnp.broadcast_to(positions & (LANES - 1), shape)
    tile = jnp.broadcast_to(positions >> 7, shape)
    result = None
    for number, source in enumerate(sources):
        found = jnp.take_along_axis(source, lane, axis=1, mode="promise_in_bounds")
        result = found if result is None else jnp.where(tile == number, found, result)
    return result


def base_owner(pairs, plane):
    owners = (pairs // plane).astype(jnp.float32)
    lowest = jnp.min(owners, axis=1, keepdims=True).astype(jnp.int32)
    highest = jnp.max(owners, axis=1, keepdims=True).astype(jnp.int32)
    return jnp.where(highest - lowest <= 1, lowest, highest)


def prep_kernel(
    plane, state, pairs, metric, jacobians, rotor, far, near, shift, rows, mixing,
    pairs_here, metric_here, rim, tiles, sems,
):
    n = lax.axis_size("space")
    me = lax.axis_index("space")
    count = plane // LANES
    copies = fetch_all(
        [(pairs, pairs_here)]
        + [
            (state.at[0, :, :, pl.ds(2 * RIM + tile * LANES, LANES)], tiles.at[tile])
            for tile in range(count)
        ]
        + [(state.at[0, :, :, pl.ds(0, 2 * RIM)], rim)]
        + [(metric, metric_here), (jacobians, mixing)],
        sems,
    )
    copies[0].wait()
    shift[0] = lax.rem(jnp.max(base_owner(pairs_here[...], plane)) - me + n, n)
    rows[1:2, :plane] = pairs_here[...].astype(jnp.float32)
    for tile in range(count):
        copies[1 + tile].wait()
        for field in range(FIELDS):
            rotor[field * FACE : (field + 1) * FACE, tile_of(tile)] = tiles[
                tile, field, pl.ds(0, FACE, stride=4), :
            ]
    for copy in copies[count + 1 :]:
        copy.wait()
    rows[0:1, :] = metric_here[...]
    odd = lax.rem(me, 2) == 1
    lane = lax.broadcasted_iota(jnp.int32, (MODES // 2, 2 * RIM), 1)
    pieces = [
        rim[field, 32 * half : 32 * half + 32, :] for field in range(FIELDS) for half in range(2)
    ]
    for k in range(FIELDS):
        top, bottom = pieces[k], pieces[k + FIELDS]
        head = jnp.where(lane < RIM, top, pltpu.roll(bottom, RIM, 1))
        tail = jnp.where(lane < RIM, pltpu.roll(top, RIM, 1), bottom)
        far[32 * k : 32 * k + 32, :] = jnp.where(odd, tail, head)
        near[32 * k : 32 * k + 32, :] = jnp.where(odd, head, tail)


def derivative_parts(lane):
    table = -gll_table()
    table[0, 0] -= 3.0
    table[3, 3] += 3.0
    table = table.astype(np.float32).tolist()
    row = lax.broadcasted_iota(jnp.int32, (16, LANES), 0)
    column = jnp.broadcast_to(lane & 15, (16, LANES))
    band = (lane & 63) >> 4

    def entry(i, j):
        value = jnp.zeros(j.shape, jnp.float32)
        for first in range(4):
            for second in range(4):
                value = jnp.where((i == first) & (j == second), table[first][second], value)
        return value

    middle = jnp.where((row & 3) == (column & 3), entry(row >> 2, column >> 2), 0.0)
    last = jnp.where((row >> 2) == (column >> 2), entry(row & 3, column & 3), 0.0)
    parts = [[], [], []]
    for a in range(4):
        along = jnp.zeros(lane.shape, jnp.float32)
        for second in range(4):
            along = jnp.where(band == second, table[a][second], along)
        parts[0].append(jnp.where(row == column, along, 0.0))
        parts[1].append(jnp.where(band == a, middle, 0.0))
        parts[2].append(jnp.where(band == a, last, 0.0))
    return parts


def own_kernel(
    state, neighbours, rows, mixing, dissipation, omega, angle, counts,
    tendency, outer, forward, loss, frequency, turn, live_count, matrix, cells, trace, sems,
):
    copies = fetch_all(
        [(dissipation, loss), (omega, frequency), (angle, turn), (counts, live_count)], sems
    )
    count = cells.shape[0]
    elems = state.shape[-1]

    for tile in range(count):
        cells[tile] = state[0, :, :, tile_of(tile)]
    for face in range(6):
        for tile in range(count):
            load_trace(cells, tile, face ^ 1, trace.at[face])

    for face in range(6):
        for tile in range(count):
            sources = [trace[face, source] for source in range(count)]
            outer[face, tile] = choose(sources, neighbours[face : face + 1, tile_of(tile)] - RIM)

    lane = lax.broadcasted_iota(jnp.int32, (1, LANES), 1)
    parts = derivative_parts(lane)
    layout = [((0, 1), 0, 5), ((2, 3), 1, 6), ((4, 0), 2, 7), ((1, 2), 3, None), ((3, 4), 4, None)]
    for g in range(FIELDS):
        values = [
            [jnp.broadcast_to(mixing[g, d : d + 1, f : f + 1], (1, LANES)) for f in range(FIELDS)]
            for d in range(3)
        ]
        for (left, right), high_place, low_place in layout:
            weight = [jnp.where(lane < MODES, values[d][left], values[d][right]) for d in range(3)]
            for a in range(4):
                block = weight[0] * parts[0][a] + weight[1] * parts[1][a] + weight[2] * parts[2][a]
                high, low = split(block)
                band = slice(g * MODES + 16 * a, g * MODES + 16 * a + 16)
                matrix[band, tile_of(high_place)] = high
                if low_place is not None:
                    if left == FIELDS - 1:
                        low = jnp.where(lane < MODES, low, jnp.zeros_like(low))
                    matrix[band, tile_of(low_place)] = low
    high, low = split(state[0].reshape(FIELDS * MODES, elems))
    stacked = jnp.concatenate([high, low, high, jnp.zeros_like(high[:MODES])], axis=0)
    product = jnp.dot(matrix[...], stacked, preferred_element_type=jnp.float32)
    for tile in range(count):
        tendency[tile] = product[:, tile_of(tile)].reshape(FIELDS, MODES, LANES)

    forward[0:2, :] = rows[0:2, :]
    for copy in copies:
        copy.wait()
    for row, value in enumerate(
        [loss[...], frequency[...], turn[...], live_count[...].astype(jnp.float32)]
    ):
        forward[2 + row : 3 + row, :] = jnp.broadcast_to(value, (1, elems))


def flux_row(g, direction, field):
    return (direction * FIELDS + g) * FIELDS + field


FRAME = 3 * FIELDS * FIELDS
WEIGHTS = FRAME + 5


def halo_kernel(
    plane, state, neighbours, forward, mixing, tendency, outer, from_far, from_near,
    partial, small, rim, trace,
):
    n = lax.axis_size("space")
    inst_count = lax.axis_size("inst")
    inst = lax.axis_index("inst")
    count = partial.shape[0]
    elems = state.shape[-1]
    for g in range(FIELDS):
        for d in range(3):
            for field in range(FIELDS):
                row = flux_row(g, d, field)
                small[row : row + 1, :] = jnp.broadcast_to(
                    mixing[g, d : d + 1, field : field + 1], (1, LANES)
                )
    loss, frequency, turn, live_count = [
        forward[2 + row : 3 + row, :LANES] for row in range(4)
    ]
    small[FRAME : FRAME + 1, :] = 3.0 * loss
    small[FRAME + 1 : FRAME + 2, :] = jnp.cos(turn)
    small[FRAME + 2 : FRAME + 3, :] = jnp.sin(turn)

    odd = lax.rem(lax.axis_index("space"), 2) == 1
    half_lane = lax.broadcasted_iota(jnp.int32, (MODES // 2, 2 * RIM), 1)
    for k in range(2 * FIELDS):
        field, half = k // 2, k % 2
        piece = pl.ds(32 * (k % FIELDS), 32)
        left = jnp.where(odd, from_near[piece, :], from_far[piece, :])
        right = jnp.where(odd, from_far[piece, :], from_near[piece, :])
        if k < FIELDS:
            right = pltpu.roll(right, RIM, 1)
        else:
            left = pltpu.roll(left, RIM, 1)
        rim[0, field, 32 * half : 32 * half + 32, :] = jnp.where(half_lane < RIM, left, right)
    for face in range(6):
        load_trace(rim, 0, face ^ 1, trace.at[pl.ds(face, 1)])
    partial[...] = tendency[...]
    lane = lax.broadcasted_iota(jnp.int32, (1, LANES), 1)
    for face in range(6):
        for tile in range(count):
            number = neighbours[face : face + 1, tile_of(tile)]
            previous = number < RIM
            remote = previous | (number >= RIM + elems)
            found = choose([trace[face]], jnp.where(previous, number, number - elems))
            found = jnp.where(remote, found, outer[face, tile])
            if face == 5:
                column = lane + tile * LANES
                sliding = (column >= 2 * RIM) & (column < 2 * RIM + plane)
                found = jnp.where(sliding, 0.0, found)
            parts = [found[field * FACE : (field + 1) * FACE] for field in range(FIELDS)]
            lift(partial, tile, face, mix(small, face, parts), 1.0)

    node = lax.broadcasted_iota(jnp.int32, (MODES, LANES), 0)
    faces = jnp.zeros((MODES, LANES), jnp.float32)
    for index in (node >> 4, (node >> 2) & 3, node & 3):
        faces = faces + jnp.where((index == 0) | (index == 3), 1.0, 0.0)
    spectral = spectral_values(inst_count)
    for tile in range(count):
        scale = forward[0:1, tile_of(tile)]
        step = COURANT / (scale * loss + frequency)
        live = (lane + tile * LANES).astype(jnp.float32) < live_count
        step = jnp.where(live, step, 0.0)
        keep = jnp.where(live, 1.0, 0.0) - step * (frequency * spectral[0])
        keep = keep - (3.0 * loss * step * scale) * faces
        partial[tile] = keep * state[0, :, :, tile_of(tile)] + (step * scale) * partial[tile]
        small[WEIGHTS + tile : WEIGHTS + tile + 1, :] = step * scale
        for away in range(1, inst_count):
            value = jnp.where(
                inst + away < inst_count, spectral[-away], spectral[inst_count - away]
            )
            row = WEIGHTS + away * count + tile
            small[row : row + 1, :] = -step * (frequency * value)

    pairs = forward[1:2, :plane].astype(jnp.int32)
    place = pairs - base_owner(pairs, plane) * plane
    place = jnp.where(place < 0, place + n * plane, place).astype(jnp.float32)
    for tile in range(plane // LANES):
        row = WEIGHTS + inst_count * count + tile
        small[row : row + 1, :] = place[:, tile_of(tile)]


def mix(small, face, parts):
    mixed = []
    for g in range(FIELDS):
        total = None
        for field in range(FIELDS):
            row = flux_row(g, face // 2, field)
            term = small[row : row + 1, :] * parts[field]
            total = term if total is None else total + term
        mixed.append((3.0 if face % 2 else -3.0) * total - small[FRAME : FRAME + 1, :] * parts[g])
    return mixed


def lift(cells, tile, face, mixed, scale):
    for g in range(FIELDS):
        change = scale * mixed[g]
        for rows, nodes in face_pieces(face):
            cells[tile, g, nodes, :] = cells[tile, g, nodes, :] - change[rows]


def final_kernel(plane, partial, small, first, second, *refs):
    inst_count = lax.axis_size("inst")
    others, (result, buffer, sems) = refs[: inst_count - 1], refs[inst_count - 1 :]
    count = buffer.shape[0]
    start, stop = 2 * RIM // LANES, (2 * RIM + plane) // LANES
    copies = []
    for tile in [*range(start), *range(stop, count), *range(start, stop)]:
        for field in range(FIELDS):
            total = partial[tile, field]
            for away in range(1, inst_count):
                row = WEIGHTS + away * count + tile
                other = others[away - 1][0, field, :, tile_of(tile)]
                total = total + small[row : row + 1, :] * other
            buffer[tile, field] = total
        if start <= tile < stop:
            row = WEIGHTS + inst_count * count + tile - start
            found = choose(
                [
                    block[:, tile_of(source)]
                    for block in (first, second)
                    for source in range(plane // LANES)
                ],
                small[row : row + 1, :].astype(jnp.int32),
            )
            parts = [found[field * FACE : (field + 1) * FACE] for field in range(FIELDS)]
            cosine, sine = small[FRAME + 1 : FRAME + 2, :], small[FRAME + 2 : FRAME + 3, :]
            parts[2], parts[3] = (
                cosine * parts[2] - sine * parts[3],
                sine * parts[2] + cosine * parts[3],
            )
            scale = small[WEIGHTS + tile : WEIGHTS + tile + 1, :]
            lift(buffer, tile, 5, mix(small, 5, parts), scale)
        copies.append(
            pltpu.make_async_copy(
                buffer.at[tile], result.at[0, :, :, pl.ds(tile * LANES, LANES)], sems.at[tile]
            )
        )
        copies[-1].start()
    for copy in copies:
        copy.wait()


def shards(
    state, metric, jacobians, dissipation, omega, rotor_angle, counts, neighbours, mortar_pairs
):
    elems = state.shape[-1]
    tiles = elems // LANES
    plane = mortar_pairs.shape[-1]
    n = lax.axis_size("space")
    inst_count = lax.axis_size("inst")
    f32 = jnp.float32
    shape = jax.ShapeDtypeStruct
    sems = pltpu.SemaphoreType.DMA
    scalar = pltpu.VMEM((1, 1), f32)
    params = pltpu.CompilerParams(vmem_limit_bytes=32 * 2**20)
    cost = pl.CostEstimate(flops=2**31, bytes_accessed=2**22, transcendentals=0)

    others = [
        lax.ppermute(state, "inst", [((i + away) % inst_count, i) for i in range(inst_count)])
        for away in range(1, inst_count)
    ]

    rotor, far, near, shift, rows, mixing = pl.pallas_call(
        functools.partial(prep_kernel, plane),
        out_shape=(
            shape((TRACE, plane), f32),
            shape((FIELDS * MODES // 2, 2 * RIM), f32),
            shape((FIELDS * MODES // 2, 2 * RIM), f32),
            shape((1,), jnp.int32),
            shape((8, elems), f32),
            shape((FIELDS, 3, FIELDS), f32),
        ),
        in_specs=[HBM] * 4,
        out_specs=(VMEM, VMEM, VMEM, SMEM, VMEM, VMEM),
        scratch_shapes=[
            pltpu.VMEM((1, plane), jnp.int32),
            pltpu.VMEM((1, elems), f32),
            pltpu.VMEM((FIELDS, MODES, 2 * RIM), f32),
            pltpu.VMEM((plane // LANES, FIELDS, MODES, LANES), f32),
            sems((plane // LANES + 4,)),
        ],
        name="prep",
    )(state, mortar_pairs, metric.reshape(1, elems), jnp.transpose(jacobians, (1, 0, 2)))

    def fetch(away, block):
        if away == 0:
            return block
        return lax.ppermute(block, "space", [((i + away) % n, i) for i in range(n)])

    ends = [(i, (i + 1) % n) for i in range(1, n, 2)]
    middles = [(i, i + 1) for i in range(0, n, 2)]

    def swap(pairs, block):
        return lax.ppermute(block, "space", pairs + [(j, i) for i, j in pairs])

    def branch(away, rotor, far, near, *operands):
        first = fetch(away, rotor)
        from_far, from_near = swap(ends, far), swap(middles, near)
        own = pl.pallas_call(
            own_kernel,
            out_shape=(
                shape((tiles, FIELDS, MODES, LANES), f32),
                shape((6, tiles, TRACE, LANES), f32),
                shape((8, elems), f32),
            ),
            in_specs=[VMEM] * 4 + [HBM] * 4,
            out_specs=(VMEM,) * 3,
            scratch_shapes=[
                scalar,
                scalar,
                scalar,
                pltpu.VMEM((1, 1), jnp.int32),
                pltpu.VMEM((FIELDS * MODES, 8 * LANES), jnp.bfloat16),
                pltpu.VMEM((tiles, FIELDS, MODES, LANES), f32),
                pltpu.VMEM((6, tiles, TRACE, LANES), f32),
                sems((4,)),
            ],
            compiler_params=params,
            cost_estimate=cost,
            name="own",
        )(*operands)
        return first, from_far, from_near, own

    first, from_far, from_near, (tendency, outer, forward) = lax.switch(
        shift[0],
        [functools.partial(branch, away) for away in range(n)],
        rotor, far, near, state, neighbours, rows, mixing, dissipation.reshape(1, 1),
        omega.reshape(1, 1), rotor_angle.reshape(1, 1), counts.reshape(1, 1),
    )
    second = fetch(1, first)

    partial, small = pl.pallas_call(
        functools.partial(halo_kernel, plane),
        out_shape=(
            shape((tiles, FIELDS, MODES, LANES), f32),
            shape((-(-(WEIGHTS + inst_count * tiles + plane // LANES) // 8) * 8, LANES), f32),
        ),
        in_specs=[VMEM] * 8,
        out_specs=(VMEM, VMEM),
        scratch_shapes=[
            pltpu.VMEM((1, FIELDS, MODES, 2 * RIM), f32),
            pltpu.VMEM((6, TRACE, LANES), f32),
        ],
        compiler_params=params,
        cost_estimate=cost,
        name="halo",
    )(state, neighbours, forward, mixing, tendency, outer, from_far, from_near)

    return pl.pallas_call(
        functools.partial(final_kernel, plane),
        out_shape=shape(state.shape, f32),
        in_specs=[VMEM] * (3 + inst_count),
        out_specs=ANY,
        scratch_shapes=[
            pltpu.VMEM((tiles, FIELDS, MODES, LANES), f32),
            sems((tiles,)),
        ],
        compiler_params=params,
        name="final",
    )(partial, small, first, second, *others)


def solution(mesh):
    return jax.shard_map(
        shards,
        mesh=mesh,
        in_specs=(
            P("inst", None, None, "space"),
            P("space"),
            P(),
            P(),
            P(),
            P("inst"),
            P("space"),
            P(None, "space"),
            P("inst", "space"),
        ),
        out_specs=P("inst", None, None, "space"),
        check_vma=False,
    )
```

```python
import functools
import math

import jax
import jax.numpy as jnp
import numpy as np
from jax import lax
from jax.experimental import pallas as pl
from jax.experimental.pallas import tpu as pltpu
from jax.sharding import PartitionSpec as P

RIM = 64
FIELDS = 5
MODES = 64
FACE = 16
TRACE = FIELDS * FACE
LANES = 128
COURANT = 0.5

VMEM = pl.BlockSpec(memory_space=pltpu.VMEM)
SMEM = pl.BlockSpec(memory_space=pltpu.SMEM)
ANY = pl.BlockSpec(memory_space=pl.ANY)
HBM = pl.BlockSpec(memory_space=pltpu.HBM)


def gll_table():
    nodes = np.array([-1.0, -1.0 / math.sqrt(5.0), 1.0 / math.sqrt(5.0), 1.0])
    barycentric = np.array(
        [1.0 / np.prod([nodes[j] - nodes[k] for k in range(4) if k != j]) for j in range(4)]
    )
    derivative = np.zeros((4, 4))
    for i in range(4):
        for j in range(4):
            if i != j:
                derivative[i, j] = barycentric[j] / barycentric[i] / (nodes[i] - nodes[j])
        derivative[i, i] = -np.sum(derivative[i])
    return derivative


def face_nodes(face):
    direction, index = face // 2, 3 * (face % 2)
    nodes = []
    for first in range(4):
        for second in range(4):
            if direction == 0:
                nodes.append(16 * index + 4 * first + second)
            elif direction == 1:
                nodes.append(16 * first + 4 * index + second)
            else:
                nodes.append(16 * first + 4 * second + index)
    return nodes


def spectral_values(count):
    values = {0: (count * count + 2.0) / (12.0 * count)}
    for k in range(1 - count, count):
        if k:
            parity = -1.0 if k % 2 else 1.0
            angle = math.pi * k / count
            values[k] = 0.5 * parity / math.tan(angle) + parity / (
                2.0 * count * math.sin(angle) ** 2
            )
    return values


def split(value):
    high = value.astype(jnp.bfloat16)
    low = (value - high.astype(jnp.float32)).astype(jnp.bfloat16)
    return high, low


def fetch_all(pairs, sems):
    copies = [
        pltpu.make_async_copy(source, target, sems.at[k]) for k, (source, target) in enumerate(pairs)
    ]
    for copy in copies:
        copy.start()
    return copies


def tile_of(number):
    return slice(number * LANES, (number + 1) * LANES)


def face_pieces(face):
    direction, index = face // 2, 3 * (face % 2)
    if direction == 0:
        return [(slice(0, 16), slice(16 * index, 16 * index + 16))]
    if direction == 1:
        return [
            (slice(4 * a, 4 * a + 4), slice(16 * a + 4 * index, 16 * a + 4 * index + 4))
            for a in range(4)
        ]
    return [(slice(0, 16), pl.ds(index, 16, stride=4))]


def load_trace(cells, tile, face, trace):
    for field in range(FIELDS):
        for rows, nodes in face_pieces(face):
            target = slice(field * FACE + rows.start, field * FACE + rows.stop)
            trace[tile, target, :] = cells[tile, field, nodes, :]


def choose(sources, positions):
    shape = sources[0].shape
    lane = jnp.broadcast_to(positions & (LANES - 1), shape)
    tile = jnp.broadcast_to(positions >> 7, shape)
    result = None
    for number, source in enumerate(sources):
        found = jnp.take_along_axis(source, lane, axis=1, mode="promise_in_bounds")
        result = found if result is None else jnp.where(tile == number, found, result)
    return result


def base_owner(pairs, plane):
    owners = (pairs // plane).astype(jnp.float32)
    lowest = jnp.min(owners, axis=1, keepdims=True).astype(jnp.int32)
    highest = jnp.max(owners, axis=1, keepdims=True).astype(jnp.int32)
    return jnp.where(highest - lowest <= 1, lowest, highest)


def prep_kernel(
    plane, state, pairs, metric, jacobians, rotor, far, near, shift, rows, mixing,
    pairs_here, metric_here, rim, tiles, sems,
):
    n = lax.axis_size("space")
    me = lax.axis_index("space")
    count = plane // LANES
    copies = fetch_all(
        [(pairs, pairs_here)]
        + [
            (state.at[0, :, :, pl.ds(2 * RIM + tile * LANES, LANES)], tiles.at[tile])
            for tile in range(count)
        ]
        + [(state.at[0, :, :, pl.ds(0, 2 * RIM)], rim)]
        + [(metric, metric_here), (jacobians, mixing)],
        sems,
    )
    copies[0].wait()
    shift[0] = lax.rem(jnp.max(base_owner(pairs_here[...], plane)) - me + n, n)
    rows[1:2, :plane] = pairs_here[...].astype(jnp.float32)
    for tile in range(count):
        copies[1 + tile].wait()
        for field in range(FIELDS):
            rotor[field * FACE : (field + 1) * FACE, tile_of(tile)] = tiles[
                tile, field, pl.ds(0, FACE, stride=4), :
            ]
    for copy in copies[count + 1 :]:
        copy.wait()
    rows[0:1, :] = metric_here[...]
    odd = lax.rem(me, 2) == 1
    lane = lax.broadcasted_iota(jnp.int32, (MODES // 2, 2 * RIM), 1)
    pieces = [
        rim[field, 32 * half : 32 * half + 32, :] for field in range(FIELDS) for half in range(2)
    ]
    for k in range(FIELDS):
        top, bottom = pieces[k], pieces[k + FIELDS]
        head = jnp.where(lane < RIM, top, pltpu.roll(bottom, RIM, 1))
        tail = jnp.where(lane < RIM, pltpu.roll(top, RIM, 1), bottom)
        far[32 * k : 32 * k + 32, :] = jnp.where(odd, tail, head)
        near[32 * k : 32 * k + 32, :] = jnp.where(odd, head, tail)


def derivative_parts(lane):
    table = -gll_table()
    table[0, 0] -= 3.0
    table[3, 3] += 3.0
    table = table.astype(np.float32).tolist()
    row = lax.broadcasted_iota(jnp.int32, (16, LANES), 0)
    column = jnp.broadcast_to(lane & 15, (16, LANES))
    band = (lane & 63) >> 4

    def entry(i, j):
        value = jnp.zeros(j.shape, jnp.float32)
        for first in range(4):
            for second in range(4):
                value = jnp.where((i == first) & (j == second), table[first][second], value)
        return value

    middle = jnp.where((row & 3) == (column & 3), entry(row >> 2, column >> 2), 0.0)
    last = jnp.where((row >> 2) == (column >> 2), entry(row & 3, column & 3), 0.0)
    parts = [[], [], []]
    for a in range(4):
        along = jnp.zeros(lane.shape, jnp.float32)
        for second in range(4):
            along = jnp.where(band == second, table[a][second], along)
        parts[0].append(jnp.where(row == column, along, 0.0))
        parts[1].append(jnp.where(band == a, middle, 0.0))
        parts[2].append(jnp.where(band == a, last, 0.0))
    return parts


def own_kernel(
    state, neighbours, rows, mixing, dissipation, omega, angle, counts,
    tendency, outer, forward, loss, frequency, turn, live_count, matrix, cells, trace, sems,
):
    copies = fetch_all(
        [(dissipation, loss), (omega, frequency), (angle, turn), (counts, live_count)], sems
    )
    count = cells.shape[0]
    elems = state.shape[-1]

    for tile in range(count):
        cells[tile] = state[0, :, :, tile_of(tile)]
    for face in range(6):
        for tile in range(count):
            load_trace(cells, tile, face ^ 1, trace.at[face])

    for face in range(6):
        for tile in range(count):
            sources = [trace[face, source] for source in range(count)]
            outer[face, tile] = choose(sources, neighbours[face : face + 1, tile_of(tile)] - RIM)

    lane = lax.broadcasted_iota(jnp.int32, (1, LANES), 1)
    parts = derivative_parts(lane)
    layout = [((0, 1), 0, 5), ((2, 3), 1, 6), ((4, 0), 2, 7), ((1, 2), 3, None), ((3, 4), 4, None)]
    for g in range(FIELDS):
        values = [
            [jnp.broadcast_to(mixing[g, d : d + 1, f : f + 1], (1, LANES)) for f in range(FIELDS)]
            for d in range(3)
        ]
        for (left, right), high_place, low_place in layout:
            weight = [jnp.where(lane < MODES, values[d][left], values[d][right]) for d in range(3)]
            for a in range(4):
                block = weight[0] * parts[0][a] + weight[1] * parts[1][a] + weight[2] * parts[2][a]
                high, low = split(block)
                band = slice(g * MODES + 16 * a, g * MODES + 16 * a + 16)
                matrix[band, tile_of(high_place)] = high
                if low_place is not None:
                    if left == FIELDS - 1:
                        low = jnp.where(lane < MODES, low, jnp.zeros_like(low))
                    matrix[band, tile_of(low_place)] = low
    high, low = split(state[0].reshape(FIELDS * MODES, elems))
    stacked = jnp.concatenate([high, low, high, jnp.zeros_like(high[:MODES])], axis=0)
    product = jnp.dot(matrix[...], stacked, preferred_element_type=jnp.float32)
    for tile in range(count):
        tendency[tile] = product[:, tile_of(tile)].reshape(FIELDS, MODES, LANES)

    forward[0:2, :] = rows[0:2, :]
    for copy in copies:
        copy.wait()
    for row, value in enumerate(
        [loss[...], frequency[...], turn[...], live_count[...].astype(jnp.float32)]
    ):
        forward[2 + row : 3 + row, :] = jnp.broadcast_to(value, (1, elems))


def flux_row(g, direction, field):
    return (direction * FIELDS + g) * FIELDS + field


FRAME = 3 * FIELDS * FIELDS
WEIGHTS = FRAME + 5


def halo_kernel(
    plane, state, neighbours, forward, mixing, tendency, outer, far_source, near_source,
    partial, small, rim, trace, from_far, from_near, sems,
):
    copies = fetch_all([(far_source, from_far), (near_source, from_near)], sems)
    n = lax.axis_size("space")
    inst_count = lax.axis_size("inst")
    inst = lax.axis_index("inst")
    count = partial.shape[0]
    elems = state.shape[-1]
    for g in range(FIELDS):
        for d in range(3):
            for field in range(FIELDS):
                row = flux_row(g, d, field)
                small[row : row + 1, :] = jnp.broadcast_to(
                    mixing[g, d : d + 1, field : field + 1], (1, LANES)
                )
    loss, frequency, turn, live_count = [
        forward[2 + row : 3 + row, :LANES] for row in range(4)
    ]
    small[FRAME : FRAME + 1, :] = 3.0 * loss
    small[FRAME + 1 : FRAME + 2, :] = jnp.cos(turn)
    small[FRAME + 2 : FRAME + 3, :] = jnp.sin(turn)

    lane = lax.broadcasted_iota(jnp.int32, (1, LANES), 1)
    spectral = spectral_values(inst_count)
    keeps, scales = [], []
    for tile in range(count):
        scale = forward[0:1, tile_of(tile)]
        step = COURANT / (scale * loss + frequency)
        live = (lane + tile * LANES).astype(jnp.float32) < live_count
        step = jnp.where(live, step, 0.0)
        keeps.append(jnp.where(live, 1.0, 0.0) - step * (frequency * spectral[0]))
        scales.append(step * scale)
        small[WEIGHTS + tile : WEIGHTS + tile + 1, :] = scales[tile]
        for away in range(1, inst_count):
            value = jnp.where(
                inst + away < inst_count, spectral[-away], spectral[inst_count - away]
            )
            row = WEIGHTS + away * count + tile
            small[row : row + 1, :] = -step * (frequency * value)

    pairs = forward[1:2, :plane].astype(jnp.int32)
    place = pairs - base_owner(pairs, plane) * plane
    place = jnp.where(place < 0, place + n * plane, place).astype(jnp.float32)
    for tile in range(plane // LANES):
        row = WEIGHTS + inst_count * count + tile
        small[row : row + 1, :] = place[:, tile_of(tile)]

    partial[...] = tendency[...]
    for copy in copies:
        copy.wait()
    odd = lax.rem(lax.axis_index("space"), 2) == 1
    half_lane = lax.broadcasted_iota(jnp.int32, (MODES // 2, 2 * RIM), 1)
    for k in range(2 * FIELDS):
        field, half = k // 2, k % 2
        piece = pl.ds(32 * (k % FIELDS), 32)
        left = jnp.where(odd, from_near[piece, :], from_far[piece, :])
        right = jnp.where(odd, from_far[piece, :], from_near[piece, :])
        if k < FIELDS:
            right = pltpu.roll(right, RIM, 1)
        else:
            left = pltpu.roll(left, RIM, 1)
        rim[0, field, 32 * half : 32 * half + 32, :] = jnp.where(half_lane < RIM, left, right)
    for face in range(6):
        load_trace(rim, 0, face ^ 1, trace.at[pl.ds(face, 1)])
    for face in range(6):
        for tile in range(count):
            number = neighbours[face : face + 1, tile_of(tile)]
            previous = number < RIM
            remote = previous | (number >= RIM + elems)
            found = choose([trace[face]], jnp.where(previous, number, number - elems))
            found = jnp.where(remote, found, outer[face, tile])
            if face == 5:
                column = lane + tile * LANES
                sliding = (column >= 2 * RIM) & (column < 2 * RIM + plane)
                found = jnp.where(sliding, 0.0, found)
            parts = [found[field * FACE : (field + 1) * FACE] for field in range(FIELDS)]
            lift(partial, tile, face, mix(small, face, parts), 1.0)

    node = lax.broadcasted_iota(jnp.int32, (MODES, LANES), 0)
    faces = jnp.zeros((MODES, LANES), jnp.float32)
    for index in (node >> 4, (node >> 2) & 3, node & 3):
        faces = faces + jnp.where((index == 0) | (index == 3), 1.0, 0.0)
    for tile in range(count):
        keep = keeps[tile] - (3.0 * loss * scales[tile]) * faces
        partial[tile] = keep * state[0, :, :, tile_of(tile)] + scales[tile] * partial[tile]


def mix(small, face, parts):
    mixed = []
    for g in range(FIELDS):
        total = None
        for field in range(FIELDS):
            row = flux_row(g, face // 2, field)
            term = small[row : row + 1, :] * parts[field]
            total = term if total is None else total + term
        mixed.append((3.0 if face % 2 else -3.0) * total - small[FRAME : FRAME + 1, :] * parts[g])
    return mixed


def lift(cells, tile, face, mixed, scale):
    for g in range(FIELDS):
        change = scale * mixed[g]
        for rows, nodes in face_pieces(face):
            cells[tile, g, nodes, :] = cells[tile, g, nodes, :] - change[rows]


def final_kernel(plane, partial, small, first, second, *refs):
    inst_count = lax.axis_size("inst")
    others, (result, buffer, sems) = refs[: inst_count - 1], refs[inst_count - 1 :]
    count = buffer.shape[0]
    start, stop = 2 * RIM // LANES, (2 * RIM + plane) // LANES
    copies = []
    for tile in [*range(start), *range(stop, count), *range(start, stop)]:
        for field in range(FIELDS):
            total = partial[tile, field]
            for away in range(1, inst_count):
                row = WEIGHTS + away * count + tile
                other = others[away - 1][0, field, :, tile_of(tile)]
                total = total + small[row : row + 1, :] * other
            buffer[tile, field] = total
        if start <= tile < stop:
            row = WEIGHTS + inst_count * count + tile - start
            found = choose(
                [
                    block[:, tile_of(source)]
                    for block in (first, second)
                    for source in range(plane // LANES)
                ],
                small[row : row + 1, :].astype(jnp.int32),
            )
            parts = [found[field * FACE : (field + 1) * FACE] for field in range(FIELDS)]
            cosine, sine = small[FRAME + 1 : FRAME + 2, :], small[FRAME + 2 : FRAME + 3, :]
            parts[2], parts[3] = (
                cosine * parts[2] - sine * parts[3],
                sine * parts[2] + cosine * parts[3],
            )
            scale = small[WEIGHTS + tile : WEIGHTS + tile + 1, :]
            lift(buffer, tile, 5, mix(small, 5, parts), scale)
        copies.append(
            pltpu.make_async_copy(
                buffer.at[tile], result.at[0, :, :, pl.ds(tile * LANES, LANES)], sems.at[tile]
            )
        )
        copies[-1].start()
    for copy in copies:
        copy.wait()


def shards(
    state, metric, jacobians, dissipation, omega, rotor_angle, counts, neighbours, mortar_pairs
):
    elems = state.shape[-1]
    tiles = elems // LANES
    plane = mortar_pairs.shape[-1]
    n = lax.axis_size("space")
    inst_count = lax.axis_size("inst")
    f32 = jnp.float32
    shape = jax.ShapeDtypeStruct
    sems = pltpu.SemaphoreType.DMA
    scalar = pltpu.VMEM((1, 1), f32)
    params = pltpu.CompilerParams(vmem_limit_bytes=32 * 2**20)
    cost = pl.CostEstimate(flops=2**31, bytes_accessed=2**22, transcendentals=0)

    others = [
        lax.ppermute(state, "inst", [((i + away) % inst_count, i) for i in range(inst_count)])
        for away in range(1, inst_count)
    ]

    rotor, far, near, shift, rows, mixing = pl.pallas_call(
        functools.partial(prep_kernel, plane),
        out_shape=(
            shape((TRACE, plane), f32),
            shape((FIELDS * MODES // 2, 2 * RIM), f32),
            shape((FIELDS * MODES // 2, 2 * RIM), f32),
            shape((1,), jnp.int32),
            shape((8, elems), f32),
            shape((FIELDS, 3, FIELDS), f32),
        ),
        in_specs=[HBM] * 4,
        out_specs=(VMEM, VMEM, VMEM, SMEM, VMEM, VMEM),
        scratch_shapes=[
            pltpu.VMEM((1, plane), jnp.int32),
            pltpu.VMEM((1, elems), f32),
            pltpu.VMEM((FIELDS, MODES, 2 * RIM), f32),
            pltpu.VMEM((plane // LANES, FIELDS, MODES, LANES), f32),
            sems((plane // LANES + 4,)),
        ],
        name="prep",
    )(state, mortar_pairs, metric.reshape(1, elems), jnp.transpose(jacobians, (1, 0, 2)))

    def fetch(away, block):
        if away == 0:
            return block
        return lax.ppermute(block, "space", [((i + away) % n, i) for i in range(n)])

    ends = [(i, (i + 1) % n) for i in range(1, n, 2)]
    middles = [(i, i + 1) for i in range(0, n, 2)]

    def swap(pairs, block):
        return lax.ppermute(block, "space", pairs + [(j, i) for i, j in pairs])

    def branch(away, rotor, far, near, *operands):
        first = fetch(away, rotor)
        from_far, from_near = swap(ends, far), swap(middles, near)
        own = pl.pallas_call(
            own_kernel,
            out_shape=(
                shape((tiles, FIELDS, MODES, LANES), f32),
                shape((6, tiles, TRACE, LANES), f32),
                shape((8, elems), f32),
            ),
            in_specs=[VMEM] * 4 + [HBM] * 4,
            out_specs=(VMEM,) * 3,
            scratch_shapes=[
                scalar,
                scalar,
                scalar,
                pltpu.VMEM((1, 1), jnp.int32),
                pltpu.VMEM((FIELDS * MODES, 8 * LANES), jnp.bfloat16),
                pltpu.VMEM((tiles, FIELDS, MODES, LANES), f32),
                pltpu.VMEM((6, tiles, TRACE, LANES), f32),
                sems((4,)),
            ],
            compiler_params=params,
            cost_estimate=cost,
            name="own",
        )(*operands)
        return first, from_far, from_near, own

    first, from_far, from_near, (tendency, outer, forward) = lax.switch(
        shift[0],
        [functools.partial(branch, away) for away in range(n)],
        rotor, far, near, state, neighbours, rows, mixing, dissipation.reshape(1, 1),
        omega.reshape(1, 1), rotor_angle.reshape(1, 1), counts.reshape(1, 1),
    )
    second = fetch(1, first)

    partial, small = pl.pallas_call(
        functools.partial(halo_kernel, plane),
        out_shape=(
            shape((tiles, FIELDS, MODES, LANES), f32),
            shape((-(-(WEIGHTS + inst_count * tiles + plane // LANES) // 8) * 8, LANES), f32),
        ),
        in_specs=[VMEM] * 6 + [ANY] * 2,
        out_specs=(VMEM, VMEM),
        scratch_shapes=[
            pltpu.VMEM((1, FIELDS, MODES, 2 * RIM), f32),
            pltpu.VMEM((6, TRACE, LANES), f32),
            pltpu.VMEM((FIELDS * MODES // 2, 2 * RIM), f32),
            pltpu.VMEM((FIELDS * MODES // 2, 2 * RIM), f32),
            sems((2,)),
        ],
        compiler_params=params,
        cost_estimate=cost,
        name="halo",
    )(state, neighbours, forward, mixing, tendency, outer, from_far, from_near)

    return pl.pallas_call(
        functools.partial(final_kernel, plane),
        out_shape=shape(state.shape, f32),
        in_specs=[VMEM] * (3 + inst_count),
        out_specs=ANY,
        scratch_shapes=[
            pltpu.VMEM((tiles, FIELDS, MODES, LANES), f32),
            sems((tiles,)),
        ],
        compiler_params=params,
        name="final",
    )(partial, small, first, second, *others)


def solution(mesh):
    return jax.shard_map(
        shards,
        mesh=mesh,
        in_specs=(
            P("inst", None, None, "space"),
            P("space"),
            P(),
            P(),
            P(),
            P("inst"),
            P("space"),
            P(None, "space"),
            P("inst", "space"),
        ),
        out_specs=P("inst", None, None, "space"),
        check_vma=False,
    )
```

```python
import functools
import math

import jax
import jax.numpy as jnp
import numpy as np
from jax import lax
from jax.experimental import pallas as pl
from jax.experimental.pallas import tpu as pltpu
from jax.sharding import PartitionSpec as P

RIM = 64
FIELDS = 5
MODES = 64
FACE = 16
TRACE = FIELDS * FACE
LANES = 128
COURANT = 0.5

VMEM = pl.BlockSpec(memory_space=pltpu.VMEM)
SMEM = pl.BlockSpec(memory_space=pltpu.SMEM)
ANY = pl.BlockSpec(memory_space=pl.ANY)
HBM = pl.BlockSpec(memory_space=pltpu.HBM)


def gll_table():
    nodes = np.array([-1.0, -1.0 / math.sqrt(5.0), 1.0 / math.sqrt(5.0), 1.0])
    barycentric = np.array(
        [1.0 / np.prod([nodes[j] - nodes[k] for k in range(4) if k != j]) for j in range(4)]
    )
    derivative = np.zeros((4, 4))
    for i in range(4):
        for j in range(4):
            if i != j:
                derivative[i, j] = barycentric[j] / barycentric[i] / (nodes[i] - nodes[j])
        derivative[i, i] = -np.sum(derivative[i])
    return derivative


def face_nodes(face):
    direction, index = face // 2, 3 * (face % 2)
    nodes = []
    for first in range(4):
        for second in range(4):
            if direction == 0:
                nodes.append(16 * index + 4 * first + second)
            elif direction == 1:
                nodes.append(16 * first + 4 * index + second)
            else:
                nodes.append(16 * first + 4 * second + index)
    return nodes


def spectral_values(count):
    values = {0: (count * count + 2.0) / (12.0 * count)}
    for k in range(1 - count, count):
        if k:
            parity = -1.0 if k % 2 else 1.0
            angle = math.pi * k / count
            values[k] = 0.5 * parity / math.tan(angle) + parity / (
                2.0 * count * math.sin(angle) ** 2
            )
    return values


def split(value):
    high = value.astype(jnp.bfloat16)
    low = (value - high.astype(jnp.float32)).astype(jnp.bfloat16)
    return high, low


def fetch_all(pairs, sems):
    copies = [
        pltpu.make_async_copy(source, target, sems.at[k]) for k, (source, target) in enumerate(pairs)
    ]
    for copy in copies:
        copy.start()
    return copies


def tile_of(number):
    return slice(number * LANES, (number + 1) * LANES)


def face_pieces(face):
    direction, index = face // 2, 3 * (face % 2)
    if direction == 0:
        return [(slice(0, 16), slice(16 * index, 16 * index + 16))]
    if direction == 1:
        return [
            (slice(4 * a, 4 * a + 4), slice(16 * a + 4 * index, 16 * a + 4 * index + 4))
            for a in range(4)
        ]
    return [(slice(0, 16), pl.ds(index, 16, stride=4))]


def load_trace(cells, tile, face, trace):
    for field in range(FIELDS):
        for rows, nodes in face_pieces(face):
            target = slice(field * FACE + rows.start, field * FACE + rows.stop)
            trace[tile, target, :] = cells[tile, field, nodes, :]


def choose(sources, positions):
    shape = sources[0].shape
    lane = jnp.broadcast_to(positions & (LANES - 1), shape)
    tile = jnp.broadcast_to(positions >> 7, shape)
    result = None
    for number, source in enumerate(sources):
        found = jnp.take_along_axis(source, lane, axis=1, mode="promise_in_bounds")
        result = found if result is None else jnp.where(tile == number, found, result)
    return result


def base_owner(pairs, plane):
    owners = (pairs // plane).astype(jnp.float32)
    lowest = jnp.min(owners, axis=1, keepdims=True).astype(jnp.int32)
    highest = jnp.max(owners, axis=1, keepdims=True).astype(jnp.int32)
    return jnp.where(highest - lowest <= 1, lowest, highest)


def prep_kernel(
    plane, state, pairs, metric, jacobians, rotor, far, near, shift, rows, mixing,
    pairs_here, metric_here, rim, tiles, sems,
):
    n = lax.axis_size("space")
    me = lax.axis_index("space")
    count = plane // LANES
    copies = fetch_all(
        [(pairs, pairs_here)]
        + [
            (state.at[0, :, :, pl.ds(2 * RIM + tile * LANES, LANES)], tiles.at[tile])
            for tile in range(count)
        ]
        + [(state.at[0, :, :, pl.ds(0, 2 * RIM)], rim)]
        + [(metric, metric_here), (jacobians, mixing)],
        sems,
    )
    copies[0].wait()
    shift[0] = lax.rem(jnp.max(base_owner(pairs_here[...], plane)) - me + n, n)
    rows[1:2, :plane] = pairs_here[...].astype(jnp.float32)
    for tile in range(count):
        copies[1 + tile].wait()
        for field in range(FIELDS):
            rotor[field * FACE : (field + 1) * FACE, tile_of(tile)] = tiles[
                tile, field, pl.ds(0, FACE, stride=4), :
            ]
    for copy in copies[count + 1 :]:
        copy.wait()
    rows[0:1, :] = metric_here[...]
    odd = lax.rem(me, 2) == 1
    lane = lax.broadcasted_iota(jnp.int32, (MODES // 2, 2 * RIM), 1)
    pieces = [
        rim[field, 32 * half : 32 * half + 32, :] for field in range(FIELDS) for half in range(2)
    ]
    for k in range(FIELDS):
        top, bottom = pieces[k], pieces[k + FIELDS]
        head = jnp.where(lane < RIM, top, pltpu.roll(bottom, RIM, 1))
        tail = jnp.where(lane < RIM, pltpu.roll(top, RIM, 1), bottom)
        far[32 * k : 32 * k + 32, :] = jnp.where(odd, tail, head)
        near[32 * k : 32 * k + 32, :] = jnp.where(odd, head, tail)


def derivative_parts(lane):
    table = -gll_table()
    table[0, 0] -= 3.0
    table[3, 3] += 3.0
    table = table.astype(np.float32).tolist()
    row = lax.broadcasted_iota(jnp.int32, (16, LANES), 0)
    column = jnp.broadcast_to(lane & 15, (16, LANES))
    band = (lane & 63) >> 4

    def entry(i, j):
        value = jnp.zeros(j.shape, jnp.float32)
        for first in range(4):
            for second in range(4):
                value = jnp.where((i == first) & (j == second), table[first][second], value)
        return value

    middle = jnp.where((row & 3) == (column & 3), entry(row >> 2, column >> 2), 0.0)
    last = jnp.where((row >> 2) == (column >> 2), entry(row & 3, column & 3), 0.0)
    parts = [[], [], []]
    for a in range(4):
        along = jnp.zeros(lane.shape, jnp.float32)
        for second in range(4):
            along = jnp.where(band == second, table[a][second], along)
        parts[0].append(jnp.where(row == column, along, 0.0))
        parts[1].append(jnp.where(band == a, middle, 0.0))
        parts[2].append(jnp.where(band == a, last, 0.0))
    return parts


def own_kernel(state, neighbours, mixing, tendency, outer, matrix, cells, trace):
    count = cells.shape[0]
    elems = state.shape[-1]

    for tile in range(count):
        cells[tile] = state[0, :, :, tile_of(tile)]
    for face in range(6):
        for tile in range(count):
            load_trace(cells, tile, face ^ 1, trace.at[face])

    for face in range(6):
        for tile in range(count):
            sources = [trace[face, source] for source in range(count)]
            outer[face, tile] = choose(sources, neighbours[face : face + 1, tile_of(tile)] - RIM)

    lane = lax.broadcasted_iota(jnp.int32, (1, LANES), 1)
    parts = derivative_parts(lane)
    layout = [((0, 1), 0, 5), ((2, 3), 1, 6), ((4, 0), 2, 7), ((1, 2), 3, None), ((3, 4), 4, None)]
    for g in range(FIELDS):
        values = [
            [jnp.broadcast_to(mixing[g, d : d + 1, f : f + 1], (1, LANES)) for f in range(FIELDS)]
            for d in range(3)
        ]
        for (left, right), high_place, low_place in layout:
            weight = [jnp.where(lane < MODES, values[d][left], values[d][right]) for d in range(3)]
            for a in range(4):
                block = weight[0] * parts[0][a] + weight[1] * parts[1][a] + weight[2] * parts[2][a]
                high, low = split(block)
                band = slice(g * MODES + 16 * a, g * MODES + 16 * a + 16)
                matrix[band, tile_of(high_place)] = high
                if low_place is not None:
                    if left == FIELDS - 1:
                        low = jnp.where(lane < MODES, low, jnp.zeros_like(low))
                    matrix[band, tile_of(low_place)] = low
    high, low = split(state[0].reshape(FIELDS * MODES, elems))
    stacked = jnp.concatenate([high, low, high, jnp.zeros_like(high[:MODES])], axis=0)
    product = jnp.dot(matrix[...], stacked, preferred_element_type=jnp.float32)
    for tile in range(count):
        tendency[tile] = product[:, tile_of(tile)].reshape(FIELDS, MODES, LANES)


def flux_row(g, direction, field):
    return (direction * FIELDS + g) * FIELDS + field


FRAME = 3 * FIELDS * FIELDS
WEIGHTS = FRAME + 5


def halo_kernel(
    plane, state, neighbours, rows, scalars, mixing, tendency, outer, far_source, near_source,
    partial, small, rim, trace, from_far, from_near, sems,
):
    copies = fetch_all([(far_source, from_far), (near_source, from_near)], sems)
    n = lax.axis_size("space")
    inst_count = lax.axis_size("inst")
    inst = lax.axis_index("inst")
    count = partial.shape[0]
    elems = state.shape[-1]
    for g in range(FIELDS):
        for d in range(3):
            for field in range(FIELDS):
                row = flux_row(g, d, field)
                small[row : row + 1, :] = jnp.broadcast_to(
                    mixing[g, d : d + 1, field : field + 1], (1, LANES)
                )
    loss, frequency, turn, live_count = [
        scalars[row : row + 1, :] for row in range(4)
    ]
    small[FRAME : FRAME + 1, :] = 3.0 * loss
    small[FRAME + 1 : FRAME + 2, :] = jnp.cos(turn)
    small[FRAME + 2 : FRAME + 3, :] = jnp.sin(turn)

    lane = lax.broadcasted_iota(jnp.int32, (1, LANES), 1)
    spectral = spectral_values(inst_count)
    keeps, scales = [], []
    for tile in range(count):
        scale = rows[0:1, tile_of(tile)]
        step = COURANT / (scale * loss + frequency)
        live = (lane + tile * LANES).astype(jnp.float32) < live_count
        step = jnp.where(live, step, 0.0)
        keeps.append(jnp.where(live, 1.0, 0.0) - step * (frequency * spectral[0]))
        scales.append(step * scale)
        small[WEIGHTS + tile : WEIGHTS + tile + 1, :] = scales[tile]
        for away in range(1, inst_count):
            value = jnp.where(
                inst + away < inst_count, spectral[-away], spectral[inst_count - away]
            )
            row = WEIGHTS + away * count + tile
            small[row : row + 1, :] = -step * (frequency * value)

    pairs = rows[1:2, :plane].astype(jnp.int32)
    place = pairs - base_owner(pairs, plane) * plane
    place = jnp.where(place < 0, place + n * plane, place).astype(jnp.float32)
    for tile in range(plane // LANES):
        row = WEIGHTS + inst_count * count + tile
        small[row : row + 1, :] = place[:, tile_of(tile)]

    partial[...] = tendency[...]
    for copy in copies:
        copy.wait()
    odd = lax.rem(lax.axis_index("space"), 2) == 1
    half_lane = lax.broadcasted_iota(jnp.int32, (MODES // 2, 2 * RIM), 1)
    for k in range(2 * FIELDS):
        field, half = k // 2, k % 2
        piece = pl.ds(32 * (k % FIELDS), 32)
        left = jnp.where(odd, from_near[piece, :], from_far[piece, :])
        right = jnp.where(odd, from_far[piece, :], from_near[piece, :])
        if k < FIELDS:
            right = pltpu.roll(right, RIM, 1)
        else:
            left = pltpu.roll(left, RIM, 1)
        rim[0, field, 32 * half : 32 * half + 32, :] = jnp.where(half_lane < RIM, left, right)
    for face in range(6):
        load_trace(rim, 0, face ^ 1, trace.at[pl.ds(face, 1)])
    for face in range(6):
        for tile in range(count):
            number = neighbours[face : face + 1, tile_of(tile)]
            previous = number < RIM
            remote = previous | (number >= RIM + elems)
            found = choose([trace[face]], jnp.where(previous, number, number - elems))
            found = jnp.where(remote, found, outer[face, tile])
            if face == 5:
                column = lane + tile * LANES
                sliding = (column >= 2 * RIM) & (column < 2 * RIM + plane)
                found = jnp.where(sliding, 0.0, found)
            parts = [found[field * FACE : (field + 1) * FACE] for field in range(FIELDS)]
            lift(partial, tile, face, mix(small, face, parts), 1.0)

    node = lax.broadcasted_iota(jnp.int32, (MODES, LANES), 0)
    faces = jnp.zeros((MODES, LANES), jnp.float32)
    for index in (node >> 4, (node >> 2) & 3, node & 3):
        faces = faces + jnp.where((index == 0) | (index == 3), 1.0, 0.0)
    for tile in range(count):
        keep = keeps[tile] - (3.0 * loss * scales[tile]) * faces
        partial[tile] = keep * state[0, :, :, tile_of(tile)] + scales[tile] * partial[tile]


def mix(small, face, parts):
    mixed = []
    for g in range(FIELDS):
        total = None
        for field in range(FIELDS):
            row = flux_row(g, face // 2, field)
            term = small[row : row + 1, :] * parts[field]
            total = term if total is None else total + term
        mixed.append((3.0 if face % 2 else -3.0) * total - small[FRAME : FRAME + 1, :] * parts[g])
    return mixed


def lift(cells, tile, face, mixed, scale):
    for g in range(FIELDS):
        change = scale * mixed[g]
        for rows, nodes in face_pieces(face):
            cells[tile, g, nodes, :] = cells[tile, g, nodes, :] - change[rows]


def final_kernel(plane, partial, small, first, second, *refs):
    inst_count = lax.axis_size("inst")
    others, (result, buffer, sems) = refs[: inst_count - 1], refs[inst_count - 1 :]
    count = buffer.shape[0]
    start, stop = 2 * RIM // LANES, (2 * RIM + plane) // LANES
    copies = []
    for tile in [*range(start), *range(stop, count), *range(start, stop)]:
        for field in range(FIELDS):
            total = partial[tile, field]
            for away in range(1, inst_count):
                row = WEIGHTS + away * count + tile
                other = others[away - 1][0, field, :, tile_of(tile)]
                total = total + small[row : row + 1, :] * other
            buffer[tile, field] = total
        if start <= tile < stop:
            row = WEIGHTS + inst_count * count + tile - start
            found = choose(
                [
                    block[:, tile_of(source)]
                    for block in (first, second)
                    for source in range(plane // LANES)
                ],
                small[row : row + 1, :].astype(jnp.int32),
            )
            parts = [found[field * FACE : (field + 1) * FACE] for field in range(FIELDS)]
            cosine, sine = small[FRAME + 1 : FRAME + 2, :], small[FRAME + 2 : FRAME + 3, :]
            parts[2], parts[3] = (
                cosine * parts[2] - sine * parts[3],
                sine * parts[2] + cosine * parts[3],
            )
            scale = small[WEIGHTS + tile : WEIGHTS + tile + 1, :]
            lift(buffer, tile, 5, mix(small, 5, parts), scale)
        copies.append(
            pltpu.make_async_copy(
                buffer.at[tile], result.at[0, :, :, pl.ds(tile * LANES, LANES)], sems.at[tile]
            )
        )
        copies[-1].start()
    for copy in copies:
        copy.wait()


def shards(
    state, metric, jacobians, dissipation, omega, rotor_angle, counts, neighbours, mortar_pairs
):
    elems = state.shape[-1]
    tiles = elems // LANES
    plane = mortar_pairs.shape[-1]
    n = lax.axis_size("space")
    inst_count = lax.axis_size("inst")
    f32 = jnp.float32
    shape = jax.ShapeDtypeStruct
    sems = pltpu.SemaphoreType.DMA
    params = pltpu.CompilerParams(vmem_limit_bytes=32 * 2**20)
    cost = pl.CostEstimate(flops=2**31, bytes_accessed=2**22, transcendentals=0)

    others = [
        lax.ppermute(state, "inst", [((i + away) % inst_count, i) for i in range(inst_count)])
        for away in range(1, inst_count)
    ]

    rotor, far, near, shift, rows, mixing = pl.pallas_call(
        functools.partial(prep_kernel, plane),
        out_shape=(
            shape((TRACE, plane), f32),
            shape((FIELDS * MODES // 2, 2 * RIM), f32),
            shape((FIELDS * MODES // 2, 2 * RIM), f32),
            shape((1,), jnp.int32),
            shape((8, elems), f32),
            shape((FIELDS, 3, FIELDS), f32),
        ),
        in_specs=[HBM] * 4,
        out_specs=(VMEM, VMEM, VMEM, SMEM, VMEM, VMEM),
        scratch_shapes=[
            pltpu.VMEM((1, plane), jnp.int32),
            pltpu.VMEM((1, elems), f32),
            pltpu.VMEM((FIELDS, MODES, 2 * RIM), f32),
            pltpu.VMEM((plane // LANES, FIELDS, MODES, LANES), f32),
            sems((plane // LANES + 4,)),
        ],
        name="prep",
    )(state, mortar_pairs, metric.reshape(1, elems), jnp.transpose(jacobians, (1, 0, 2)))

    def fetch(away, block):
        if away == 0:
            return block
        return lax.ppermute(block, "space", [((i + away) % n, i) for i in range(n)])

    ends = [(i, (i + 1) % n) for i in range(1, n, 2)]
    middles = [(i, i + 1) for i in range(0, n, 2)]

    def swap(pairs, block):
        return lax.ppermute(block, "space", pairs + [(j, i) for i, j in pairs])

    def branch(away, rotor, far, near, state, neighbours, mixing, *single):
        first = fetch(away, rotor)
        from_far, from_near = swap(ends, far), swap(middles, near)
        scalars = jnp.concatenate(
            [jnp.broadcast_to(value.astype(f32).reshape(1, 1), (1, LANES)) for value in single],
            axis=0,
        )
        own = pl.pallas_call(
            own_kernel,
            out_shape=(
                shape((tiles, FIELDS, MODES, LANES), f32),
                shape((6, tiles, TRACE, LANES), f32),
            ),
            in_specs=[VMEM] * 3,
            out_specs=(VMEM,) * 2,
            scratch_shapes=[
                pltpu.VMEM((FIELDS * MODES, 8 * LANES), jnp.bfloat16),
                pltpu.VMEM((tiles, FIELDS, MODES, LANES), f32),
                pltpu.VMEM((6, tiles, TRACE, LANES), f32),
            ],
            compiler_params=params,
            cost_estimate=cost,
            name="own",
        )(state, neighbours, mixing)
        return first, from_far, from_near, own, scalars

    first, from_far, from_near, (tendency, outer), scalars = lax.switch(
        shift[0],
        [functools.partial(branch, away) for away in range(n)],
        rotor, far, near, state, neighbours, mixing, dissipation, omega, rotor_angle, counts,
    )
    second = fetch(1, first)

    partial, small = pl.pallas_call(
        functools.partial(halo_kernel, plane),
        out_shape=(
            shape((tiles, FIELDS, MODES, LANES), f32),
            shape((-(-(WEIGHTS + inst_count * tiles + plane // LANES) // 8) * 8, LANES), f32),
        ),
        in_specs=[VMEM] * 7 + [ANY] * 2,
        out_specs=(VMEM, VMEM),
        scratch_shapes=[
            pltpu.VMEM((1, FIELDS, MODES, 2 * RIM), f32),
            pltpu.VMEM((6, TRACE, LANES), f32),
            pltpu.VMEM((FIELDS * MODES // 2, 2 * RIM), f32),
            pltpu.VMEM((FIELDS * MODES // 2, 2 * RIM), f32),
            sems((2,)),
        ],
        compiler_params=params,
        cost_estimate=cost,
        name="halo",
    )(state, neighbours, rows, scalars, mixing, tendency, outer, from_far, from_near)

    return pl.pallas_call(
        functools.partial(final_kernel, plane),
        out_shape=shape(state.shape, f32),
        in_specs=[VMEM] * (3 + inst_count),
        out_specs=ANY,
        scratch_shapes=[
            pltpu.VMEM((tiles, FIELDS, MODES, LANES), f32),
            sems((tiles,)),
        ],
        compiler_params=params,
        name="final",
    )(partial, small, first, second, *others)


def solution(mesh):
    return jax.shard_map(
        shards,
        mesh=mesh,
        in_specs=(
            P("inst", None, None, "space"),
            P("space"),
            P(),
            P(),
            P(),
            P("inst"),
            P("space"),
            P(None, "space"),
            P("inst", "space"),
        ),
        out_specs=P("inst", None, None, "space"),
        check_vma=False,
    )
```

```python
import functools
import math

import jax
import jax.numpy as jnp
import numpy as np
from jax import lax
from jax.experimental import pallas as pl
from jax.experimental.pallas import tpu as pltpu
from jax.sharding import PartitionSpec as P

RIM = 64
FIELDS = 5
MODES = 64
FACE = 16
TRACE = FIELDS * FACE
LANES = 128
COURANT = 0.5

VMEM = pl.BlockSpec(memory_space=pltpu.VMEM)
SMEM = pl.BlockSpec(memory_space=pltpu.SMEM)
ANY = pl.BlockSpec(memory_space=pl.ANY)
HBM = pl.BlockSpec(memory_space=pltpu.HBM)


def gll_table():
    nodes = np.array([-1.0, -1.0 / math.sqrt(5.0), 1.0 / math.sqrt(5.0), 1.0])
    barycentric = np.array(
        [1.0 / np.prod([nodes[j] - nodes[k] for k in range(4) if k != j]) for j in range(4)]
    )
    derivative = np.zeros((4, 4))
    for i in range(4):
        for j in range(4):
            if i != j:
                derivative[i, j] = barycentric[j] / barycentric[i] / (nodes[i] - nodes[j])
        derivative[i, i] = -np.sum(derivative[i])
    return derivative


def face_nodes(face):
    direction, index = face // 2, 3 * (face % 2)
    nodes = []
    for first in range(4):
        for second in range(4):
            if direction == 0:
                nodes.append(16 * index + 4 * first + second)
            elif direction == 1:
                nodes.append(16 * first + 4 * index + second)
            else:
                nodes.append(16 * first + 4 * second + index)
    return nodes


def spectral_values(count):
    values = {0: (count * count + 2.0) / (12.0 * count)}
    for k in range(1 - count, count):
        if k:
            parity = -1.0 if k % 2 else 1.0
            angle = math.pi * k / count
            values[k] = 0.5 * parity / math.tan(angle) + parity / (
                2.0 * count * math.sin(angle) ** 2
            )
    return values


def split(value):
    high = value.astype(jnp.bfloat16)
    low = (value - high.astype(jnp.float32)).astype(jnp.bfloat16)
    return high, low


def fetch_all(pairs, sems):
    copies = [
        pltpu.make_async_copy(source, target, sems.at[k]) for k, (source, target) in enumerate(pairs)
    ]
    for copy in copies:
        copy.start()
    return copies


def tile_of(number):
    return slice(number * LANES, (number + 1) * LANES)


def face_pieces(face):
    direction, index = face // 2, 3 * (face % 2)
    if direction == 0:
        return [(slice(0, 16), slice(16 * index, 16 * index + 16))]
    if direction == 1:
        return [
            (slice(4 * a, 4 * a + 4), slice(16 * a + 4 * index, 16 * a + 4 * index + 4))
            for a in range(4)
        ]
    return [(slice(0, 16), pl.ds(index, 16, stride=4))]


def load_trace(cells, tile, face, trace):
    for field in range(FIELDS):
        for rows, nodes in face_pieces(face):
            target = slice(field * FACE + rows.start, field * FACE + rows.stop)
            trace[tile, target, :] = cells[tile, field, nodes, :]


def choose(sources, positions):
    shape = sources[0].shape
    lane = jnp.broadcast_to(positions & (LANES - 1), shape)
    tile = jnp.broadcast_to(positions >> 7, shape)
    result = None
    for number, source in enumerate(sources):
        found = jnp.take_along_axis(source, lane, axis=1, mode="promise_in_bounds")
        result = found if result is None else jnp.where(tile == number, found, result)
    return result


def base_owner(pairs, plane):
    owners = (pairs // plane).astype(jnp.float32)
    lowest = jnp.min(owners, axis=1, keepdims=True).astype(jnp.int32)
    highest = jnp.max(owners, axis=1, keepdims=True).astype(jnp.int32)
    return jnp.where(highest - lowest <= 1, lowest, highest)


def prep_kernel(
    plane, state, pairs, metric, jacobians, rotor, far, near, shift, rows, mixing,
    pairs_here, metric_here, rim, tiles, sems,
):
    n = lax.axis_size("space")
    me = lax.axis_index("space")
    count = plane // LANES
    copies = fetch_all(
        [(pairs, pairs_here)]
        + [
            (state.at[0, :, :, pl.ds(2 * RIM + tile * LANES, LANES)], tiles.at[tile])
            for tile in range(count)
        ]
        + [(state.at[0, :, :, pl.ds(0, 2 * RIM)], rim)]
        + [(metric, metric_here), (jacobians, mixing)],
        sems,
    )
    copies[0].wait()
    shift[0] = lax.rem(jnp.max(base_owner(pairs_here[...], plane)) - me + n, n)
    rows[1:2, :plane] = pairs_here[...].astype(jnp.float32)
    for tile in range(count):
        copies[1 + tile].wait()
        for field in range(FIELDS):
            rotor[field * FACE : (field + 1) * FACE, tile_of(tile)] = tiles[
                tile, field, pl.ds(0, FACE, stride=4), :
            ]
    for copy in copies[count + 1 :]:
        copy.wait()
    rows[0:1, :] = metric_here[...]
    odd = lax.rem(me, 2) == 1
    lane = lax.broadcasted_iota(jnp.int32, (MODES // 2, 2 * RIM), 1)
    pieces = [
        rim[field, 32 * half : 32 * half + 32, :] for field in range(FIELDS) for half in range(2)
    ]
    for k in range(FIELDS):
        top, bottom = pieces[k], pieces[k + FIELDS]
        head = jnp.where(lane < RIM, top, pltpu.roll(bottom, RIM, 1))
        tail = jnp.where(lane < RIM, pltpu.roll(top, RIM, 1), bottom)
        far[32 * k : 32 * k + 32, :] = jnp.where(odd, tail, head)
        near[32 * k : 32 * k + 32, :] = jnp.where(odd, head, tail)


def derivative_parts(lane):
    table = -gll_table()
    table[0, 0] -= 3.0
    table[3, 3] += 3.0
    table = table.astype(np.float32).tolist()
    row = lax.broadcasted_iota(jnp.int32, (16, LANES), 0)
    column = jnp.broadcast_to(lane & 15, (16, LANES))
    band = (lane & 63) >> 4

    def entry(i, j):
        value = jnp.zeros(j.shape, jnp.float32)
        for first in range(4):
            for second in range(4):
                value = jnp.where((i == first) & (j == second), table[first][second], value)
        return value

    middle = jnp.where((row & 3) == (column & 3), entry(row >> 2, column >> 2), 0.0)
    last = jnp.where((row >> 2) == (column >> 2), entry(row & 3, column & 3), 0.0)
    parts = [[], [], []]
    for a in range(4):
        along = jnp.zeros(lane.shape, jnp.float32)
        for second in range(4):
            along = jnp.where(band == second, table[a][second], along)
        parts[0].append(jnp.where(row == column, along, 0.0))
        parts[1].append(jnp.where(band == a, middle, 0.0))
        parts[2].append(jnp.where(band == a, last, 0.0))
    return parts


def own_kernel(
    state, neighbours, rows, mixing, dissipation, omega, angle, counts,
    tendency, outer, forward, loss, frequency, turn, live_count, matrix, cells, trace, sems,
):
    copies = fetch_all(
        [(dissipation, loss), (omega, frequency), (angle, turn), (counts, live_count)], sems
    )
    count = cells.shape[0]
    elems = state.shape[-1]

    for tile in range(count):
        cells[tile] = state[0, :, :, tile_of(tile)]
    for face in range(6):
        for tile in range(count):
            load_trace(cells, tile, face ^ 1, trace.at[face])

    for face in range(6):
        for tile in range(count):
            sources = [trace[face, source] for source in range(count)]
            outer[face, tile] = choose(sources, neighbours[face : face + 1, tile_of(tile)] - RIM)

    lane = lax.broadcasted_iota(jnp.int32, (1, LANES), 1)
    parts = derivative_parts(lane)
    layout = [((0, 1), 0, 5), ((2, 3), 1, 6), ((4, 0), 2, 7), ((1, 2), 3, None), ((3, 4), 4, None)]
    for g in range(FIELDS):
        values = [
            [jnp.broadcast_to(mixing[g, d : d + 1, f : f + 1], (1, LANES)) for f in range(FIELDS)]
            for d in range(3)
        ]
        for (left, right), high_place, low_place in layout:
            weight = [jnp.where(lane < MODES, values[d][left], values[d][right]) for d in range(3)]
            for a in range(4):
                block = weight[0] * parts[0][a] + weight[1] * parts[1][a] + weight[2] * parts[2][a]
                high, low = split(block)
                band = slice(g * MODES + 16 * a, g * MODES + 16 * a + 16)
                matrix[band, tile_of(high_place)] = high
                if low_place is not None:
                    if left == FIELDS - 1:
                        low = jnp.where(lane < MODES, low, jnp.zeros_like(low))
                    matrix[band, tile_of(low_place)] = low
    high, low = split(state[0].reshape(FIELDS * MODES, elems))
    stacked = jnp.concatenate([high, low, high, jnp.zeros_like(high[:MODES])], axis=0)
    product = jnp.dot(matrix[...], stacked, preferred_element_type=jnp.float32)
    for tile in range(count):
        tendency[tile] = product[:, tile_of(tile)].reshape(FIELDS, MODES, LANES)

    forward[0:2, :] = rows[0:2, :]
    for copy in copies:
        copy.wait()
    for row, value in enumerate(
        [loss[...], frequency[...], turn[...], live_count[...].astype(jnp.float32)]
    ):
        forward[2 + row : 3 + row, :] = jnp.broadcast_to(value, (1, elems))


def flux_row(g, direction, field):
    return (direction * FIELDS + g) * FIELDS + field


FRAME = 3 * FIELDS * FIELDS
WEIGHTS = FRAME + 5


def halo_kernel(
    plane, state, neighbours, forward, mixing, tendency, outer, far_source, near_source,
    partial, small, rim, trace, from_far, from_near, sems,
):
    copies = fetch_all([(far_source, from_far), (near_source, from_near)], sems)
    n = lax.axis_size("space")
    inst_count = lax.axis_size("inst")
    inst = lax.axis_index("inst")
    count = partial.shape[0]
    elems = state.shape[-1]
    for g in range(FIELDS):
        for d in range(3):
            for field in range(FIELDS):
                row = flux_row(g, d, field)
                small[row : row + 1, :] = jnp.broadcast_to(
                    mixing[g, d : d + 1, field : field + 1], (1, LANES)
                )
    loss, frequency, turn, live_count = [
        forward[2 + row : 3 + row, :LANES] for row in range(4)
    ]
    small[FRAME : FRAME + 1, :] = 3.0 * loss
    small[FRAME + 1 : FRAME + 2, :] = jnp.cos(turn)
    small[FRAME + 2 : FRAME + 3, :] = jnp.sin(turn)

    lane = lax.broadcasted_iota(jnp.int32, (1, LANES), 1)
    spectral = spectral_values(inst_count)
    keeps, scales = [], []
    for tile in range(count):
        scale = forward[0:1, tile_of(tile)]
        step = COURANT / (scale * loss + frequency)
        live = (lane + tile * LANES).astype(jnp.float32) < live_count
        step = jnp.where(live, step, 0.0)
        keeps.append(jnp.where(live, 1.0, 0.0) - step * (frequency * spectral[0]))
        scales.append(step * scale)
        small[WEIGHTS + tile : WEIGHTS + tile + 1, :] = scales[tile]
        for away in range(1, inst_count):
            value = jnp.where(
                inst + away < inst_count, spectral[-away], spectral[inst_count - away]
            )
            row = WEIGHTS + away * count + tile
            small[row : row + 1, :] = -step * (frequency * value)

    pairs = forward[1:2, :plane].astype(jnp.int32)
    place = pairs - base_owner(pairs, plane) * plane
    place = jnp.where(place < 0, place + n * plane, place).astype(jnp.float32)
    for tile in range(plane // LANES):
        row = WEIGHTS + inst_count * count + tile
        small[row : row + 1, :] = place[:, tile_of(tile)]

    partial[...] = tendency[...]
    for copy in copies:
        copy.wait()
    odd = lax.rem(lax.axis_index("space"), 2) == 1
    half_lane = lax.broadcasted_iota(jnp.int32, (MODES // 2, 2 * RIM), 1)
    for k in range(2 * FIELDS):
        field, half = k // 2, k % 2
        piece = pl.ds(32 * (k % FIELDS), 32)
        left = jnp.where(odd, from_near[piece, :], from_far[piece, :])
        right = jnp.where(odd, from_far[piece, :], from_near[piece, :])
        if k < FIELDS:
            right = pltpu.roll(right, RIM, 1)
        else:
            left = pltpu.roll(left, RIM, 1)
        rim[0, field, 32 * half : 32 * half + 32, :] = jnp.where(half_lane < RIM, left, right)
    for face in range(6):
        load_trace(rim, 0, face ^ 1, trace.at[pl.ds(face, 1)])
    for face in range(6):
        for tile in range(count):
            number = neighbours[face : face + 1, tile_of(tile)]
            previous = number < RIM
            remote = previous | (number >= RIM + elems)
            found = choose([trace[face]], jnp.where(previous, number, number - elems))
            found = jnp.where(remote, found, outer[face, tile])
            if face == 5:
                column = lane + tile * LANES
                sliding = (column >= 2 * RIM) & (column < 2 * RIM + plane)
                found = jnp.where(sliding, 0.0, found)
            parts = [found[field * FACE : (field + 1) * FACE] for field in range(FIELDS)]
            lift(partial, tile, face, mix(small, face, parts), 1.0)

    node = lax.broadcasted_iota(jnp.int32, (MODES, LANES), 0)
    faces = jnp.zeros((MODES, LANES), jnp.float32)
    for index in (node >> 4, (node >> 2) & 3, node & 3):
        faces = faces + jnp.where((index == 0) | (index == 3), 1.0, 0.0)
    for tile in range(count):
        keep = keeps[tile] - (3.0 * loss * scales[tile]) * faces
        partial[tile] = keep * state[0, :, :, tile_of(tile)] + scales[tile] * partial[tile]


def mix(small, face, parts):
    mixed = []
    for g in range(FIELDS):
        total = None
        for field in range(FIELDS):
            row = flux_row(g, face // 2, field)
            term = small[row : row + 1, :] * parts[field]
            total = term if total is None else total + term
        mixed.append((3.0 if face % 2 else -3.0) * total - small[FRAME : FRAME + 1, :] * parts[g])
    return mixed


def lift(cells, tile, face, mixed, scale):
    for g in range(FIELDS):
        change = scale * mixed[g]
        for rows, nodes in face_pieces(face):
            cells[tile, g, nodes, :] = cells[tile, g, nodes, :] - change[rows]


def final_kernel(plane, partial, small, first, second, *refs):
    inst_count = lax.axis_size("inst")
    others, (result, buffer, sems) = refs[: inst_count - 1], refs[inst_count - 1 :]
    count = buffer.shape[0]
    start, stop = 2 * RIM // LANES, (2 * RIM + plane) // LANES
    copies = []
    for tile in [*range(start), *range(stop, count), *range(start, stop)]:
        for field in range(FIELDS):
            total = partial[tile, field]
            for away in range(1, inst_count):
                row = WEIGHTS + away * count + tile
                other = others[away - 1][0, field, :, tile_of(tile)]
                total = total + small[row : row + 1, :] * other
            buffer[tile, field] = total
        if start <= tile < stop:
            row = WEIGHTS + inst_count * count + tile - start
            found = choose(
                [
                    block[:, tile_of(source)]
                    for block in (first, second)
                    for source in range(plane // LANES)
                ],
                small[row : row + 1, :].astype(jnp.int32),
            )
            parts = [found[field * FACE : (field + 1) * FACE] for field in range(FIELDS)]
            cosine, sine = small[FRAME + 1 : FRAME + 2, :], small[FRAME + 2 : FRAME + 3, :]
            parts[2], parts[3] = (
                cosine * parts[2] - sine * parts[3],
                sine * parts[2] + cosine * parts[3],
            )
            scale = small[WEIGHTS + tile : WEIGHTS + tile + 1, :]
            lift(buffer, tile, 5, mix(small, 5, parts), scale)
        copies.append(
            pltpu.make_async_copy(
                buffer.at[tile], result.at[0, :, :, pl.ds(tile * LANES, LANES)], sems.at[tile]
            )
        )
        copies[-1].start()
    for copy in copies:
        copy.wait()


def shards(
    state, metric, jacobians, dissipation, omega, rotor_angle, counts, neighbours, mortar_pairs
):
    elems = state.shape[-1]
    tiles = elems // LANES
    plane = mortar_pairs.shape[-1]
    n = lax.axis_size("space")
    inst_count = lax.axis_size("inst")
    f32 = jnp.float32
    shape = jax.ShapeDtypeStruct
    sems = pltpu.SemaphoreType.DMA
    scalar = pltpu.VMEM((1, 1), f32)
    params = pltpu.CompilerParams(vmem_limit_bytes=16 * 2**20)
    cost = pl.CostEstimate(flops=2**31, bytes_accessed=2**22, transcendentals=0)

    others = [
        lax.ppermute(state, "inst", [((i + away) % inst_count, i) for i in range(inst_count)])
        for away in range(1, inst_count)
    ]

    rotor, far, near, shift, rows, mixing = pl.pallas_call(
        functools.partial(prep_kernel, plane),
        out_shape=(
            shape((TRACE, plane), f32),
            shape((FIELDS * MODES // 2, 2 * RIM), f32),
            shape((FIELDS * MODES // 2, 2 * RIM), f32),
            shape((1,), jnp.int32),
            shape((8, elems), f32),
            shape((FIELDS, 3, FIELDS), f32),
        ),
        in_specs=[HBM] * 4,
        out_specs=(VMEM, VMEM, VMEM, SMEM, VMEM, VMEM),
        scratch_shapes=[
            pltpu.VMEM((1, plane), jnp.int32),
            pltpu.VMEM((1, elems), f32),
            pltpu.VMEM((FIELDS, MODES, 2 * RIM), f32),
            pltpu.VMEM((plane // LANES, FIELDS, MODES, LANES), f32),
            sems((plane // LANES + 4,)),
        ],
        name="prep",
    )(state, mortar_pairs, metric.reshape(1, elems), jnp.transpose(jacobians, (1, 0, 2)))

    def fetch(away, block):
        if away == 0:
            return block
        return lax.ppermute(block, "space", [((i + away) % n, i) for i in range(n)])

    ends = [(i, (i + 1) % n) for i in range(1, n, 2)]
    middles = [(i, i + 1) for i in range(0, n, 2)]

    def swap(pairs, block):
        return lax.ppermute(block, "space", pairs + [(j, i) for i, j in pairs])

    def branch(away, rotor, far, near, *operands):
        first = fetch(away, rotor)
        from_far, from_near = swap(ends, far), swap(middles, near)
        own = pl.pallas_call(
            own_kernel,
            out_shape=(
                shape((tiles, FIELDS, MODES, LANES), f32),
                shape((6, tiles, TRACE, LANES), f32),
                shape((8, elems), f32),
            ),
            in_specs=[VMEM] * 4 + [HBM] * 4,
            out_specs=(VMEM,) * 3,
            scratch_shapes=[
                scalar,
                scalar,
                scalar,
                pltpu.VMEM((1, 1), jnp.int32),
                pltpu.VMEM((FIELDS * MODES, 8 * LANES), jnp.bfloat16),
                pltpu.VMEM((tiles, FIELDS, MODES, LANES), f32),
                pltpu.VMEM((6, tiles, TRACE, LANES), f32),
                sems((4,)),
            ],
            compiler_params=params,
            cost_estimate=cost,
            name="own",
        )(*operands)
        return first, from_far, from_near, own

    first, from_far, from_near, (tendency, outer, forward) = lax.switch(
        shift[0],
        [functools.partial(branch, away) for away in range(n)],
        rotor, far, near, state, neighbours, rows, mixing, dissipation.reshape(1, 1),
        omega.reshape(1, 1), rotor_angle.reshape(1, 1), counts.reshape(1, 1),
    )
    second = fetch(1, first)

    partial, small = pl.pallas_call(
        functools.partial(halo_kernel, plane),
        out_shape=(
            shape((tiles, FIELDS, MODES, LANES), f32),
            shape((-(-(WEIGHTS + inst_count * tiles + plane // LANES) // 8) * 8, LANES), f32),
        ),
        in_specs=[VMEM] * 6 + [ANY] * 2,
        out_specs=(VMEM, VMEM),
        scratch_shapes=[
            pltpu.VMEM((1, FIELDS, MODES, 2 * RIM), f32),
            pltpu.VMEM((6, TRACE, LANES), f32),
            pltpu.VMEM((FIELDS * MODES // 2, 2 * RIM), f32),
            pltpu.VMEM((FIELDS * MODES // 2, 2 * RIM), f32),
            sems((2,)),
        ],
        compiler_params=params,
        cost_estimate=cost,
        name="halo",
    )(state, neighbours, forward, mixing, tendency, outer, from_far, from_near)

    return pl.pallas_call(
        functools.partial(final_kernel, plane),
        out_shape=shape(state.shape, f32),
        in_specs=[VMEM] * (3 + inst_count),
        out_specs=ANY,
        scratch_shapes=[
            pltpu.VMEM((tiles, FIELDS, MODES, LANES), f32),
            sems((tiles,)),
        ],
        compiler_params=params,
        name="final",
    )(partial, small, first, second, *others)


def solution(mesh):
    return jax.shard_map(
        shards,
        mesh=mesh,
        in_specs=(
            P("inst", None, None, "space"),
            P("space"),
            P(),
            P(),
            P(),
            P("inst"),
            P("space"),
            P(None, "space"),
            P("inst", "space"),
        ),
        out_specs=P("inst", None, None, "space"),
        check_vma=False,
    )
```
